32 devices in a mesh: dp: 16 (over z, x, core), tensor: 2 (over y).
Axes of the slice: x: 2, y: 2, z: 4, core: 2. Of those that a mesh axis runs over, the one named last changes fastest.
Arguments:
- inputs: bfloat16 [32, 1024, 768], P('dp', 'tensor'), may hold values from -6 to 6
- cotangent: bfloat16 [32, 1024, 768], P('dp', 'tensor'), may hold values from -6 to 6
- lengths: int32 [32], P('dp'), may hold values from 256 to 1024, as said below
- routes: int32 [32, 1024, 1], P('dp'), may hold values from 0 to 3
- norm1_gain: bfloat16 [768], replicated, may hold values from 0.25 to 1.75
- w_query: bfloat16 [768, 768], P(None, 'tensor'), may hold values from -0.21875 to 0.21875
- w_key: bfloat16 [768, 768], P(None, 'tensor'), may hold values from -0.21875 to 0.21875
- w_value: bfloat16 [768, 768], P(None, 'tensor'), may hold values from -0.21875 to 0.21875
- w_attn_out: bfloat16 [768, 768], P('tensor'), may hold values from -2 to 2
- norm2_gain: bfloat16 [768], replicated, may hold values from 0.25 to 1.75
- w_router: bfloat16 [768, 4], replicated, may hold values from -0.109375 to 0.109375
- w_expert_in: bfloat16 [4, 768, 3072], P(None, None, 'tensor'), may hold values from -0.21875 to 0.21875
- w_expert_out: bfloat16 [4, 3072, 768], P(None, 'tensor'), may hold values from -0.4375 to 0.4375
Outputs:
- activations: bfloat16 [32, 1024, 768], P('dp', 'tensor')
- input_grad: float32 [32, 1024, 768], P('dp', 'tensor')
- grad_norm1_gain: float32 [768], P(('dp', 'tensor'))
- grad_query: float32 [768, 768], P('dp', 'tensor')
- grad_key: float32 [768, 768], P('dp', 'tensor')
- grad_value: float32 [768, 768], P('dp', 'tensor')
- grad_attn_out: float32 [768, 768], P('tensor', 'dp')
- grad_norm2_gain: float32 [768], P(('dp', 'tensor'))
- grad_router: float32 [768, 4], P(('dp', 'tensor'))
- grad_expert_in: float32 [4, 768, 3072], P(None, 'dp', 'tensor')
- grad_expert_out: float32 [4, 3072, 768], P(None, 'tensor', 'dp')
The draws below stay inside these ranges and needn't reach their ends.
Inputs may be any that keep to these rules, and one draw needn't show every extreme that they name: `lengths`: in each group of 2 sequences of one index of dp, one sequence has exactly 1024 valid slots.
All inputs are finite; a program needn't handle non-finite values.
Results may differ from the reference program's by a relative error of at most 0.018.
Values may be sent and summed in bfloat16 or wider, within the bound.
No kernel may reach another device: no remote copies, remote signals or barrier semaphores. Data moves between devices by JAX's collectives and lax.ppermute only.
A program may use at most 256 MiB of HBM per device.

```python
import jax
import jax.numpy as jnp
from jax import lax

D = 768
HEADS = 12
HEAD_DIM = 64
FF = 3072
EXPERTS = 4
SLOTS = 1024
MIN_LEN = 256
SEQ_GRP = 2
SEQS = 32
INNER = 768
CAP = 640


def draw_lengths(key, part):
    key = jax.random.fold_in(key, 11)
    first_key, second_key = jax.random.split(key)
    drawn = jax.random.randint(first_key, (SEQS,), MIN_LEN, SLOTS + 1)
    picked = jax.random.randint(second_key, (SEQS // SEQ_GRP, 1), 0, SEQ_GRP)
    chosen = (jnp.arange(SEQ_GRP)[None, :] == picked).reshape(SEQS)
    return jnp.where(chosen, SLOTS, drawn).astype(jnp.int32)


def draw_routes(key, part):
    key = jax.random.fold_in(key, 13)
    favour_key, pick_key, spread_key = jax.random.split(key, 3)
    groups = SEQS // SEQ_GRP
    favoured = jax.random.randint(favour_key, (groups, 1), 0, EXPERTS)
    picks = jax.random.randint(pick_key, (groups, SEQ_GRP * SLOTS), 0, 10)
    spread = jax.random.randint(spread_key, (groups, SEQ_GRP * SLOTS), 0, EXPERTS)
    chosen = jnp.where(picks < 3, favoured, spread)
    return chosen.reshape(SEQS, SLOTS, 1).astype(jnp.int32)


def steps_of(stream_key, extent, cuts, least, high):
    def one(dim, blocks):
        heights = jax.random.uniform(jax.random.fold_in(jax.random.fold_in(stream_key, 6), dim), (blocks,), jnp.float32, least / len(cuts), high / len(cuts))
        return jnp.repeat(jnp.exp(heights), extent[dim] // blocks).reshape((-1,) + (1,) * (len(extent) - dim - 1))

    factor_of = one(*cuts[0])
    for cut in cuts[1:]:
        factor_of = factor_of * one(*cut)
    return factor_of


def scatter_about(stream_key, dims, scale, bound, pieces=(), dtype=jnp.bfloat16):
    values = jax.random.normal(stream_key, dims, jnp.float32) * scale
    if len(pieces) > 0:
        values = steps_of(stream_key, dims, pieces, -0.22, 0.18) * values
    return jnp.clip(values, min=-bound, max=bound).astype(dtype)


def setup_inputs(seed: int = 0) -> dict:
    streams_of = jax.random.split(jax.random.key(seed), 14)
    inputs = scatter_about(streams_of[0], (SEQS, SLOTS, D), 1.0, 6.0, ((0, 16), (1, 2)))
    cotangent = scatter_about(streams_of[1], (SEQS, SLOTS, D), 1.0, 6.0, ((0, 16), (1, 2)))
    lengths = draw_lengths(jax.random.fold_in(streams_of[13], 71), 0)
    routes = draw_routes(jax.random.fold_in(streams_of[13], 71), 0)
    norm1_gain = jnp.clip(1.0 + 0.15 * jax.random.normal(streams_of[4], (D,), jnp.float32), 0.25, 1.75).astype(jnp.bfloat16)
    w_query = scatter_about(streams_of[5], (D, INNER), D ** -0.5, 0.21875, ((1, 2),))
    w_key = scatter_about(streams_of[6], (D, INNER), D ** -0.5, 0.21875, ((1, 2),))
    w_value = scatter_about(streams_of[7], (D, INNER), D ** -0.5, 0.21875, ((1, 2),))
    w_attn_out = scatter_about(streams_of[8], (INNER, D), 8 ** -0.5, 2.0, ((0, 2),))
    norm2_gain = jnp.clip(1.0 + 0.15 * jax.random.normal(streams_of[9], (D,), jnp.float32), 0.25, 1.75).astype(jnp.bfloat16)
    w_router = scatter_about(streams_of[10], (D, EXPERTS), (4 * D) ** -0.5, 0.109375)
    w_expert_in = scatter_about(streams_of[11], (EXPERTS, D, FF), D ** -0.5, 0.21875, ((2, 2),))
    w_expert_out = scatter_about(streams_of[12], (EXPERTS, FF, D), (FF // 16) ** -0.5, 0.4375, ((1, 2),))
    return dict(inputs=inputs, cotangent=cotangent, lengths=lengths, routes=routes, norm1_gain=norm1_gain, w_query=w_query, w_key=w_key, w_value=w_value, w_attn_out=w_attn_out, norm2_gain=norm2_gain, w_router=w_router, w_expert_in=w_expert_in, w_expert_out=w_expert_out)


@jax.custom_vjp
def low(v):
    return lax.optimization_barrier(v.astype(jnp.bfloat16)).astype(jnp.float32)

@jax.custom_vjp
def low_back(v):
    return v

def low_keep(v):
    return (low(v), None)

def low_pass(kept, grad):
    return (grad,)

def back_keep(v):
    return (v, None)

def back_low(kept, grad):
    return (low(grad),)
low.defvjp(low_keep, low_pass)
low_back.defvjp(back_keep, back_low)
highest = lax.Precision.HIGHEST
norm_eps = 1e-06

def matmul(left, right):
    return jnp.dot(left, right, precision=highest, preferred_element_type=jnp.float32)

def rms_norm(values_in, norm_gain):
    return values_in * lax.rsqrt(lax.optimization_barrier(jnp.mean(values_in * values_in, axis=-1, keepdims=True)) + norm_eps) * norm_gain

def slot_index(route_flat, valid_flat, group_lengths):
    hits = jnp.logical_and(route_flat[:, None] == jnp.arange(EXPERTS)[None, :], valid_flat[:, None]).astype(jnp.int32)
    counts = jnp.cumsum(hits, axis=0).astype(jnp.int32)
    position = lax.optimization_barrier(jnp.sum(counts * hits, axis=1)).astype(jnp.int32) - 1
    valid_total = jnp.sum(group_lengths).astype(jnp.int32)
    capacity = (5 * valid_total + 4 * EXPERTS - 1) // (4 * EXPERTS)
    keep = jnp.logical_and(valid_flat, position < capacity)
    return jnp.where(keep, route_flat.astype(jnp.int32) * CAP + position, EXPERTS * CAP).astype(jnp.int32)

def attend_sequence(bundle):
    query_seq, key_seq, value_seq, length = bundle
    factor = HEAD_DIM ** (-0.5)
    scores = jnp.einsum('qhd,khd->hqk', query_seq, key_seq, precision=highest) * factor
    visible = jnp.arange(SLOTS) < length
    scores = low_back(jnp.where(visible[None, None, :], scores, -1000000000.0))
    weights = low(jax.nn.softmax(scores, axis=-1))
    return jnp.einsum('hqk,khd->qhd', weights, value_seq, precision=highest)

def group_forward(params, group_rows, group_lengths, group_routes):
    gain_one, query_weight, key_weight, value_weight, attn_weight, gain_two, router_weight, expert_in, expert_out = params
    heads_shape = (SEQ_GRP, SLOTS, HEADS, HEAD_DIM)
    normed_one = low(rms_norm(group_rows, gain_one))
    queries = low_back(low(matmul(normed_one, query_weight))).reshape(heads_shape)
    keys_all = low_back(low(matmul(normed_one, key_weight))).reshape(heads_shape)
    values_all = low_back(low(matmul(normed_one, value_weight))).reshape(heads_shape)
    context = lax.map(jax.checkpoint(attend_sequence), (queries, keys_all, values_all, group_lengths))
    context = low_back(low(context.reshape(SEQ_GRP, SLOTS, INNER)))
    residual = group_rows + low_back(matmul(context, attn_weight))
    normed_two = low(rms_norm(residual, gain_two))
    router_probs = jax.nn.softmax(matmul(normed_two, router_weight), axis=-1).reshape(-1, EXPERTS)
    route_flat = group_routes[:, :, 0].reshape(-1)
    valid_flat = (jnp.arange(SLOTS)[None, :] < group_lengths[:, None]).reshape(-1)
    chosen = route_flat[:, None] == jnp.arange(EXPERTS)[None, :]
    gate = lax.optimization_barrier(jnp.sum(jnp.where(chosen, router_probs, 0.0), axis=-1))
    slots_taken = slot_index(route_flat, valid_flat, group_lengths)
    buffer = jnp.zeros((EXPERTS * CAP + 1, D), jnp.float32).at[slots_taken].add(normed_two.reshape(-1, D))
    dispatched = buffer[:EXPERTS * CAP].reshape(EXPERTS, CAP, D)
    hidden_pre = low_back(jnp.einsum('ecd,edf->ecf', dispatched, expert_in, precision=highest))
    hidden = low(jax.nn.gelu(hidden_pre, approximate=True))
    expert_result = low_back(jnp.einsum('ecf,efd->ecd', hidden, expert_out, precision=highest))
    padded_result = jnp.concatenate([expert_result.reshape(EXPERTS * CAP, D), jnp.zeros((1, D), jnp.float32)], 0)
    combined = padded_result[slots_taken]
    mixed = residual.reshape(-1, D) + gate[:, None] * combined
    return jnp.where(valid_flat[:, None], mixed, 0.0).reshape(SEQ_GRP, SLOTS, D)

def reference(inputs, cotangent, lengths, routes, norm1_gain, w_query, w_key, w_value, w_attn_out, norm2_gain, w_router, w_expert_in, w_expert_out):
    params = tuple((weight.astype(jnp.float32) for weight in (norm1_gain, w_query, w_key, w_value, w_attn_out, norm2_gain, w_router, w_expert_in, w_expert_out)))
    groups = SEQS // SEQ_GRP
    inputs_grouped = inputs.astype(jnp.float32).reshape(groups, SEQ_GRP, SLOTS, D)
    cotangent_grouped = cotangent.astype(jnp.float32).reshape(groups, SEQ_GRP, SLOTS, D)
    lengths_grouped = lengths.reshape(groups, SEQ_GRP)
    routes_grouped = routes.reshape(groups, SEQ_GRP, SLOTS, 1)

    def accumulate(running, bundle):
        group_rows, group_cotangent, group_lengths, group_routes = bundle

        def forward(weights_now, rows_now):
            return group_forward(weights_now, rows_now, group_lengths, group_routes)
        output, pullback = jax.vjp(forward, params, group_rows)
        weight_grads, rows_grads = pullback(group_cotangent)
        running = tuple((before + update for before, update in zip(running, weight_grads)))
        return (running, (output, rows_grads))
    start = tuple((jnp.zeros_like(weight) for weight in params))
    running, (outputs, rows_grads) = lax.scan(accumulate, start, (inputs_grouped, cotangent_grouped, lengths_grouped, routes_grouped))
    activations = outputs.reshape(SEQS, SLOTS, D).astype(jnp.bfloat16)
    input_grad = rows_grads.reshape(SEQS, SLOTS, D)
    return (activations, input_grad, running[0], running[1], running[2], running[3], running[4], running[5], running[6], running[7], running[8])
```

```python
import functools
import math

import jax
import jax.numpy as jnp
from jax import lax
from jax.experimental import pallas as pl
from jax.experimental.pallas import tpu as pltpu
from jax.sharding import PartitionSpec as P

HEAD_DIM = 64
EXPERTS = 4
CAP = 640
PAIR = 2 * HEAD_DIM
LOG_SCALE = math.log2(math.e) * HEAD_DIM ** (-0.5)

highest = lax.Precision.HIGHEST
norm_eps = 1e-06
bf16 = jnp.bfloat16
f32 = jnp.float32


def dot(left, right):
    return lax.dot_general(left, right, (((1,), (0,)), ((), ())), preferred_element_type=f32)


def dot_nt(left, right):
    return lax.dot_general(left, right, (((1,), (1,)), ((), ())), preferred_element_type=f32)


def dot_tn(left, right):
    return lax.dot_general(left, right, (((0,), (0,)), ((), ())), preferred_element_type=f32)


def attend_kernel(query_rows, info, own, oth, ctx_own, ctx_oth, log_ref):
    half = own.shape[0]
    row = lax.broadcasted_iota(jnp.int32, (half, PAIR), 0)
    lane = lax.broadcasted_iota(jnp.int32, (half, PAIR), 1)
    zeros = jnp.zeros((half, PAIR), bf16)
    hidden_key = jnp.full((half, PAIR), -1e30, bf16)
    sides = ((own, ctx_own, row + info[1] < info[0]), (oth, ctx_oth, row + info[2] < info[0]))
    keys = []
    for head in range(2):
        mine = (lane < HEAD_DIM) == (head == 0)
        spare = lane == (HEAD_DIM if head == 0 else 0)
        parts = []
        for ref, _, seen in sides:
            mask_value = jnp.where(seen, zeros, hidden_key)
            key = ref[:, PAIR : 2 * PAIR]
            parts.append(jnp.where(mine, key, jnp.where(spare, mask_value, zeros)))
        keys.append(jnp.concatenate(parts, 0))
    values_t = jnp.transpose(jnp.concatenate([own[:, 2 * PAIR :], oth[:, 2 * PAIR :]], 0))
    q_lane = lax.broadcasted_iota(jnp.int32, (query_rows, PAIR), 1)
    steps = [
        (side, block, head)
        for side in range(2)
        for block in range(half // query_rows)
        for head in range(2)
    ]

    def scores_of(step):
        side, block, head = step
        query = sides[side][0][block * query_rows : (block + 1) * query_rows, :PAIR]
        mine = (q_lane < HEAD_DIM) == (head == 0)
        spare = q_lane == (HEAD_DIM if head == 0 else 0)
        query = jnp.where(
            mine, query, jnp.where(spare, jnp.ones_like(query), jnp.zeros_like(query))
        )
        return dot_nt(keys[head], query)

    current = scores_of(steps[0])
    outs = [None, None]
    for index, (side, block, head) in enumerate(steps):
        following = scores_of(steps[index + 1]) if index + 1 < len(steps) else None
        top = jnp.max(current, axis=0, keepdims=True) * LOG_SCALE
        exponent = jnp.exp2(current * LOG_SCALE - top)
        total = jnp.sum(exponent, axis=0, keepdims=True)
        head_values = values_t[head * HEAD_DIM : (head + 1) * HEAD_DIM, :]
        outs[head] = dot(head_values, exponent.astype(bf16)) * (1.0 / total)
        first = side * half + block * query_rows
        log_ref[head : head + 1, first : first + query_rows] = top + jnp.log2(total)
        if head == 1:
            sides[side][1][block * query_rows : (block + 1) * query_rows, :] = jnp.transpose(
                jnp.concatenate(outs, 0)
            ).astype(bf16)
        current = following


def attend(info, own, oth, seq):
    half, width = oth.shape
    pairs = width // (3 * PAIR)
    query_rows = min(512, half)
    out = pl.BlockSpec((half, PAIR), lambda p: (0, p))
    shape = jax.ShapeDtypeStruct((half, width // 3), bf16)
    return pl.pallas_call(
        functools.partial(attend_kernel, query_rows),
        grid=(pairs,),
        in_specs=[
            pl.BlockSpec(memory_space=pltpu.SMEM),
            pl.BlockSpec((half, 3 * PAIR), lambda p: (seq, p)),
            pl.BlockSpec((half, 3 * PAIR), lambda p: (0, p)),
        ],
        out_specs=[out, out, pl.BlockSpec((8, 2 * half), lambda p: (p, 0))],
        out_shape=[shape, shape, jax.ShapeDtypeStruct((8 * pairs, 2 * half), f32)],
        compiler_params=pltpu.CompilerParams(vmem_limit_bytes=40 * 2**20),
        cost_estimate=pl.CostEstimate(
            flops=32 * pairs * half * half * PAIR,
            bytes_accessed=8 * half * width,
            transcendentals=8 * pairs * half * half,
        ),
        name="attend",
    )(info, own, oth)


def attend_back_kernel(
    query_rows, info, own, oth, ctx_own, ctx_oth, up_own, up_oth, log_ref, out_own, out_oth,
    key_sum, value_sum,
):
    half = own.shape[0]
    row = lax.broadcasted_iota(jnp.int32, (half, PAIR), 0)
    zeros = jnp.zeros((half, PAIR), bf16)
    seen = (row + info[1] < info[0], row + info[2] < info[0])
    sides = ((own, ctx_own, up_own, out_own), (oth, ctx_oth, up_oth, out_oth))

    def all_keys(part):
        first, last = part * PAIR, (part + 1) * PAIR
        return jnp.concatenate(
            [
                jnp.where(seen[0], own[:, first:last], zeros),
                jnp.where(seen[1], oth[:, first:last], zeros),
            ],
            0,
        )

    keys, values = all_keys(1), all_keys(2)
    keys_t = jnp.transpose(keys)
    lane = lax.broadcasted_iota(jnp.int32, (query_rows, PAIR), 1)
    sum_lane = lax.broadcasted_iota(jnp.int32, (8, PAIR), 1)
    sum_row = lax.broadcasted_iota(jnp.int32, (8, PAIR), 0)
    head_sum = jnp.where((sum_lane < HEAD_DIM) == (sum_row == 0), 1.0, 0.0).astype(bf16)
    for side, (src, ctx, up, out) in enumerate(sides):
        for block in range(half // query_rows):
            rows = slice(block * query_rows, (block + 1) * query_rows)
            first = side * half + block * query_rows
            query, grad = src[rows, :PAIR], up[rows, :]
            product = grad.astype(f32) * ctx[rows, :].astype(f32)
            coarse = product.astype(bf16)
            fine = (product - coarse.astype(f32)).astype(bf16)
            delta = dot_nt(head_sum, coarse) + dot_nt(head_sum, fine)
            query_grads, key_grads, value_grads = [], [], []
            for head in range(2):
                mine = (lane < HEAD_DIM) == (head == 0)
                query_h = jnp.where(mine, query, jnp.zeros_like(query))
                grad_h = jnp.where(mine, grad, jnp.zeros_like(grad))
                log_row = log_ref[head : head + 1, first : first + query_rows]
                scores = dot_nt(keys, query_h)
                probs = jnp.exp2(jnp.minimum(scores * LOG_SCALE - log_row, 0.0))
                prob_grad = dot_nt(values, grad_h)
                score_grad = (probs * (prob_grad - delta[head : head + 1, :])).astype(bf16)
                value_grads.append(dot(probs.astype(bf16), grad_h))
                key_grads.append(dot(score_grad, query_h))
                query_grads.append(
                    dot(keys_t[head * HEAD_DIM : (head + 1) * HEAD_DIM, :], score_grad)
                )
            value_grad = value_grads[0] + value_grads[1]
            key_grad = key_grads[0] + key_grads[1]
            if side == 0 and block == 0:
                value_sum[...] = value_grad
                key_sum[...] = key_grad
            else:
                value_sum[...] += value_grad
                key_sum[...] += key_grad
            query_grad = jnp.transpose(jnp.concatenate(query_grads, 0)) * HEAD_DIM ** (-0.5)
            out[rows, :PAIR] = query_grad.astype(bf16)
    for side in range(2):
        part, out = slice(side * half, (side + 1) * half), sides[side][3]
        key_grad = jnp.where(seen[side], key_sum[part, :] * HEAD_DIM ** (-0.5), 0.0)
        out[:, PAIR : 2 * PAIR] = key_grad.astype(bf16)
        out[:, 2 * PAIR :] = jnp.where(seen[side], value_sum[part, :], 0.0).astype(bf16)


def attend_back(info, own, oth, seq, ctx_own, ctx_oth, up_own, up_oth, logs):
    half, width = oth.shape
    pairs = width // (3 * PAIR)
    query_rows = min(256, half)
    one = pl.BlockSpec((half, PAIR), lambda p: (0, p))
    three = pl.BlockSpec((half, 3 * PAIR), lambda p: (0, p))
    shape = jax.ShapeDtypeStruct((half, width), bf16)
    return pl.pallas_call(
        functools.partial(attend_back_kernel, query_rows),
        grid=(pairs,),
        in_specs=[
            pl.BlockSpec(memory_space=pltpu.SMEM),
            pl.BlockSpec((half, 3 * PAIR), lambda p: (seq, p)),
            three, one, one, one, one,
            pl.BlockSpec((8, 2 * half), lambda p: (p, 0)),
        ],
        out_specs=[three, three],
        out_shape=[shape, shape],
        scratch_shapes=[pltpu.VMEM((2 * half, PAIR), f32), pltpu.VMEM((2 * half, PAIR), f32)],
        compiler_params=pltpu.CompilerParams(vmem_limit_bytes=40 * 2**20),
        cost_estimate=pl.CostEstimate(
            flops=80 * pairs * half * half * PAIR,
            bytes_accessed=14 * half * width,
            transcendentals=8 * pairs * half * half,
        ),
        name="attend_back",
    )(info, own, oth, ctx_own, ctx_oth, up_own, up_oth, logs)


def inverse_rms(rows):
    return lax.rsqrt(jnp.mean(rows * rows, axis=-1, keepdims=True) + norm_eps)


def norm_back(rows, inverse, gain, upstream):
    weighted = upstream * gain
    inner_mean = jnp.mean(rows * weighted, axis=-1, keepdims=True)
    return inverse * weighted - rows * inverse**3 * inner_mean


def slot_index(route_flat, valid_flat, group_lengths):
    hits = jnp.logical_and(
        route_flat[:, None] == jnp.arange(EXPERTS)[None, :], valid_flat[:, None]
    ).astype(jnp.int32)
    counts = jnp.cumsum(hits, axis=0)
    position = jnp.sum(counts * hits, axis=1) - 1
    valid_total = jnp.sum(group_lengths)
    capacity = (5 * valid_total + 4 * EXPERTS - 1) // (4 * EXPERTS)
    keep = jnp.logical_and(valid_flat, position < capacity)
    return jnp.where(keep, route_flat * CAP + position, EXPERTS * CAP)


def body(
    inputs,
    cotangent,
    lengths,
    routes,
    norm1_gain,
    w_query,
    w_key,
    w_value,
    w_attn_out,
    norm2_gain,
    w_router,
    w_expert_in,
    w_expert_out,
):
    seqs, half, width = inputs.shape
    slots = routes.shape[1]
    inner = w_query.shape[1]
    pairs = inner // PAIR
    side = lax.axis_index("tensor")
    dp_index = lax.axis_index("dp")
    dp_size = lax.axis_size("dp")
    own_tokens = seqs * half
    gain_one = norm1_gain.astype(f32)
    gain_two = norm2_gain.astype(f32)

    def swap(array):
        return lax.ppermute(array, "tensor", [(0, 1), (1, 0)])

    def local_order(per_slot):
        halves = per_slot.reshape(seqs, 2, half)
        first, last = halves[:, 0].reshape(-1), halves[:, 1].reshape(-1)
        return jnp.where(
            side == 0, jnp.concatenate([first, last]), jnp.concatenate([last, first])
        )

    rows = inputs.astype(f32)
    inverse_one = inverse_rms(rows)
    normed_own = (rows * inverse_one * gain_one).astype(bf16)
    normed_oth = [swap(normed_own[s]) for s in range(seqs)]
    cot_oth = swap(cotangent)
    attn_out_oth = swap(w_attn_out)
    w_pairs = jnp.concatenate(
        [w[:, p * PAIR : (p + 1) * PAIR] for p in range(pairs) for w in (w_query, w_key, w_value)],
        1,
    )
    proj_own = dot(normed_own.reshape(own_tokens, width), w_pairs).astype(bf16)
    valid = jnp.arange(slots)[None, :] < lengths[:, None]
    slots_taken = local_order(
        slot_index(routes.reshape(-1), valid.reshape(-1), lengths).reshape(seqs, slots)
    )
    route_local = local_order(routes[:, :, 0])
    valid_local = local_order(valid)
    chosen = route_local[:, None] == jnp.arange(EXPERTS)[None, :]
    infos = [
        jnp.stack([lengths[s], side * half, (1 - side) * half]).astype(jnp.int32)
        for s in range(seqs)
    ]
    proj_oth, ctx_own, ctx_oth, ctx_recv, logs = [], [], [], [], []
    residual, inverse_two, normed_two, two_oth = [], [], [], []
    for s in range(seqs):
        proj_oth.append(dot(normed_oth[s], w_pairs).astype(bf16))
        own_part, oth_part, log_part = attend(infos[s], proj_own, proj_oth[s], s)
        ctx_own.append(own_part)
        ctx_oth.append(oth_part)
        logs.append(log_part)
        ctx_recv.append(swap(oth_part))
    for s in range(seqs):
        residual.append(
            rows[s] + dot(ctx_own[s], w_attn_out) + dot(ctx_recv[s], attn_out_oth)
        )
        inverse_two.append(inverse_rms(residual[s]))
        normed_two.append((residual[s] * inverse_two[s] * gain_two).astype(bf16))
        two_oth.append(swap(normed_two[s]))

    tokens = jnp.concatenate(normed_two + two_oth, 0)
    router_probs = jax.nn.softmax(dot(tokens, w_router), axis=-1)
    gate = jnp.sum(jnp.where(chosen, router_probs, 0.0), axis=-1)
    upstream_all = jnp.concatenate(
        [cotangent.reshape(own_tokens, width), cot_oth.reshape(own_tokens, width)], 0
    ).astype(f32)
    upstream_all = jnp.where(valid_local[:, None], upstream_all, 0.0)
    gated = (gate[:, None] * upstream_all).astype(bf16)
    place = (jnp.arange(EXPERTS * CAP)[:, None] == slots_taken[None, :]).astype(bf16)

    def dispatch(token_rows):
        return dot(place, token_rows).astype(bf16).reshape(EXPERTS, CAP, width)

    def collect(expert_rows):
        return dot_tn(place, expert_rows.astype(bf16).reshape(EXPERTS * CAP, width))

    def ein(spec, left, right):
        return jnp.einsum(spec, left, right, preferred_element_type=f32)

    dispatched = dispatch(tokens)
    hidden_pre = ein("ecd,edf->ecf", dispatched, w_expert_in)
    result_grad = dispatch(gated)
    hidden_grad = ein("ecd,efd->ecf", result_grad, w_expert_out)
    hidden, gelu_pull = jax.vjp(lambda pre: jax.nn.gelu(pre, approximate=True), hidden_pre)
    hidden_low = hidden.astype(bf16)
    pre_grad = gelu_pull(hidden_grad)[0].astype(bf16)
    slot_gate_grad = jnp.sum(hidden_grad * hidden_low.astype(f32), axis=-1).reshape(-1)
    back_rows = collect(ein("ecf,edf->ecd", pre_grad, w_expert_in))
    back_recv = swap(back_rows[own_tokens:].astype(bf16))
    gate_grad = jnp.sum(jnp.where(place > 0, slot_gate_grad[:, None], 0.0), axis=0)
    gate_recv = swap(gate_grad)
    result_rows = collect(ein("ecf,efd->ecd", hidden_low, w_expert_out))
    result_recv = swap(result_rows[own_tokens:].astype(bf16))
    grad_expert_out_t = ein("ecd,ecf->edf", result_grad, hidden_low).astype(bf16)
    share_out_t = lax.psum_scatter(grad_expert_out_t, "dp", scatter_dimension=1, tiled=True)
    grad_expert_in = ein("ecd,ecf->edf", dispatched, pre_grad).astype(bf16)
    share_in = lax.psum_scatter(grad_expert_in, "dp", scatter_dimension=1, tiled=True)

    gate_grad = gate_grad + jnp.concatenate([gate_recv[own_tokens:], gate_recv[:own_tokens]])
    logit_grad = (chosen.astype(f32) - router_probs) * gate_grad[:, None]
    grad_router = lax.dot_general(
        tokens.astype(f32), logit_grad, (((0,), (0,)), ((), ())), precision=highest
    )
    router_back = lax.dot_general(
        logit_grad[:own_tokens],
        w_router.astype(f32),
        (((1,), (1,)), ((), ())),
        precision=highest,
    )
    residual_grad, residual_low, up_own, up_oth = [], [], [], []
    for s in range(seqs):
        part = slice(s * half, (s + 1) * half)
        two_grad = back_rows[part] + back_recv[part].astype(f32) + router_back[part]
        residual_grad.append(
            upstream_all[part] + norm_back(residual[s], inverse_two[s], gain_two, two_grad)
        )
        residual_low.append(residual_grad[s].astype(bf16))
        up_oth.append(swap(dot_nt(residual_low[s], attn_out_oth).astype(bf16)))
        up_own.append(dot_nt(residual_low[s], w_attn_out).astype(bf16))
    residual_all = jnp.concatenate(residual_low, 0)
    grad_attn_send = dot_tn(residual_all, jnp.concatenate(ctx_recv, 0)).astype(bf16)
    grad_attn_recv = swap(grad_attn_send)
    grad_attn_t = dot_tn(residual_all, jnp.concatenate(ctx_own, 0)) + grad_attn_recv.astype(f32)

    back_own, back_oth, one_recv = [], [], []
    for s in range(seqs):
        own_part, oth_part = attend_back(
            infos[s], proj_own, proj_oth[s], s, ctx_own[s], ctx_oth[s], up_own[s], up_oth[s], logs[s]
        )
        back_own.append(own_part)
        back_oth.append(oth_part)
        one_recv.append(swap(dot_nt(oth_part, w_pairs).astype(bf16)))
    grad_pairs = dot_tn(
        jnp.concatenate([normed_own.reshape(own_tokens, width)] + normed_oth, 0),
        jnp.concatenate(back_own + back_oth, 0),
    )
    router_high = grad_router.astype(bf16)
    router_low = (grad_router - router_high.astype(f32)).astype(bf16)
    small = jnp.concatenate([router_high, router_low], 1)
    small = jnp.pad(small, ((0, 0), (0, PAIR - 2 * EXPERTS)))
    last_grads = jnp.concatenate([grad_pairs.astype(bf16), grad_attn_t.astype(bf16), small], 1)
    last_share = lax.psum_scatter(last_grads, "dp", scatter_dimension=0, tiled=True).astype(f32)
    input_grad, activations = [], []
    for s in range(seqs):
        part = slice(s * half, (s + 1) * half)
        one_grad = dot_nt(back_own[s], w_pairs) + one_recv[s].astype(f32)
        input_grad.append(
            residual_grad[s] + norm_back(rows[s], inverse_one[s], gain_one, one_grad)
        )
        combined = result_rows[part] + result_recv[part].astype(f32)
        mixed = residual[s] + gate[part][:, None] * combined
        activations.append(jnp.where(valid_local[part][:, None], mixed, 0.0).astype(bf16))

    dp_rows = width // dp_size
    own_rows = dp_rows // 2

    def share_rows(array, axis=0):
        return lax.dynamic_slice_in_dim(array, dp_index * dp_rows, dp_rows, axis)

    pair_share = last_share[:, : 3 * inner]
    shares = [
        jnp.concatenate(
            [pair_share[:, (3 * p + k) * PAIR : (3 * p + k + 1) * PAIR] for p in range(pairs)], 1
        )
        for k in range(3)
    ]
    attn_share = last_share[:, 3 * inner : 4 * inner].T
    router_share = (
        last_share[:, 4 * inner : 4 * inner + EXPERTS]
        + last_share[:, 4 * inner + EXPERTS : 4 * inner + 2 * EXPERTS]
    )
    in_share = share_in.astype(f32)
    out_share = jnp.swapaxes(share_out_t, 1, 2).astype(f32)
    sum_one = jnp.sum(pair_share * share_rows(w_pairs).astype(f32), axis=1)
    sum_two = jnp.sum(in_share * share_rows(w_expert_in, 1).astype(f32), axis=(0, 2))
    sums = jnp.stack([sum_one, sum_two])
    sums = sums + swap(sums)
    router_sum = jnp.sum(router_share * share_rows(w_router).astype(f32), axis=1)
    gain_grads = jnp.stack(
        [sums[0] / share_rows(gain_one), (sums[1] + router_sum) / share_rows(gain_two)]
    )
    gain_grads = lax.dynamic_slice_in_dim(gain_grads, side * own_rows, own_rows, 1)
    router_out = lax.dynamic_slice_in_dim(router_share, side * own_rows, own_rows, 0)
    return (
        jnp.stack(activations),
        jnp.stack(input_grad),
        gain_grads[0],
        shares[0],
        shares[1],
        shares[2],
        attn_share,
        gain_grads[1],
        router_out,
        in_share,
        out_share,
    )


def solution(mesh):
    in_specs = (
        P("dp", "tensor", None),
        P("dp", "tensor", None),
        P("dp"),
        P("dp", None, None),
        P(),
        P(None, "tensor"),
        P(None, "tensor"),
        P(None, "tensor"),
        P("tensor", None),
        P(),
        P(),
        P(None, None, "tensor"),
        P(None, "tensor", None),
    )
    out_specs = (
        P("dp", "tensor", None),
        P("dp", "tensor", None),
        P(("dp", "tensor")),
        P("dp", "tensor"),
        P("dp", "tensor"),
        P("dp", "tensor"),
        P("tensor", "dp"),
        P(("dp", "tensor")),
        P(("dp", "tensor"), None),
        P(None, "dp", "tensor"),
        P(None, "tensor", "dp"),
    )
    return jax.shard_map(body, mesh=mesh, in_specs=in_specs, out_specs=out_specs, check_vma=False)
```

```python
import functools
import math

import jax
import jax.numpy as jnp
from jax import lax
from jax.experimental import pallas as pl
from jax.experimental.pallas import tpu as pltpu
from jax.sharding import PartitionSpec as P

HEAD_DIM = 64
EXPERTS = 4
CAP = 640
PAIR = 2 * HEAD_DIM
FORWARD_BLOCK = 320
BACKWARD_BLOCK = 320
GELU_C = math.sqrt(2.0 / math.pi)
GELU_A = 0.044715
LOG_SCALE = math.log2(math.e) * HEAD_DIM ** (-0.5)

norm_eps = 1e-06
bf16 = jnp.bfloat16
f32 = jnp.float32
SMALL_COST = pl.CostEstimate(flops=1, bytes_accessed=1, transcendentals=0)


def dot(left, right):
    return lax.dot_general(left, right, (((1,), (0,)), ((), ())), preferred_element_type=f32)


def dot_nt(left, right):
    return lax.dot_general(left, right, (((1,), (1,)), ((), ())), preferred_element_type=f32)


def dot_tn(left, right):
    return lax.dot_general(left, right, (((0,), (0,)), ((), ())), preferred_element_type=f32)


def whole_spec(shape):
    return pl.BlockSpec(shape, lambda *_: (0,) * len(shape))


SMEM_SPEC = pl.BlockSpec(memory_space=pltpu.SMEM)


def kernel_call(kernel, grid, in_specs, out_specs, out_shape, scratch, name, limit=58):
    return pl.pallas_call(
        kernel,
        grid=grid,
        in_specs=in_specs,
        out_specs=out_specs,
        out_shape=out_shape,
        scratch_shapes=scratch,
        compiler_params=pltpu.CompilerParams(vmem_limit_bytes=limit * 2**20),
        cost_estimate=SMALL_COST,
        name=name,
    )


def shaped(shape, dtype):
    return jax.ShapeDtypeStruct(shape, dtype)


def inverse_rms(rows):
    return lax.rsqrt(jnp.mean(rows * rows, axis=-1, keepdims=True) + norm_eps)


def norm_back(rows, inverse, gain, upstream):
    weighted = upstream * gain
    inner_mean = jnp.mean(rows * weighted, axis=-1, keepdims=True)
    return inverse * weighted - rows * inverse**3 * inner_mean


def as_column(row):
    return jnp.transpose(jnp.broadcast_to(row, (PAIR, row.shape[1])))[:, :1]


def plan_kernel(info, routes, slots_rows, slots_column, chosen, bounds):
    half = slots_rows.shape[1]
    side = info[2]
    before_of = lax.broadcasted_iota(jnp.int32, (half, half), 0)
    upto = jnp.where(before_of <= lax.broadcasted_iota(jnp.int32, (half, half), 1), 1.0, 0.0)
    upto = upto.astype(bf16)
    expert = lax.broadcasted_iota(jnp.int32, (8, half), 0)
    capacity = (5 * (info[0] + info[1]) + 4 * EXPERTS - 1) // (4 * EXPERTS)
    column = jnp.zeros((8, 1), f32)
    row = jnp.zeros((8, 8), f32)
    limit = capacity.astype(f32)
    for seq in range(2):
        for part in range(2):
            local = seq + jnp.where(side == part, 0, 2)
            route = routes[seq : seq + 1, part * half : (part + 1) * half]
            slot = lax.broadcasted_iota(jnp.int32, (1, half), 1) + part * half
            valid = slot < info[seq]
            routed = expert == route
            hit = jnp.where(jnp.logical_and(routed, valid), 1.0, 0.0)
            counts = dot(hit.astype(bf16), upto) + column
            position = jnp.sum(hit * counts, axis=0, keepdims=True).astype(jnp.int32) - 1
            keep = jnp.logical_and(valid, position < capacity)
            taken = jnp.where(keep, route * CAP + position, EXPERTS * CAP)
            slots_rows[pl.ds(local, 1), :] = taken
            first = pl.multiple_of(local * half, half)
            slots_column[pl.ds(first, half), :] = as_column(taken.astype(f32)).astype(jnp.int32)
            picked = jnp.where(expert == EXPERTS, jnp.where(valid, 1.0, 0.0), 0.0)
            chosen[:, pl.ds(first, half)] = jnp.where(routed, 1.0, picked)
            bounds[pl.ds(local, 1), :] = jnp.minimum(row[:1], limit).astype(jnp.int32)
            column += jnp.sum(hit, axis=1, keepdims=True)
            row += dot_nt(jnp.ones((8, half), bf16), hit.astype(bf16))
            bounds[pl.ds(4 + local, 1), :] = jnp.minimum(row[:1], limit).astype(jnp.int32)
    bounds[8:16, :] = jnp.minimum(row, limit).astype(jnp.int32)


def plan(info, routes):
    seqs, slots = routes.shape
    half = slots // 2
    return kernel_call(
        plan_kernel,
        (1,),
        [SMEM_SPEC, whole_spec((seqs, slots))],
        [
            whole_spec((4, half)),
            whole_spec((4 * half, 1)),
            whole_spec((8, 4 * half)),
            whole_spec((16, 8)),
        ],
        [
            shaped((4, half), jnp.int32),
            shaped((4 * half, 1), jnp.int32),
            shaped((8, 4 * half), f32),
            shaped((16, 8), jnp.int32),
        ],
        [],
        "plan",
    )(info, routes)


def project_kernel(rows, gain, weights, normed, proj):
    x = rows[...].astype(f32)
    low = (x * inverse_rms(x) * gain[...]).astype(bf16)
    normed[...] = low
    proj[...] = dot(low, weights[...]).astype(bf16)


def project(rows, gain, weights, name):
    count, width = rows.shape
    columns = weights.shape[1]
    block = min(256, count)
    tile = pl.BlockSpec((block, width), lambda i: (i, 0))
    return kernel_call(
        project_kernel,
        (count // block,),
        [tile, whole_spec((1, width)), whole_spec((width, columns))],
        [tile, pl.BlockSpec((block, columns), lambda i: (i, 0))],
        [shaped((count, width), bf16), shaped((count, columns), bf16)],
        [],
        name,
        40,
    )(rows, gain, weights)


def residual_kernel(rows, ctx_own, ctx_recv, w_own, w_oth, gain, residual, normed):
    total = rows[...].astype(f32) + dot(ctx_own[...], w_own[...])
    total += dot(ctx_recv[...], w_oth[...])
    residual[...] = total
    normed[...] = (total * inverse_rms(total) * gain[...]).astype(bf16)


def residual_of(rows, seq, ctx_own, ctx_recv, w_own, w_oth, gain):
    half, inner = ctx_own.shape
    width = rows.shape[1]
    block = min(256, half)
    steps = half // block
    tile = pl.BlockSpec((block, width), lambda i: (i, 0))
    ctx = pl.BlockSpec((block, inner), lambda i: (i, 0))
    weight = whole_spec((inner, width))
    return kernel_call(
        residual_kernel,
        (steps,),
        [
            pl.BlockSpec((block, width), lambda i: (i + seq * steps, 0)),
            ctx, ctx, weight, weight, whole_spec((1, width)),
        ],
        [tile, tile],
        [shaped((half, width), f32), shaped((half, width), bf16)],
        [],
        "residual",
        40,
    )(rows, ctx_own, ctx_recv, w_own, w_oth, gain)


def attend_kernel(query_rows, info, own, oth, ctx_own, ctx_oth, log_ref):
    half = own.shape[0]
    row = lax.broadcasted_iota(jnp.int32, (half, PAIR), 0)
    lane = lax.broadcasted_iota(jnp.int32, (half, PAIR), 1)
    zeros = jnp.zeros((half, PAIR), bf16)
    hidden_key = jnp.full((half, PAIR), -1e30, bf16)
    sides = ((own, ctx_own, row + info[1] < info[0]), (oth, ctx_oth, row + info[2] < info[0]))
    keys = []
    for head in range(2):
        mine = (lane < HEAD_DIM) == (head == 0)
        spare = lane == (HEAD_DIM if head == 0 else 0)
        parts = []
        for ref, _, seen in sides:
            mask_value = jnp.where(seen, zeros, hidden_key)
            key = ref[:, PAIR : 2 * PAIR]
            parts.append(jnp.where(mine, key, jnp.where(spare, mask_value, zeros)))
        keys.append(jnp.concatenate(parts, 0))
    values_t = jnp.transpose(jnp.concatenate([own[:, 2 * PAIR :], oth[:, 2 * PAIR :]], 0))
    q_lane = lax.broadcasted_iota(jnp.int32, (query_rows, PAIR), 1)
    steps = [
        (side, block, head)
        for side in range(2)
        for block in range(half // query_rows)
        for head in range(2)
    ]

    def scores_of(step):
        side, block, head = step
        query = sides[side][0][block * query_rows : (block + 1) * query_rows, :PAIR]
        mine = (q_lane < HEAD_DIM) == (head == 0)
        spare = q_lane == (HEAD_DIM if head == 0 else 0)
        query = jnp.where(
            mine, query, jnp.where(spare, jnp.ones_like(query), jnp.zeros_like(query))
        )
        return dot_nt(keys[head], query)

    current = scores_of(steps[0])
    outs = [None, None]
    for index, (side, block, head) in enumerate(steps):
        following = scores_of(steps[index + 1]) if index + 1 < len(steps) else None
        top = jnp.max(current, axis=0, keepdims=True) * LOG_SCALE
        exponent = jnp.exp2(current * LOG_SCALE - top)
        total = jnp.sum(exponent, axis=0, keepdims=True)
        head_values = values_t[head * HEAD_DIM : (head + 1) * HEAD_DIM, :]
        outs[head] = dot(head_values, exponent.astype(bf16)) * (1.0 / total)
        first = side * half + block * query_rows
        log_ref[head : head + 1, first : first + query_rows] = top + jnp.log2(total)
        if head == 1:
            sides[side][1][block * query_rows : (block + 1) * query_rows, :] = jnp.transpose(
                jnp.concatenate(outs, 0)
            ).astype(bf16)
        current = following


def attend(info, own, oth, seq):
    half, width = oth.shape
    pairs = width // (3 * PAIR)
    query_rows = min(512, half)
    out = pl.BlockSpec((half, PAIR), lambda p: (0, p))
    shape = jax.ShapeDtypeStruct((half, width // 3), bf16)
    return pl.pallas_call(
        functools.partial(attend_kernel, query_rows),
        grid=(pairs,),
        in_specs=[
            pl.BlockSpec(memory_space=pltpu.SMEM),
            pl.BlockSpec((half, 3 * PAIR), lambda p: (seq, p)),
            pl.BlockSpec((half, 3 * PAIR), lambda p: (0, p)),
        ],
        out_specs=[out, out, pl.BlockSpec((8, 2 * half), lambda p: (p, 0))],
        out_shape=[shape, shape, jax.ShapeDtypeStruct((8 * pairs, 2 * half), f32)],
        compiler_params=pltpu.CompilerParams(vmem_limit_bytes=40 * 2**20),
        cost_estimate=SMALL_COST,
        name="attend",
    )(info, own, oth)


WINDOW = 256


def window_rows(count_low, count_high):
    start = (count_low // 16) * 16
    windows = jnp.where(count_high > count_low, (count_high - start + WINDOW - 1) // WINDOW, 0)
    return start, windows


def dispatch_rows(bounds, slots, sources, total, expert):
    total[...] = jnp.zeros_like(total)
    for seg, source in enumerate(sources):
        start, windows = window_rows(bounds[seg, expert], bounds[4 + seg, expert])
        taken = slots[seg : seg + 1, :] - expert * CAP

        @pl.loop(0, windows)
        def _(step, start=start, taken=taken, source=source):
            begin = start + step * WINDOW
            row = pl.multiple_of(jnp.minimum(begin, CAP - WINDOW), 16)
            offset = jnp.where(taken >= begin, taken - row, -1)
            slot = lax.broadcasted_iota(jnp.int32, (WINDOW, offset.shape[1]), 0)
            place = jnp.where(slot == offset, 1.0, 0.0).astype(bf16)
            total[pl.ds(row, WINDOW), :] += dot(place, source[...])


def expert_forward_kernel(
    block, chunk, bounds, slots, seg0, seg1, seg2, seg3, w_in, w_out, w_route, chosen,
    x_out, hidden_out, slope_out, result_out, probs_out, gate_out, total,
):
    expert = pl.program_id(0)
    half = seg0.shape[0]

    @pl.when(expert == 0)
    def _():
        row = lax.broadcasted_iota(jnp.int32, (8, half), 0)
        for index, seg in enumerate((seg0, seg1, seg2, seg3)):
            part = slice(index * half, (index + 1) * half)
            logits = jnp.where(row < EXPERTS, dot_nt(w_route[...], seg[...]), -1e30)
            exponent = jnp.exp(logits - jnp.max(logits, axis=0, keepdims=True))
            probs = exponent / jnp.sum(exponent, axis=0, keepdims=True)
            probs = jnp.where(row < EXPERTS, probs, 0.0)
            probs_out[:, part] = probs
            gate = jnp.sum(probs * chosen[:, part], axis=0, keepdims=True)
            gate = jnp.where(chosen[EXPERTS : EXPERTS + 1, part] > 0, gate, 0.0)
            gate_out[part, :] = as_column(gate)

    dispatch_rows(bounds, slots, (seg0, seg1, seg2, seg3), total, expert)
    x_out[0] = total[...].astype(bf16)
    blocks = (bounds[8, expert] + block - 1) // block
    hidden_units = w_in.shape[2]
    columns = [slice(c, c + chunk) for c in range(0, hidden_units, chunk)]

    @pl.loop(0, blocks)
    def _(step):
        rows = pl.ds(pl.multiple_of(step * block, block), block)
        x = x_out[0, rows, :]
        pre = dot(x, w_in[0, :, columns[0]])
        result = None
        for index, cols in enumerate(columns):
            following = None
            if index + 1 < len(columns):
                following = dot(x, w_in[0, :, columns[index + 1]])
            square = pre * pre
            bend = jnp.tanh(pre * (GELU_C + GELU_C * GELU_A * square))
            half_up = 0.5 + 0.5 * bend
            hidden = (pre * half_up).astype(bf16)
            slope = half_up + pre * (0.5 * GELU_C + 1.5 * GELU_C * GELU_A * square) * (
                1.0 - bend * bend
            )
            hidden_out[0, rows, cols] = hidden
            slope_out[0, rows, cols] = slope.astype(bf16)
            part = dot(hidden, w_out[0, cols, :])
            result = part if result is None else result + part
            pre = following
        result_out[0, rows, :] = result.astype(bf16)

    @pl.loop(blocks, CAP // block)
    def _(step):
        rows = pl.ds(pl.multiple_of(step * block, block), block)
        hidden_out[0, rows, :] = jnp.zeros((block, hidden_units), bf16)
        slope_out[0, rows, :] = jnp.zeros((block, hidden_units), bf16)
        result_out[0, rows, :] = jnp.zeros((block, result_out.shape[2]), bf16)


def expert_backward_kernel(
    block, chunk, bounds, slots, cot_own, cot_oth, w_in, w_out, gate, hidden, slope,
    up_out, pre_out, back_out, total, gated,
):
    expert = pl.program_id(0)
    seqs, half = cot_own.shape[:2]
    parts = [pl.ds(index * half, half) for index in range(2 * seqs)]

    @pl.when(expert == 0)
    def _():
        for index, part in enumerate(parts):
            cot = (cot_own if index < seqs else cot_oth)[index % seqs].astype(f32)
            gated[part, :] = (gate[part, :] * cot).astype(bf16)

    dispatch_rows(bounds, slots, [gated.at[part] for part in parts], total, expert)
    up_out[0] = total[...].astype(bf16)
    blocks = (bounds[8, expert] + block - 1) // block
    width, hidden_units = w_in.shape[1], w_in.shape[2]
    columns = [slice(c, c + chunk) for c in range(0, hidden_units, chunk)]
    lane = lax.broadcasted_iota(jnp.int32, (block, PAIR), 1)

    @pl.loop(0, blocks)
    def _(step):
        rows = pl.ds(pl.multiple_of(step * block, block), block)
        up = up_out[0, rows, :]
        grad = dot_nt(up, w_out[0, columns[0], :])
        back, gate_grad = None, None
        for index, cols in enumerate(columns):
            following = None
            if index + 1 < len(columns):
                following = dot_nt(up, w_out[0, columns[index + 1], :])
            pre_grad = (grad * slope[0, rows, cols].astype(f32)).astype(bf16)
            pre_out[0, rows, cols] = pre_grad
            share = jnp.sum(grad * hidden[0, rows, cols].astype(f32), axis=1, keepdims=True)
            part = dot_nt(pre_grad, w_in[0, :, cols])
            back = part if back is None else back + part
            gate_grad = share if gate_grad is None else gate_grad + share
            grad = following
        back_out[0, rows, :width] = back.astype(bf16)
        high = gate_grad.astype(bf16).astype(f32)
        extra = jnp.where(lane == 0, high, jnp.where(lane == 1, gate_grad - high, 0.0))
        back_out[0, rows, width:] = extra.astype(bf16)

    @pl.loop(blocks, CAP // block)
    def _(step):
        rows = pl.ds(pl.multiple_of(step * block, block), block)
        pre_out[0, rows, :] = jnp.zeros((block, hidden_units), bf16)
        back_out[0, rows, :] = jnp.zeros((block, width + PAIR), bf16)


def slot_spec(columns):
    return pl.BlockSpec((1, CAP, columns), lambda e: (e, 0, 0))


def slot_shape(columns):
    return shaped((EXPERTS, CAP, columns), bf16)


def weight_spec(weights):
    return pl.BlockSpec((1,) + weights.shape[1:], lambda e: (e, 0, 0))


def expert_forward(bounds, slots, segments, w_in, w_out, w_route, chosen):
    _, width, hidden_units = w_in.shape
    half = segments[0].shape[0]
    return kernel_call(
        functools.partial(expert_forward_kernel, FORWARD_BLOCK, 512),
        (EXPERTS,),
        [SMEM_SPEC, whole_spec((4, half))]
        + [whole_spec((half, width))] * 4
        + [weight_spec(w_in), weight_spec(w_out), whole_spec((8, width)), whole_spec((8, 4 * half))],
        [
            slot_spec(width),
            slot_spec(hidden_units),
            slot_spec(hidden_units),
            slot_spec(width),
            whole_spec((8, 4 * half)),
            whole_spec((4 * half, 1)),
        ],
        [
            slot_shape(width),
            slot_shape(hidden_units),
            slot_shape(hidden_units),
            slot_shape(width),
            shaped((8, 4 * half), f32),
            shaped((4 * half, 1), f32),
        ],
        [pltpu.VMEM((CAP, width), f32)],
        "expert_forward",
    )(bounds, slots, *segments, w_in, w_out, w_route, chosen)


def expert_backward(bounds, slots, cot_own, cot_oth, w_in, w_out, gate, hidden, slope):
    _, width, hidden_units = w_in.shape
    half = slots.shape[1]
    return kernel_call(
        functools.partial(expert_backward_kernel, BACKWARD_BLOCK, 512),
        (EXPERTS,),
        [SMEM_SPEC, whole_spec((4, half)), whole_spec(cot_own.shape), whole_spec(cot_oth.shape)]
        + [weight_spec(w_in), weight_spec(w_out), whole_spec((4 * half, 1))]
        + [slot_spec(hidden_units), slot_spec(hidden_units)],
        [slot_spec(width), slot_spec(hidden_units), slot_spec(width + PAIR)],
        [slot_shape(width), slot_shape(hidden_units), slot_shape(width + PAIR)],
        [pltpu.VMEM((CAP, width), f32), pltpu.VMEM((4 * half, width), bf16)],
        "expert_backward",
    )(bounds, slots, cot_own, cot_oth, w_in, w_out, gate, hidden, slope)


def expert_grad_kernel(chunk, split, bounds, parity, left, right, mine, send, left_t):
    expert = pl.program_id(0)
    left_t[...] = jnp.transpose(left[0])
    taken, odd = bounds[8, expert], parity[0]
    sizes = [rows for rows in (256, 512) if rows < CAP] + [CAP]
    below = -1
    for rows in sizes:

        @pl.when(jnp.logical_and(taken > below, taken <= rows))
        def _(rows=rows):
            for c in range(0, right.shape[2], chunk):
                product = dot(left_t[:, :rows], right[0, :rows, c : c + chunk]).astype(bf16)
                if not split:
                    mine[0, :, c : c + chunk] = product
                    continue
                block = mine.shape[2]
                for pair in range(mine.shape[1]):
                    even = product[2 * pair * block : (2 * pair + 1) * block]
                    other = product[(2 * pair + 1) * block : (2 * pair + 2) * block]
                    mine[0, pair, :, c : c + chunk] = jnp.where(odd == 0, even, other)
                    send[0, pair, :, c : c + chunk] = jnp.where(odd == 0, other, even)

        below = rows


def expert_grad(bounds, parity, left, right, blocks, name):
    width, hidden_units = left.shape[2], right.shape[2]
    block = width // blocks
    split = block % 16 == 0
    shape = (EXPERTS, blocks // 2, block, hidden_units) if split else (EXPERTS, width, hidden_units)
    spec = pl.BlockSpec((1,) + shape[1:], lambda e: (e,) + (0,) * (len(shape) - 1))
    mine, send = kernel_call(
        functools.partial(expert_grad_kernel, 512, split),
        (EXPERTS,),
        [SMEM_SPEC, SMEM_SPEC, slot_spec(width), slot_spec(hidden_units)],
        [spec, spec],
        [shaped(shape, bf16)] * 2,
        [pltpu.VMEM((width, CAP), bf16)],
        name,
    )(bounds, parity, left, right)
    if split:
        return mine, send
    return split_even_odd(mine.reshape(EXPERTS, blocks, block, hidden_units), parity[0])


def collect_kernel(first_seg, segs, bounds, slots, rows_in, *refs):
    outs, total = refs[:-1], refs[-1]
    expert = pl.program_id(0)
    half = outs[0].shape[0] // segs

    @pl.when(expert == 0)
    def _():
        total[...] = jnp.zeros_like(total)

    for index in range(segs):
        seg = first_seg + index
        start, windows = window_rows(bounds[seg, expert], bounds[4 + seg, expert])
        part = slice(index * half, (index + 1) * half)
        taken = slots[part, :] - expert * CAP

        @pl.loop(0, windows)
        def _(step, start=start, part=part, taken=taken):
            begin = start + step * WINDOW
            row = pl.multiple_of(jnp.minimum(begin, CAP - WINDOW), 16)
            offset = jnp.where(taken >= begin, taken - row, -1)
            slot = lax.broadcasted_iota(jnp.int32, (half, WINDOW), 1)
            place = jnp.where(slot == offset, 1.0, 0.0).astype(bf16)
            total[part, :] += dot(place, rows_in[0, pl.ds(row, WINDOW), :])

    @pl.when(expert == EXPERTS - 1)
    def _():
        width = outs[0].shape[1]
        for index in range(segs):
            part = slice(index * half, (index + 1) * half)
            outs[0][part, :] = total[part, :width].astype(outs[0].dtype)
            if len(outs) > 1:
                outs[1][:, part] = jnp.transpose(total[part, width:])[:8, :]


def collect(bounds, slots_column, rows_in, first_seg, segs, width, dtype, name):
    columns = rows_in.shape[2]
    half = slots_column.shape[0] // 4
    out_specs = [pl.BlockSpec((segs * half, width), lambda e: (0, 0))]
    out_shape = [jax.ShapeDtypeStruct((segs * half, width), dtype)]
    if columns > width:
        out_specs.append(pl.BlockSpec((8, segs * half), lambda e: (0, 0)))
        out_shape.append(jax.ShapeDtypeStruct((8, segs * half), f32))
    return pl.pallas_call(
        functools.partial(collect_kernel, first_seg, segs),
        grid=(EXPERTS,),
        in_specs=[
            pl.BlockSpec(memory_space=pltpu.SMEM),
            pl.BlockSpec((segs * half, 1), lambda e: (first_seg // segs, 0)),
            slot_spec(columns),
        ],
        out_specs=out_specs,
        out_shape=out_shape,
        scratch_shapes=[pltpu.VMEM((segs * half, columns), f32)],
        compiler_params=pltpu.CompilerParams(vmem_limit_bytes=58 * 2**20),
        cost_estimate=SMALL_COST,
        name=name,
    )(bounds, slots_column, rows_in)


def residual_grad_kernel(
    seq, info, back_own, back_recv, probs, chosen, gate_own, gate_recv, w_route, residual, cot,
    gain, w_own, w_oth, grad_out, low_out, up_own, up_send,
):
    block = residual.shape[0]
    gate_grad = gate_own[:1, :] + gate_own[1:2, :] + gate_recv[:1, :] + gate_recv[1:2, :]
    logit_grad = jnp.where(
        lax.broadcasted_iota(jnp.int32, chosen.shape, 0) < EXPERTS, chosen[...] - probs[...], 0.0
    ) * gate_grad
    two_grad = back_own[...] + back_recv[...].astype(f32)
    for _ in range(3):
        part = logit_grad.astype(bf16)
        two_grad += dot_tn(part, w_route[...])
        logit_grad = logit_grad - part.astype(f32)
    rows = residual[...]
    slot = lax.broadcasted_iota(jnp.int32, (block, 1), 0) + pl.program_id(0) * block
    valid = slot + info[2] * (block * pl.num_programs(0)) < info[seq]
    upstream = jnp.where(valid, cot[...].astype(f32), 0.0)
    grad = upstream + norm_back(rows, inverse_rms(rows), gain[...], two_grad)
    grad_out[...] = grad
    low = grad.astype(bf16)
    low_out[...] = low
    up_send[...] = dot_nt(low, w_oth[...]).astype(bf16)
    up_own[...] = dot_nt(low, w_own[...]).astype(bf16)


def residual_grad_of(
    seq, info, back_own, back_recv, probs, chosen, gate_own, gate_recv, w_route, residual, cot,
    gain, w_own, w_oth,
):
    half, width = residual.shape
    inner = w_own.shape[0]
    block = min(256, half)
    steps = half // block
    tile = pl.BlockSpec((block, width), lambda i: (i, 0))
    seq_tile = pl.BlockSpec((block, width), lambda i: (i + seq * steps, 0))
    seq_columns = pl.BlockSpec((8, block), lambda i: (0, i + seq * steps))
    recv_columns = pl.BlockSpec((8, block), lambda i: (0, i + (seq + 2) * steps))
    ctx = pl.BlockSpec((block, inner), lambda i: (i, 0))
    weight = whole_spec((inner, width))
    return kernel_call(
        functools.partial(residual_grad_kernel, seq),
        (steps,),
        [SMEM_SPEC, seq_tile, seq_tile, seq_columns, seq_columns, seq_columns, recv_columns]
        + [whole_spec((8, width)), tile, seq_tile, whole_spec((1, width)), weight, weight],
        [tile, tile, ctx, ctx],
        [shaped((half, width), f32), shaped((half, width), bf16)] + [shaped((half, inner), bf16)] * 2,
        [],
        "residual_grad",
    )(
        info, back_own, back_recv, probs, chosen, gate_own, gate_recv, w_route, residual, cot,
        gain, w_own, w_oth,
    )


def attn_grad_kernel(
    low0, low1, own0, own1, recv0, recv1, seg0, seg1, seg2, seg3, probs, chosen, gate_all, gate_recv,
    own_out, send_out, router_out,
):
    low_t = [jnp.transpose(low0[...]), jnp.transpose(low1[...])]
    own_out[...] = dot(low_t[0], own0[...]) + dot(low_t[1], own1[...])
    send_out[...] = (dot(low_t[0], recv0[...]) + dot(low_t[1], recv1[...])).astype(bf16)
    half = seg0.shape[0]
    total = None
    for index, seg in enumerate((seg0, seg1, seg2, seg3)):
        part = slice(index * half, (index + 1) * half)
        far = (index + 2) % 4
        far = slice(far * half, (far + 1) * half)
        gate_grad = gate_all[:1, part] + gate_all[1:2, part] + gate_recv[:1, far] + gate_recv[1:2, far]
        row = lax.broadcasted_iota(jnp.int32, (8, half), 0)
        logit_grad = jnp.where(row < EXPERTS, chosen[:, part] - probs[:, part], 0.0) * gate_grad
        for _ in range(3):
            piece = logit_grad.astype(bf16)
            product = dot(piece, seg[...])
            total = product if total is None else total + product
            logit_grad = logit_grad - piece.astype(f32)
    router_out[...] = total


def attn_grad(low, ctx_own, ctx_recv, segments, probs, chosen, gate_all, gate_recv):
    half, width = low[0].shape
    inner = ctx_own[0].shape[1]
    columns = whole_spec((8, 4 * half))
    return kernel_call(
        attn_grad_kernel,
        (1,),
        [whole_spec((half, width))] * 2
        + [whole_spec((half, inner))] * 4
        + [whole_spec((half, width))] * 4
        + [columns] * 4,
        [whole_spec((width, inner)), whole_spec((width, inner)), whole_spec((8, width))],
        [shaped((width, inner), f32), shaped((width, inner), bf16), shaped((8, width), f32)],
        [],
        "attn_grad",
    )(*low, *ctx_own, *ctx_recv, *segments, probs, chosen, gate_all, gate_recv)


def attend_back_kernel(
    query_rows, last, split, info, parity, own, oth, ctx_own, ctx_oth, up_own, up_oth, log_ref,
    normed_own, normed_oth, weights, *refs,
):
    if last:
        before, one_own, one_oth, mine, send, key_sum, value_sum, grads, normed_t, one_sum = refs
    else:
        one_own, one_oth, mine, key_sum, value_sum, grads, normed_t, one_sum = refs
    half = own.shape[0]
    row = lax.broadcasted_iota(jnp.int32, (half, PAIR), 0)
    zeros = jnp.zeros((half, PAIR), bf16)
    seen = (row + info[1] < info[0], row + info[2] < info[0])
    sides = ((own, ctx_own, up_own), (oth, ctx_oth, up_oth))

    def all_keys(part):
        first, last = part * PAIR, (part + 1) * PAIR
        return jnp.concatenate(
            [
                jnp.where(seen[0], own[:, first:last], zeros),
                jnp.where(seen[1], oth[:, first:last], zeros),
            ],
            0,
        )

    keys, values = all_keys(1), all_keys(2)
    keys_t = jnp.transpose(keys)
    lane = lax.broadcasted_iota(jnp.int32, (query_rows, PAIR), 1)
    sum_lane = lax.broadcasted_iota(jnp.int32, (8, PAIR), 1)
    sum_row = lax.broadcasted_iota(jnp.int32, (8, PAIR), 0)
    head_sum = jnp.where((sum_lane < HEAD_DIM) == (sum_row == 0), 1.0, 0.0).astype(bf16)
    for side, (src, ctx, up) in enumerate(sides):
        for block in range(half // query_rows):
            rows = slice(block * query_rows, (block + 1) * query_rows)
            first = side * half + block * query_rows
            query, grad = src[rows, :PAIR], up[rows, :]
            product = grad.astype(f32) * ctx[rows, :].astype(f32)
            coarse = product.astype(bf16)
            fine = (product - coarse.astype(f32)).astype(bf16)
            delta = dot_nt(head_sum, coarse) + dot_nt(head_sum, fine)
            query_grads, key_grads, value_grads = [], [], []
            for head in range(2):
                of_head = (lane < HEAD_DIM) == (head == 0)
                query_h = jnp.where(of_head, query, jnp.zeros_like(query))
                grad_h = jnp.where(of_head, grad, jnp.zeros_like(grad))
                log_row = log_ref[head : head + 1, first : first + query_rows]
                scores = dot_nt(keys, query_h)
                probs = jnp.exp2(jnp.minimum(scores * LOG_SCALE - log_row, 0.0))
                prob_grad = dot_nt(values, grad_h)
                score_grad = (probs * (prob_grad - delta[head : head + 1, :])).astype(bf16)
                value_grads.append(dot(probs.astype(bf16), grad_h))
                key_grads.append(dot(score_grad, query_h))
                query_grads.append(
                    dot(keys_t[head * HEAD_DIM : (head + 1) * HEAD_DIM, :], score_grad)
                )
            value_grad = value_grads[0] + value_grads[1]
            key_grad = key_grads[0] + key_grads[1]
            if side == 0 and block == 0:
                value_sum[...] = value_grad
                key_sum[...] = key_grad
            else:
                value_sum[...] += value_grad
                key_sum[...] += key_grad
            query_grad = jnp.transpose(jnp.concatenate(query_grads, 0)) * HEAD_DIM ** (-0.5)
            grads[first : first + query_rows, :PAIR] = query_grad.astype(bf16)
    for side in range(2):
        part = slice(side * half, (side + 1) * half)
        key_grad = jnp.where(seen[side], key_sum[part, :] * HEAD_DIM ** (-0.5), 0.0)
        grads[part, PAIR : 2 * PAIR] = key_grad.astype(bf16)
        grads[part, 2 * PAIR :] = jnp.where(seen[side], value_sum[part, :], 0.0).astype(bf16)

    pair = pl.program_id(0)

    @pl.when(pair == 0)
    def _():
        normed_t[:, :half] = jnp.transpose(normed_own[...])
        normed_t[:, half:] = jnp.transpose(normed_oth[...])
        one_sum[...] = jnp.zeros_like(one_sum)

    one_sum[...] += dot_nt(grads[...], weights[...])

    @pl.when(pair == pl.num_programs(0) - 1)
    def _():
        one_own[...] = one_sum[:half, :]
        one_oth[...] = one_sum[half:, :].astype(bf16)

    product = dot(normed_t[...], grads[...])
    if not last:
        mine[...] = product
        return
    product = (product + before[...]).astype(bf16)
    if not split:
        mine[...] = product
        return
    block = mine.shape[1]
    odd = parity[0]
    for index in range(mine.shape[0]):
        even = product[2 * index * block : (2 * index + 1) * block]
        other = product[(2 * index + 1) * block : (2 * index + 2) * block]
        mine[index] = jnp.where(odd == 0, even, other)
        send[index] = jnp.where(odd == 0, other, even)


def attend_back(
    info, parity, own, oth, seq, ctx_own, ctx_oth, up_own, up_oth, logs, normed_own, normed_oth,
    weights, blocks, before=None,
):
    half, columns = oth.shape
    width = weights.shape[0]
    pairs = columns // (3 * PAIR)
    query_rows = min(256, half)
    block = width // blocks
    split = block % 16 == 0
    last = before is not None
    one = pl.BlockSpec((half, PAIR), lambda p: (0, p))
    three = pl.BlockSpec((half, 3 * PAIR), lambda p: (0, p))
    weight = pl.BlockSpec((width, 3 * PAIR), lambda p: (0, p))
    out_specs = [whole_spec((half, width)), whole_spec((half, width))]
    out_shape = [shaped((half, width), f32), shaped((half, width), bf16)]
    if not last:
        out_specs.append(weight)
        out_shape.append(shaped((width, columns), f32))
    elif split:
        out_specs += [pl.BlockSpec((blocks // 2, block, 3 * PAIR), lambda p: (0, 0, p))] * 2
        out_shape += [shaped((blocks // 2, block, columns), bf16)] * 2
    else:
        out_specs += [weight, weight]
        out_shape += [shaped((width, columns), bf16)] * 2
    outs = kernel_call(
        functools.partial(attend_back_kernel, query_rows, last, split),
        (pairs,),
        [SMEM_SPEC, SMEM_SPEC, pl.BlockSpec((half, 3 * PAIR), lambda p: (seq, p)), three]
        + [one] * 4
        + [pl.BlockSpec((8, 2 * half), lambda p: (p, 0))]
        + [pl.BlockSpec((half, width), lambda p: (seq, 0)), whole_spec((half, width)), weight]
        + ([weight] if last else []),
        out_specs,
        out_shape,
        [
            pltpu.VMEM((2 * half, PAIR), f32),
            pltpu.VMEM((2 * half, PAIR), f32),
            pltpu.VMEM((2 * half, 3 * PAIR), bf16),
            pltpu.VMEM((width, 2 * half), bf16),
            pltpu.VMEM((2 * half, width), f32),
        ],
        "attend_back",
        48,
    )(
        info, parity, own, oth, ctx_own, ctx_oth, up_own, up_oth, logs, normed_own, normed_oth,
        weights, *([before] if last else []),
    )
    if last and not split:
        outs = list(outs[:2]) + list(split_even_odd(outs[2].reshape(blocks, block, columns), parity[0]))
    return outs


def finish_kernel(
    steps, info, rows, one_own0, one_own1, recv0, recv1, grad0, grad1, res0, res1, result_own,
    result_recv, gate, gain, input_grad, activations,
):
    step = pl.program_id(0)
    block = rows.shape[0]
    for seq, refs in enumerate(((one_own0, recv0, grad0, res0), (one_own1, recv1, grad1, res1))):

        @pl.when(step // steps == seq)
        def _(seq=seq, refs=refs):
            one_own, recv, grad, res = refs
            x = rows[...].astype(f32)
            one_grad = one_own[...] + recv[...].astype(f32)
            input_grad[...] = grad[...] + norm_back(x, inverse_rms(x), gain[...], one_grad)
            combined = result_own[...].astype(f32) + result_recv[...].astype(f32)
            mixed = res[...] + gate[...] * combined
            slot = lax.broadcasted_iota(jnp.int32, (block, 1), 0) + step % steps * block
            valid = slot + info[2] * (steps * block) < info[seq]
            activations[...] = jnp.where(valid, mixed, 0.0).astype(bf16)


def finish(info, rows, one_own, one_recv, grads, residual, result_own, result_recv, gate, gain):
    half, width = residual[0].shape
    block = min(256, half)
    steps = half // block
    tile = pl.BlockSpec((block, width), lambda i: (i, 0))
    first = pl.BlockSpec((block, width), lambda i: (jnp.minimum(i, steps - 1), 0))
    second = pl.BlockSpec((block, width), lambda i: (jnp.maximum(i - steps, 0), 0))
    return kernel_call(
        functools.partial(finish_kernel, steps),
        (2 * steps,),
        [SMEM_SPEC, tile]
        + [first, second] * 4
        + [tile, tile, pl.BlockSpec((block, 1), lambda i: (i, 0)), whole_spec((1, width))],
        [tile, tile],
        [shaped((2 * half, width), f32), shaped((2 * half, width), bf16)],
        [],
        "finish",
    )(info, rows, *one_own, *one_recv, *grads, *residual, result_own, result_recv, gate, gain)


def after(array, *earlier):
    return lax.optimization_barrier((array,) + earlier)[0]


def split_even_odd(array, odd):
    lead = array.shape[:-3]
    halves = array.reshape(lead + (array.shape[-3] // 2, 2) + array.shape[-2:])
    axis = len(lead) + 1
    return (
        lax.dynamic_index_in_dim(halves, odd, axis, keepdims=False),
        lax.dynamic_index_in_dim(halves, 1 - odd, axis, keepdims=False),
    )


class Halving:
    def __init__(self, parts, experts, block, bits, table, order):
        self.parts = [(array, total, first, list(bits)) for array, total, first in parts]
        self.experts, self.block, self.table = experts, block, table
        self.left, self.order, self.picked = list(bits), list(order), set()
        self.size = len(bits) + 1
        self.columns = parts[0][0].shape[-1]

    def total(self, row, dtype, transpose=False):
        size, picked = self.size, set(self.picked)
        arrays, specs = [], []
        for array, total, first, bits in self.parts:
            arrays.append(array.reshape((total,) + (2,) * len(bits) + (self.block, self.columns)))
            shape = tuple(None if bit in picked else 2 for bit in bits)

            def place(expert, table, first=first, bits=bits):
                picks = tuple(table[row * size + bit] if bit in picked else 0 for bit in bits)
                return (first + expert,) + picks + (0, 0)

            specs.append(pl.BlockSpec((1,) + shape + (self.block, self.columns), place))
        tail = (self.columns, self.block) if transpose else (self.block, self.columns)
        out = (self.experts,) + (2,) * len(self.left) + tail

        def kernel(table, *refs):
            value = refs[0][...].astype(f32)
            for ref in refs[1:-1]:
                value += ref[...].astype(f32)
            if transpose:
                refs[-1][0] = jnp.transpose(value[0]).astype(dtype)
            else:
                refs[-1][...] = value.astype(dtype)

        return pl.pallas_call(
            kernel,
            grid_spec=pltpu.PrefetchScalarGridSpec(
                num_scalar_prefetch=1,
                grid=(self.experts,),
                in_specs=specs,
                out_specs=pl.BlockSpec((1,) + out[1:], lambda e, t: (e,) + (0,) * (len(out) - 1)),
            ),
            out_shape=shaped(out, dtype),
            compiler_params=pltpu.CompilerParams(vmem_limit_bytes=58 * 2**20),
            cost_estimate=SMALL_COST,
            name="half_sum",
        )(self.table, *arrays)

    def send(self):
        bit = self.order[0]
        self.left.remove(bit)
        self.picked.add(bit)
        sent = self.total(bit, bf16)
        return sent.reshape(-1, self.columns)

    def step(self, sent):
        recv = exchange(sent, self.order.pop(0), 2**self.size)
        self.parts.append((recv, self.experts, 0, list(self.left)))

    def last_recv(self, *earlier):
        array, *rest = self.parts[-1]
        if earlier:
            self.parts[-1] = (after(array, *earlier), *rest)
        return self.parts[-1][0]


def exchange(array, bit, size):
    return lax.ppermute(array, "dp", [(i, i ^ (1 << bit)) for i in range(size)])


def body(
    inputs,
    cotangent,
    lengths,
    routes,
    norm1_gain,
    w_query,
    w_key,
    w_value,
    w_attn_out,
    norm2_gain,
    w_router,
    w_expert_in,
    w_expert_out,
):
    seqs, half, width = inputs.shape
    slots = routes.shape[1]
    inner = w_query.shape[1]
    pairs = inner // PAIR
    side = lax.axis_index("tensor")
    dp_index = lax.axis_index("dp")
    dp_size = lax.axis_size("dp")
    own_tokens = seqs * half
    gain_one = norm1_gain.astype(f32)[None, :]
    gain_two = norm2_gain.astype(f32)[None, :]

    def swap(array):
        return lax.ppermute(array, "tensor", [(0, 1), (1, 0)])

    dp_rows = width // dp_size
    bits = dp_size.bit_length() - 1
    parity = (dp_index & 1).reshape(1).astype(jnp.int32)
    rows = inputs.reshape(own_tokens, width)
    cot_rows = cotangent.reshape(own_tokens, width)
    rows_oth = [swap(inputs[0])]
    info = jnp.concatenate([lengths, side[None]]).astype(jnp.int32)
    infos = [
        jnp.stack([lengths[s], side * half, (1 - side) * half]).astype(jnp.int32)
        for s in range(seqs)
    ]
    slots_rows, slots_column, chosen, bounds = plan(info, routes.reshape(seqs, slots))
    w_pairs = jnp.concatenate(
        [w[:, p * PAIR : (p + 1) * PAIR] for p in range(pairs) for w in (w_query, w_key, w_value)],
        1,
    )
    flips = (dp_index >> jnp.arange(bits)) & 1
    table = jnp.concatenate(
        [(flips[None, :] ^ jnp.eye(bits, dtype=flips.dtype)).reshape(-1), flips]
    ).astype(jnp.int32)
    w_route = jnp.pad(w_router.T, ((0, 8 - EXPERTS), (0, 0)))
    normed_own, proj_own = project(rows, gain_one, w_pairs, "project_own")
    first_in = after(rows_oth[0], proj_own, bounds, w_route, table)
    rows_oth[0] = first_in
    for s in range(1, seqs):
        rows_oth.append(swap(after(inputs, rows_oth[-1])[s]))
    normed_oth, proj_oth, ctx_own, ctx_oth, ctx_recv, logs = [], [], [], [], [], []
    for s in range(seqs):
        raw = rows_oth[s] if s == 0 else after(rows_oth[s], ctx_oth[s - 1])
        if s == 1:
            odd = dp_index & 1
            piece = inner // 2
            attn_piece = lax.dynamic_slice_in_dim(w_attn_out, odd * piece, piece, 0)
            attn_piece = swap(after(attn_piece, raw))
            other = exchange(attn_piece, 0, dp_size)
            attn_out_oth = jnp.concatenate(
                [jnp.where(odd == 0, attn_piece, other), jnp.where(odd == 0, other, attn_piece)], 0
            )
        normed_part, proj_part = project(raw, gain_one, w_pairs, "project_oth")
        normed_oth.append(normed_part)
        proj_oth.append(proj_part)
        own_part, oth_part, log_part = attend(infos[s], proj_own, proj_part, s)
        ctx_own.append(own_part)
        ctx_oth.append(oth_part)
        logs.append(log_part)
        ctx_recv.append(swap(oth_part))
    residual, normed_two, two_oth = [], [], []
    for s in range(seqs):
        ctx_recv[s] = after(ctx_recv[s], ctx_oth[-1] if s == 0 else normed_two[s - 1])
        res_part, normed_part = residual_of(
            rows, s, ctx_own[s], ctx_recv[s], w_attn_out, attn_out_oth, gain_two
        )
        residual.append(res_part)
        normed_two.append(normed_part)
        two_oth.append(swap(normed_part))

    segments = normed_two + two_oth
    cot_oth = swap(after(cotangent, *two_oth))
    x_rows, hidden, slope, result, probs, gate = expert_forward(
        bounds, slots_rows, segments, w_expert_in, w_expert_out, w_route, chosen
    )
    (result_oth,) = collect(
        bounds, slots_column, result, seqs, seqs, width, bf16, "collect_result_oth"
    )
    (result_own,) = collect(
        bounds, slots_column, after(result, result_oth), 0, seqs, width, bf16, "collect_result_own"
    )
    cot_oth = after(cot_oth, result_own)
    up_rows, pre_grad, back = expert_backward(
        bounds, slots_rows, cotangent, cot_oth, w_expert_in, w_expert_out, gate, hidden, slope
    )
    back_oth, gate_oth = collect(
        bounds, slots_column, back, seqs, seqs, width, bf16, "collect_back_oth"
    )
    back_recv = swap(back_oth)
    halved = list(range(bits - 1, 0, -1))
    order_x = list(range(1, bits))
    order_z = list(range(2, bits)) + [1]
    columns = w_expert_in.shape[2]
    out_mine, out_send = expert_grad(
        after(bounds, back_oth), parity, up_rows, hidden, dp_size, "grad_expert_out"
    )
    out_recv = exchange(out_send.reshape(-1, columns), 0, dp_size)
    back_own, gate_own = collect(
        bounds, slots_column, after(back, out_mine), 0, seqs, width, f32, "collect_back_own"
    )
    gate_all = jnp.concatenate([gate_own, gate_oth], 1)
    gate_recv = swap(gate_all)
    in_mine, in_send = expert_grad(
        after(bounds, back_own), parity, x_rows, pre_grad, dp_size, "grad_expert_in"
    )
    recv = after(back_recv, in_mine, gate_recv)
    in_recv = exchange(after(in_send, recv).reshape(-1, columns), 0, dp_size)

    def halvings(mine, recv, order):
        parts = [(mine.reshape(-1, columns), EXPERTS, 0), (recv, EXPERTS, 0)]
        return [Halving(parts, EXPERTS, dp_rows, halved, table, order)]

    residual_grad, residual_low, up_own, up_oth = [], [], [], []
    out_sums = in_sums = None
    for s in range(seqs):
        grad_part, low_part, own_part, send_part = residual_grad_of(
            s, info, back_own, recv, probs, chosen, gate_all, gate_recv, w_route, residual[s],
            cot_rows, gain_two, w_attn_out, attn_out_oth,
        )
        residual_grad.append(grad_part)
        residual_low.append(low_part)
        up_own.append(own_part)
        up_oth.append(swap(send_part))
        if s == 0:
            out_sums = halvings(out_mine, after(out_recv, send_part), order_z)
            sents = [part.send() for part in out_sums]
            recv = after(recv, *sents)
        else:
            in_sums = halvings(in_mine, after(in_recv, send_part), order_x)
            sents += [part.send() for part in in_sums]
    sums = out_sums + in_sums
    for part, sent in zip(sums, sents):
        part.step(sent)
    low_late = after(residual_low[0], *sents)
    grad_attn_t, grad_attn_send, grad_router = attn_grad(
        [low_late] + residual_low[1:], ctx_own, ctx_recv, segments, probs, chosen, gate_all, gate_recv
    )
    grad_attn_recv = swap(after(grad_attn_send, up_oth[-1]))
    result_recv = swap(after(result_oth, grad_attn_send))

    log_rows = after(logs[0], grad_attn_t)
    one_own0, one_oth0, grad_pairs = attend_back(
        infos[0], parity, proj_own, proj_oth[0], 0, ctx_own[0], ctx_oth[0], up_own[0], up_oth[0],
        log_rows, normed_own, normed_oth[0], w_pairs, dp_size,
    )
    one_recv = [swap(one_oth0)]
    for part in sums:
        part.last_recv(one_oth0)
    sents = [part.send() for part in sums]
    grad_attn_t = grad_attn_t + after(grad_attn_recv, one_oth0).astype(f32)
    grad_router = after(grad_router, one_oth0)[:EXPERTS].T
    router_high = grad_router.astype(bf16)
    router_low = (grad_router - router_high.astype(f32)).astype(bf16)
    small = jnp.concatenate([router_high, router_low], 1)
    small = jnp.pad(small, ((0, 0), (0, PAIR - 2 * EXPERTS)))
    rest = jnp.concatenate([grad_attn_t.astype(bf16), small], 1).reshape(dp_size, dp_rows, -1)
    rest = split_even_odd(rest, parity[0])
    log_rows = after(logs[1], *rest, *sents)
    one_own1, one_oth1, *grad_pairs = attend_back(
        infos[1], parity, proj_own, proj_oth[1], 1, ctx_own[1], ctx_oth[1], up_own[1], up_oth[1],
        log_rows, normed_own, normed_oth[1], w_pairs, dp_size, grad_pairs,
    )
    for part, sent in zip(sums, sents):
        part.step(sent)
    recvs = [part.last_recv() for part in sums]
    one_recv.append(swap(one_oth1))
    last_mine, last_send = [jnp.concatenate(pair, 2) for pair in zip(grad_pairs, rest)]
    last_columns = last_mine.shape[-1]
    last_send = after(last_send.reshape(-1, last_columns), one_recv[0], result_recv, *recvs)
    last_recv = exchange(last_send, 0, dp_size)
    last_sum = Halving(
        [(last_mine.reshape(-1, last_columns), 1, 0), (last_recv, 1, 0)],
        1, dp_rows, halved, table, order_x,
    )
    for part in sums:
        part.last_recv(last_send)
        part.step(part.send())
    while last_sum.order:
        last_sum.step(last_sum.send())
    for part in sums:
        while part.order:
            part.step(part.send())
    recv_last = after(one_recv[1], *[part.last_recv() for part in sums])
    input_grad, activations = finish(
        info, rows, (one_own0, one_own1), (one_recv[0], recv_last), residual_grad, residual,
        result_own, result_recv, gate, gain_one,
    )
    last_share = last_sum.total(bits, f32)[0]
    out_share = out_sums[0].total(bits, f32, True)
    in_share = in_sums[0].total(bits, f32)

    own_rows = dp_rows // 2

    def share_rows(array, axis=0):
        return lax.dynamic_slice_in_dim(array, dp_index * dp_rows, dp_rows, axis)

    pair_share = last_share[:, : 3 * inner]
    shares = [
        jnp.concatenate(
            [pair_share[:, (3 * p + k) * PAIR : (3 * p + k + 1) * PAIR] for p in range(pairs)], 1
        )
        for k in range(3)
    ]
    attn_share = last_share[:, 3 * inner : 4 * inner].T
    router_share = (
        last_share[:, 4 * inner : 4 * inner + EXPERTS]
        + last_share[:, 4 * inner + EXPERTS : 4 * inner + 2 * EXPERTS]
    )
    sum_one = jnp.sum(pair_share * share_rows(w_pairs).astype(f32), axis=1)
    sum_two = jnp.sum(in_share * share_rows(w_expert_in, 1).astype(f32), axis=(0, 2))
    sums = jnp.stack([sum_one, sum_two])
    sums = sums + swap(sums)
    router_sum = jnp.sum(router_share * share_rows(w_router).astype(f32), axis=1)
    gain_grads = jnp.stack(
        [sums[0] / share_rows(gain_one[0]), (sums[1] + router_sum) / share_rows(gain_two[0])]
    )
    gain_grads = lax.dynamic_slice_in_dim(gain_grads, side * own_rows, own_rows, 1)
    router_out = lax.dynamic_slice_in_dim(router_share, side * own_rows, own_rows, 0)
    return (
        activations.reshape(inputs.shape),
        input_grad.reshape(inputs.shape),
        gain_grads[0],
        shares[0],
        shares[1],
        shares[2],
        attn_share,
        gain_grads[1],
        router_out,
        in_share,
        out_share,
    )


def solution(mesh):
    in_specs = (
        P("dp", "tensor", None),
        P("dp", "tensor", None),
        P("dp"),
        P("dp", None, None),
        P(),
        P(None, "tensor"),
        P(None, "tensor"),
        P(None, "tensor"),
        P("tensor", None),
        P(),
        P(),
        P(None, None, "tensor"),
        P(None, "tensor", None),
    )
    out_specs = (
        P("dp", "tensor", None),
        P("dp", "tensor", None),
        P(("dp", "tensor")),
        P("dp", "tensor"),
        P("dp", "tensor"),
        P("dp", "tensor"),
        P("tensor", "dp"),
        P(("dp", "tensor")),
        P(("dp", "tensor"), None),
        P(None, "dp", "tensor"),
        P(None, "tensor", "dp"),
    )
    return jax.shard_map(body, mesh=mesh, in_specs=in_specs, out_specs=out_specs, check_vma=False)
```

```python
import functools
import math

import jax
import jax.numpy as jnp
from jax import lax
from jax.experimental import pallas as pl
from jax.experimental.pallas import tpu as pltpu
from jax.sharding import PartitionSpec as P

HEAD_DIM = 64
EXPERTS = 4
CAP = 640
PAIR = 2 * HEAD_DIM
FORWARD_BLOCK = 320
BACKWARD_BLOCK = 320
GELU_C = math.sqrt(2.0 / math.pi)
GELU_A = 0.044715
LOG_SCALE = math.log2(math.e) * HEAD_DIM ** (-0.5)

norm_eps = 1e-06
bf16 = jnp.bfloat16
f32 = jnp.float32
SMALL_COST = pl.CostEstimate(flops=1, bytes_accessed=1, transcendentals=0)


def dot(left, right):
    return lax.dot_general(left, right, (((1,), (0,)), ((), ())), preferred_element_type=f32)


def dot_nt(left, right):
    return lax.dot_general(left, right, (((1,), (1,)), ((), ())), preferred_element_type=f32)


def dot_tn(left, right):
    return lax.dot_general(left, right, (((0,), (0,)), ((), ())), preferred_element_type=f32)


def whole_spec(shape):
    return pl.BlockSpec(shape, lambda *_: (0,) * len(shape))


SMEM_SPEC = pl.BlockSpec(memory_space=pltpu.SMEM)


def kernel_call(kernel, grid, in_specs, out_specs, out_shape, scratch, name, limit=58):
    return pl.pallas_call(
        kernel,
        grid=grid,
        in_specs=in_specs,
        out_specs=out_specs,
        out_shape=out_shape,
        scratch_shapes=scratch,
        compiler_params=pltpu.CompilerParams(vmem_limit_bytes=limit * 2**20),
        cost_estimate=SMALL_COST,
        name=name,
    )


def shaped(shape, dtype):
    return jax.ShapeDtypeStruct(shape, dtype)


def inverse_rms(rows):
    return lax.rsqrt(jnp.mean(rows * rows, axis=-1, keepdims=True) + norm_eps)


def norm_back(rows, inverse, gain, upstream):
    weighted = upstream * gain
    inner_mean = jnp.mean(rows * weighted, axis=-1, keepdims=True)
    return inverse * weighted - rows * inverse**3 * inner_mean


def as_column(row):
    return jnp.transpose(jnp.broadcast_to(row, (PAIR, row.shape[1])))[:, :1]


def plan_kernel(info, routes, slots_rows, slots_column, chosen, bounds):
    half = slots_rows.shape[1]
    side = info[2]
    before_of = lax.broadcasted_iota(jnp.int32, (half, half), 0)
    upto = jnp.where(before_of <= lax.broadcasted_iota(jnp.int32, (half, half), 1), 1.0, 0.0)
    upto = upto.astype(bf16)
    expert = lax.broadcasted_iota(jnp.int32, (8, half), 0)
    capacity = (5 * (info[0] + info[1]) + 4 * EXPERTS - 1) // (4 * EXPERTS)
    column = jnp.zeros((8, 1), f32)
    row = jnp.zeros((8, 8), f32)
    limit = capacity.astype(f32)
    for seq in range(2):
        for part in range(2):
            local = seq + jnp.where(side == part, 0, 2)
            route = routes[seq : seq + 1, part * half : (part + 1) * half]
            slot = lax.broadcasted_iota(jnp.int32, (1, half), 1) + part * half
            valid = slot < info[seq]
            routed = expert == route
            hit = jnp.where(jnp.logical_and(routed, valid), 1.0, 0.0)
            counts = dot(hit.astype(bf16), upto) + column
            position = jnp.sum(hit * counts, axis=0, keepdims=True).astype(jnp.int32) - 1
            keep = jnp.logical_and(valid, position < capacity)
            taken = jnp.where(keep, route * CAP + position, EXPERTS * CAP)
            slots_rows[pl.ds(local, 1), :] = taken
            first = pl.multiple_of(local * half, half)
            slots_column[pl.ds(first, half), :] = as_column(taken.astype(f32)).astype(jnp.int32)
            picked = jnp.where(expert == EXPERTS, jnp.where(valid, 1.0, 0.0), 0.0)
            chosen[:, pl.ds(first, half)] = jnp.where(routed, 1.0, picked)
            bounds[pl.ds(local, 1), :] = jnp.minimum(row[:1], limit).astype(jnp.int32)
            column += jnp.sum(hit, axis=1, keepdims=True)
            row += dot_nt(jnp.ones((8, half), bf16), hit.astype(bf16))
            bounds[pl.ds(4 + local, 1), :] = jnp.minimum(row[:1], limit).astype(jnp.int32)
    bounds[8:16, :] = jnp.minimum(row, limit).astype(jnp.int32)


def plan(info, routes):
    seqs, slots = routes.shape
    half = slots // 2
    return kernel_call(
        plan_kernel,
        (1,),
        [SMEM_SPEC, whole_spec((seqs, slots))],
        [
            whole_spec((4, half)),
            whole_spec((4 * half, 1)),
            whole_spec((8, 4 * half)),
            whole_spec((16, 8)),
        ],
        [
            shaped((4, half), jnp.int32),
            shaped((4 * half, 1), jnp.int32),
            shaped((8, 4 * half), f32),
            shaped((16, 8), jnp.int32),
        ],
        [],
        "plan",
    )(info, routes)


def project_kernel(rows, gain, weights, normed, proj):
    x = rows[...].astype(f32)
    low = (x * inverse_rms(x) * gain[...]).astype(bf16)
    normed[...] = low
    proj[...] = dot(low, weights[...]).astype(bf16)


def project(rows, gain, weights, name):
    count, width = rows.shape
    columns = weights.shape[1]
    block = min(256, count)
    tile = pl.BlockSpec((block, width), lambda i: (i, 0))
    return kernel_call(
        project_kernel,
        (count // block,),
        [tile, whole_spec((1, width)), whole_spec((width, columns))],
        [tile, pl.BlockSpec((block, columns), lambda i: (i, 0))],
        [shaped((count, width), bf16), shaped((count, columns), bf16)],
        [],
        name,
        40,
    )(rows, gain, weights)


def residual_kernel(rows, ctx_own, ctx_recv, w_own, w_oth, gain, residual, normed):
    total = rows[...].astype(f32) + dot(ctx_own[...], w_own[...])
    total += dot(ctx_recv[...], w_oth[...])
    residual[...] = total
    normed[...] = (total * inverse_rms(total) * gain[...]).astype(bf16)


def residual_of(rows, seq, ctx_own, ctx_recv, w_own, w_oth, gain):
    half, inner = ctx_own.shape
    width = rows.shape[1]
    block = min(256, half)
    steps = half // block
    tile = pl.BlockSpec((block, width), lambda i: (i, 0))
    ctx = pl.BlockSpec((block, inner), lambda i: (i, 0))
    weight = whole_spec((inner, width))
    return kernel_call(
        residual_kernel,
        (steps,),
        [
            pl.BlockSpec((block, width), lambda i: (i + seq * steps, 0)),
            ctx, ctx, weight, weight, whole_spec((1, width)),
        ],
        [tile, tile],
        [shaped((half, width), f32), shaped((half, width), bf16)],
        [],
        "residual",
        40,
    )(rows, ctx_own, ctx_recv, w_own, w_oth, gain)


def attend_kernel(query_rows, info, own, oth, ctx_own, ctx_oth, log_ref):
    half = own.shape[0]
    row = lax.broadcasted_iota(jnp.int32, (half, PAIR), 0)
    lane = lax.broadcasted_iota(jnp.int32, (half, PAIR), 1)
    zeros = jnp.zeros((half, PAIR), bf16)
    hidden_key = jnp.full((half, PAIR), -1e30, bf16)
    sides = ((own, ctx_own, row + info[1] < info[0]), (oth, ctx_oth, row + info[2] < info[0]))
    keys = []
    for head in range(2):
        mine = (lane < HEAD_DIM) == (head == 0)
        spare = lane == (HEAD_DIM if head == 0 else 0)
        parts = []
        for ref, _, seen in sides:
            mask_value = jnp.where(seen, zeros, hidden_key)
            key = ref[:, PAIR : 2 * PAIR]
            parts.append(jnp.where(mine, key, jnp.where(spare, mask_value, zeros)))
        keys.append(jnp.concatenate(parts, 0))
    values_t = jnp.transpose(jnp.concatenate([own[:, 2 * PAIR :], oth[:, 2 * PAIR :]], 0))
    q_lane = lax.broadcasted_iota(jnp.int32, (query_rows, PAIR), 1)
    steps = [
        (side, block, head)
        for side in range(2)
        for block in range(half // query_rows)
        for head in range(2)
    ]

    def scores_of(step):
        side, block, head = step
        query = sides[side][0][block * query_rows : (block + 1) * query_rows, :PAIR]
        mine = (q_lane < HEAD_DIM) == (head == 0)
        spare = q_lane == (HEAD_DIM if head == 0 else 0)
        query = jnp.where(
            mine, query, jnp.where(spare, jnp.ones_like(query), jnp.zeros_like(query))
        )
        return dot_nt(keys[head], query)

    current = scores_of(steps[0])
    outs = [None, None]
    for index, (side, block, head) in enumerate(steps):
        following = scores_of(steps[index + 1]) if index + 1 < len(steps) else None
        top = jnp.max(current, axis=0, keepdims=True) * LOG_SCALE
        exponent = jnp.exp2(current * LOG_SCALE - top)
        total = jnp.sum(exponent, axis=0, keepdims=True)
        head_values = values_t[head * HEAD_DIM : (head + 1) * HEAD_DIM, :]
        outs[head] = dot(head_values, exponent.astype(bf16)) * (1.0 / total)
        first = side * half + block * query_rows
        log_ref[head : head + 1, first : first + query_rows] = top + jnp.log2(total)
        if head == 1:
            sides[side][1][block * query_rows : (block + 1) * query_rows, :] = jnp.transpose(
                jnp.concatenate(outs, 0)
            ).astype(bf16)
        current = following


def attend(info, own, oth, seq):
    half, width = oth.shape
    pairs = width // (3 * PAIR)
    query_rows = min(512, half)
    out = pl.BlockSpec((half, PAIR), lambda p: (0, p))
    shape = jax.ShapeDtypeStruct((half, width // 3), bf16)
    return pl.pallas_call(
        functools.partial(attend_kernel, query_rows),
        grid=(pairs,),
        in_specs=[
            pl.BlockSpec(memory_space=pltpu.SMEM),
            pl.BlockSpec((half, 3 * PAIR), lambda p: (seq, p)),
            pl.BlockSpec((half, 3 * PAIR), lambda p: (0, p)),
        ],
        out_specs=[out, out, pl.BlockSpec((8, 2 * half), lambda p: (p, 0))],
        out_shape=[shape, shape, jax.ShapeDtypeStruct((8 * pairs, 2 * half), f32)],
        compiler_params=pltpu.CompilerParams(vmem_limit_bytes=40 * 2**20),
        cost_estimate=SMALL_COST,
        name="attend",
    )(info, own, oth)


WINDOW = 256


def window_rows(count_low, count_high):
    start = (count_low // 16) * 16
    windows = jnp.where(count_high > count_low, (count_high - start + WINDOW - 1) // WINDOW, 0)
    return start, windows


def dispatch_rows(bounds, slots, sources, total, expert):
    total[...] = jnp.zeros_like(total)
    for seg, source in enumerate(sources):
        start, windows = window_rows(bounds[seg, expert], bounds[4 + seg, expert])
        taken = slots[seg : seg + 1, :] - expert * CAP

        @pl.loop(0, windows)
        def _(step, start=start, taken=taken, source=source):
            begin = start + step * WINDOW
            row = pl.multiple_of(jnp.minimum(begin, CAP - WINDOW), 16)
            offset = jnp.where(taken >= begin, taken - row, -1)
            slot = lax.broadcasted_iota(jnp.int32, (WINDOW, offset.shape[1]), 0)
            place = jnp.where(slot == offset, 1.0, 0.0).astype(bf16)
            total[pl.ds(row, WINDOW), :] += dot(place, source[...])


def expert_forward_kernel(
    block, chunk, bounds, slots, seg0, seg1, seg2, seg3, w_in, w_out, w_route, chosen,
    x_out, hidden_out, slope_out, result_out, probs_out, gate_out, total,
):
    expert = pl.program_id(0)
    half = seg0.shape[0]

    @pl.when(expert == 0)
    def _():
        row = lax.broadcasted_iota(jnp.int32, (8, half), 0)
        for index, seg in enumerate((seg0, seg1, seg2, seg3)):
            part = slice(index * half, (index + 1) * half)
            logits = jnp.where(row < EXPERTS, dot_nt(w_route[...], seg[...]), -1e30)
            exponent = jnp.exp(logits - jnp.max(logits, axis=0, keepdims=True))
            probs = exponent / jnp.sum(exponent, axis=0, keepdims=True)
            probs = jnp.where(row < EXPERTS, probs, 0.0)
            probs_out[:, part] = probs
            gate = jnp.sum(probs * chosen[:, part], axis=0, keepdims=True)
            gate = jnp.where(chosen[EXPERTS : EXPERTS + 1, part] > 0, gate, 0.0)
            gate_out[part, :] = as_column(gate)

    dispatch_rows(bounds, slots, (seg0, seg1, seg2, seg3), total, expert)
    x_out[0] = total[...].astype(bf16)
    blocks = (bounds[8, expert] + block - 1) // block
    hidden_units = w_in.shape[2]
    columns = [slice(c, c + chunk) for c in range(0, hidden_units, chunk)]

    @pl.loop(0, blocks)
    def _(step):
        rows = pl.ds(pl.multiple_of(step * block, block), block)
        x = x_out[0, rows, :]
        pre = dot(x, w_in[0, :, columns[0]])
        result = None
        for index, cols in enumerate(columns):
            following = None
            if index + 1 < len(columns):
                following = dot(x, w_in[0, :, columns[index + 1]])
            square = pre * pre
            bend = jnp.tanh(pre * (GELU_C + GELU_C * GELU_A * square))
            half_up = 0.5 + 0.5 * bend
            hidden = (pre * half_up).astype(bf16)
            slope = half_up + pre * (0.5 * GELU_C + 1.5 * GELU_C * GELU_A * square) * (
                1.0 - bend * bend
            )
            hidden_out[0, rows, cols] = hidden
            slope_out[0, rows, cols] = slope.astype(bf16)
            part = dot(hidden, w_out[0, cols, :])
            result = part if result is None else result + part
            pre = following
        result_out[0, rows, :] = result.astype(bf16)

    @pl.loop(blocks, CAP // block)
    def _(step):
        rows = pl.ds(pl.multiple_of(step * block, block), block)
        hidden_out[0, rows, :] = jnp.zeros((block, hidden_units), bf16)
        slope_out[0, rows, :] = jnp.zeros((block, hidden_units), bf16)
        result_out[0, rows, :] = jnp.zeros((block, result_out.shape[2]), bf16)


def expert_backward_kernel(
    block, chunk, bounds, slots, cot_own, cot_oth, w_in, w_out, gate, hidden, slope,
    up_out, pre_out, back_out, total, gated,
):
    expert = pl.program_id(0)
    seqs, half = cot_own.shape[:2]
    parts = [pl.ds(index * half, half) for index in range(2 * seqs)]

    @pl.when(expert == 0)
    def _():
        for index, part in enumerate(parts):
            cot = (cot_own if index < seqs else cot_oth)[index % seqs].astype(f32)
            gated[part, :] = (gate[part, :] * cot).astype(bf16)

    dispatch_rows(bounds, slots, [gated.at[part] for part in parts], total, expert)
    up_out[0] = total[...].astype(bf16)
    blocks = (bounds[8, expert] + block - 1) // block
    width, hidden_units = w_in.shape[1], w_in.shape[2]
    columns = [slice(c, c + chunk) for c in range(0, hidden_units, chunk)]
    lane = lax.broadcasted_iota(jnp.int32, (block, PAIR), 1)

    @pl.loop(0, blocks)
    def _(step):
        rows = pl.ds(pl.multiple_of(step * block, block), block)
        up = up_out[0, rows, :]
        grad = dot_nt(up, w_out[0, columns[0], :])
        back, gate_grad = None, None
        for index, cols in enumerate(columns):
            following = None
            if index + 1 < len(columns):
                following = dot_nt(up, w_out[0, columns[index + 1], :])
            pre_grad = (grad * slope[0, rows, cols].astype(f32)).astype(bf16)
            pre_out[0, rows, cols] = pre_grad
            share = jnp.sum(grad * hidden[0, rows, cols].astype(f32), axis=1, keepdims=True)
            part = dot_nt(pre_grad, w_in[0, :, cols])
            back = part if back is None else back + part
            gate_grad = share if gate_grad is None else gate_grad + share
            grad = following
        back_out[0, rows, :width] = back.astype(bf16)
        high = gate_grad.astype(bf16).astype(f32)
        extra = jnp.where(lane == 0, high, jnp.where(lane == 1, gate_grad - high, 0.0))
        back_out[0, rows, width:] = extra.astype(bf16)

    @pl.loop(blocks, CAP // block)
    def _(step):
        rows = pl.ds(pl.multiple_of(step * block, block), block)
        pre_out[0, rows, :] = jnp.zeros((block, hidden_units), bf16)
        back_out[0, rows, :] = jnp.zeros((block, width + PAIR), bf16)


def slot_spec(columns):
    return pl.BlockSpec((1, CAP, columns), lambda e: (e, 0, 0))


def slot_shape(columns):
    return shaped((EXPERTS, CAP, columns), bf16)


def weight_spec(weights):
    return pl.BlockSpec((1,) + weights.shape[1:], lambda e: (e, 0, 0))


def expert_forward(bounds, slots, segments, w_in, w_out, w_route, chosen):
    _, width, hidden_units = w_in.shape
    half = segments[0].shape[0]
    return kernel_call(
        functools.partial(expert_forward_kernel, FORWARD_BLOCK, 512),
        (EXPERTS,),
        [SMEM_SPEC, whole_spec((4, half))]
        + [whole_spec((half, width))] * 4
        + [weight_spec(w_in), weight_spec(w_out), whole_spec((8, width)), whole_spec((8, 4 * half))],
        [
            slot_spec(width),
            slot_spec(hidden_units),
            slot_spec(hidden_units),
            slot_spec(width),
            whole_spec((8, 4 * half)),
            whole_spec((4 * half, 1)),
        ],
        [
            slot_shape(width),
            slot_shape(hidden_units),
            slot_shape(hidden_units),
            slot_shape(width),
            shaped((8, 4 * half), f32),
            shaped((4 * half, 1), f32),
        ],
        [pltpu.VMEM((CAP, width), f32)],
        "expert_forward",
    )(bounds, slots, *segments, w_in, w_out, w_route, chosen)


def expert_backward(bounds, slots, cot_own, cot_oth, w_in, w_out, gate, hidden, slope):
    _, width, hidden_units = w_in.shape
    half = slots.shape[1]
    return kernel_call(
        functools.partial(expert_backward_kernel, BACKWARD_BLOCK, 512),
        (EXPERTS,),
        [SMEM_SPEC, whole_spec((4, half)), whole_spec(cot_own.shape), whole_spec(cot_oth.shape)]
        + [weight_spec(w_in), weight_spec(w_out), whole_spec((4 * half, 1))]
        + [slot_spec(hidden_units), slot_spec(hidden_units)],
        [slot_spec(width), slot_spec(hidden_units), slot_spec(width + PAIR)],
        [slot_shape(width), slot_shape(hidden_units), slot_shape(width + PAIR)],
        [pltpu.VMEM((CAP, width), f32), pltpu.VMEM((4 * half, width), bf16)],
        "expert_backward",
    )(bounds, slots, cot_own, cot_oth, w_in, w_out, gate, hidden, slope)


def expert_grad_kernel(chunk, split, bounds, parity, left, right, mine, *refs):
    send, left_t = refs[0], refs[-1]
    expert = pl.program_id(0)
    left_t[...] = jnp.transpose(left[0])
    taken, odd = bounds[8, expert], parity[0]
    sizes = [rows for rows in (256, 512) if rows < CAP] + [CAP]
    below = -1
    for rows in sizes:

        @pl.when(jnp.logical_and(taken > below, taken <= rows))
        def _(rows=rows):
            for c in range(0, right.shape[2], chunk):
                product = dot(left_t[:, :rows], right[0, :rows, c : c + chunk]).astype(bf16)
                if not split:
                    mine[0, :, c : c + chunk] = product
                    continue
                block = mine.shape[2]
                for pair in range(mine.shape[1]):
                    even = product[2 * pair * block : (2 * pair + 1) * block]
                    other = product[(2 * pair + 1) * block : (2 * pair + 2) * block]
                    mine[0, pair, :, c : c + chunk] = jnp.where(odd == 0, even, other)
                    send[0, pair, :, c : c + chunk] = jnp.where(odd == 0, other, even)

        below = rows


def expert_grad(bounds, parity, left, right, blocks, name):
    width, hidden_units = left.shape[2], right.shape[2]
    block = width // blocks
    split = blocks > 1 and block % 16 == 0
    shape = (EXPERTS, blocks // 2, block, hidden_units) if split else (EXPERTS, width, hidden_units)
    spec = pl.BlockSpec((1,) + shape[1:], lambda e: (e,) + (0,) * (len(shape) - 1))
    mine, *send = kernel_call(
        functools.partial(expert_grad_kernel, 512, split),
        (EXPERTS,),
        [SMEM_SPEC, SMEM_SPEC, slot_spec(width), slot_spec(hidden_units)],
        [spec] * (2 if split else 1),
        [shaped(shape, bf16)] * (2 if split else 1),
        [pltpu.VMEM((width, CAP), bf16)],
        name,
    )(bounds, parity, left, right)
    if blocks == 1:
        return mine
    if split:
        return mine, send[0]
    return split_even_odd(mine.reshape(EXPERTS, blocks, block, hidden_units), parity[0])


def collect_kernel(first_seg, segs, bounds, slots, rows_in, *refs):
    outs, total = refs[:-1], refs[-1]
    expert = pl.program_id(0)
    half = slots.shape[0] // segs

    @pl.when(expert == 0)
    def _():
        total[...] = jnp.zeros_like(total)

    for index in range(segs):
        seg = first_seg + index
        start, windows = window_rows(bounds[seg, expert], bounds[4 + seg, expert])
        part = slice(index * half, (index + 1) * half)
        taken = slots[part, :] - expert * CAP

        @pl.loop(0, windows)
        def _(step, start=start, part=part, taken=taken):
            begin = start + step * WINDOW
            row = pl.multiple_of(jnp.minimum(begin, CAP - WINDOW), 16)
            offset = jnp.where(taken >= begin, taken - row, -1)
            slot = lax.broadcasted_iota(jnp.int32, (half, WINDOW), 1)
            place = jnp.where(slot == offset, 1.0, 0.0).astype(bf16)
            total[part, :] += dot(place, rows_in[0, pl.ds(row, WINDOW), :])

    @pl.when(expert == EXPERTS - 1)
    def _():
        width = outs[0].shape[1]
        for index in range(segs):
            part = slice(index * half, (index + 1) * half)
            outs[0][part, :] = total[part, :width].astype(outs[0].dtype)
            if rows_in.shape[2] == width:
                continue
            extra = jnp.transpose(total[part, width:])[:8, :]
            if len(outs) > 1:
                outs[1][:, part] = extra
            else:
                first = segs * half + 8 * index
                outs[0][first : first + 8, :half] = extra.astype(outs[0].dtype)
                outs[0][first : first + 8, half:] = jnp.zeros((8, width - half), outs[0].dtype)


def collect(bounds, slots_column, rows_in, first_seg, segs, width, dtype, name, tail=False):
    columns = rows_in.shape[2]
    half = slots_column.shape[0] // 4
    rows = segs * (half + 8) if tail else segs * half
    out_specs = [pl.BlockSpec((rows, width), lambda e: (0, 0))]
    out_shape = [jax.ShapeDtypeStruct((rows, width), dtype)]
    if columns > width and not tail:
        out_specs.append(pl.BlockSpec((8, segs * half), lambda e: (0, 0)))
        out_shape.append(jax.ShapeDtypeStruct((8, segs * half), f32))
    return pl.pallas_call(
        functools.partial(collect_kernel, first_seg, segs),
        grid=(EXPERTS,),
        in_specs=[
            pl.BlockSpec(memory_space=pltpu.SMEM),
            pl.BlockSpec((segs * half, 1), lambda e: (first_seg // segs, 0)),
            slot_spec(columns),
        ],
        out_specs=out_specs,
        out_shape=out_shape,
        scratch_shapes=[pltpu.VMEM((segs * half, columns), f32)],
        compiler_params=pltpu.CompilerParams(vmem_limit_bytes=58 * 2**20),
        cost_estimate=SMALL_COST,
        name=name,
    )(bounds, slots_column, rows_in)


def logit_grads(chosen, probs, gate_own, gate_recv):
    gate_grad = gate_own[:1, :] + gate_own[1:2, :] + gate_recv[:1, :] + gate_recv[1:2, :]
    expert = lax.broadcasted_iota(jnp.int32, chosen.shape, 0)
    return jnp.where(expert < EXPERTS, chosen - probs, 0.0) * gate_grad


def residual_grad_kernel(
    steps, info, back_own, back_recv, probs, chosen, gate_own, gate_tail, w_route, res0, res1, cot,
    gain, w_own, w_oth, grad_out, low_out, up_own, up_send,
):
    step = pl.program_id(0)
    block = cot.shape[0]
    logit_grad = logit_grads(
        chosen[...], probs[...], gate_own[...], gate_tail[:8, :].astype(f32)
    )
    two_grad = back_own[...] + back_recv[...].astype(f32)
    for _ in range(3):
        part = logit_grad.astype(bf16)
        two_grad += dot_tn(part, w_route[...])
        logit_grad = logit_grad - part.astype(f32)
    rows = jnp.where(step < steps, res0[...], res1[...])
    slot = lax.broadcasted_iota(jnp.int32, (block, 1), 0) + step % steps * block
    valid = slot + info[2] * (block * steps) < info[step // steps]
    upstream = jnp.where(valid, cot[...].astype(f32), 0.0)
    grad = upstream + norm_back(rows, inverse_rms(rows), gain[...], two_grad)
    grad_out[...] = grad
    low = grad.astype(bf16)
    low_out[...] = low
    up_send[...] = dot_nt(low, w_oth[...]).astype(bf16)
    up_own[...] = dot_nt(low, w_own[...]).astype(bf16)


def residual_grad_of(
    info, back_own, back_recv, probs, chosen, gate_own, w_route, residual, cot, gain, w_own, w_oth,
):
    half, width = residual[0].shape
    inner = w_own.shape[0]
    block = min(256, half)
    steps = half // block
    tile = pl.BlockSpec((block, width), lambda i: (i, 0))
    first = pl.BlockSpec((block, width), lambda i: (jnp.minimum(i, steps - 1), 0))
    second = pl.BlockSpec((block, width), lambda i: (jnp.maximum(i - steps, 0), 0))
    columns = pl.BlockSpec((8, block), lambda i: (0, i))
    gate_tail = pl.BlockSpec((8, block), lambda i: (2 * half // 8 + i // steps, i % steps))
    ctx = pl.BlockSpec((block, inner), lambda i: (i, 0))
    weight = whole_spec((inner, width))
    return kernel_call(
        functools.partial(residual_grad_kernel, steps),
        (2 * steps,),
        [SMEM_SPEC, tile, tile, columns, columns, columns, gate_tail]
        + [whole_spec((8, width)), first, second, tile, whole_spec((1, width)), weight, weight],
        [tile, tile, ctx, ctx],
        [shaped((2 * half, width), f32), shaped((2 * half, width), bf16)]
        + [shaped((2 * half, inner), bf16)] * 2,
        [],
        "residual_grad",
    )(
        info, back_own, back_recv, probs, chosen, gate_own, back_recv, w_route, *residual, cot, gain,
        w_own, w_oth,
    )


def attn_grad_kernel(
    low, own0, own1, recv0, recv1, seg0, seg1, probs, chosen, gate_own, gate_tail,
    own_out, send_out, router_out,
):
    half = seg0.shape[0]
    low_t = [jnp.transpose(low[:half, :]), jnp.transpose(low[half:, :])]
    own_out[...] = dot(low_t[0], own0[...]) + dot(low_t[1], own1[...])
    send = (dot(low_t[0], recv0[...]) + dot(low_t[1], recv1[...])).astype(bf16)
    inner = send_out.shape[0]
    for index in range(send_out.shape[1] // inner):
        part = slice(index * inner, (index + 1) * inner)
        send_out[:, part] = send[part, :]
    total = None
    for index, seg in enumerate((seg0, seg1)):
        part = slice(index * half, (index + 1) * half)
        tail = gate_tail[8 * index : 8 * index + 8, :half].astype(f32)
        logit_grad = logit_grads(chosen[:, part], probs[:, part], gate_own[:, part], tail)
        for _ in range(3):
            piece = logit_grad.astype(bf16)
            product = dot(piece, seg[...])
            total = product if total is None else total + product
            logit_grad = logit_grad - piece.astype(f32)
    router_out[...] = total


def attn_grad(low, ctx_own, ctx_recv, segments, probs, chosen, gate_own, back_recv):
    half, inner = ctx_own[0].shape
    width = low.shape[1]
    columns = whole_spec((8, 2 * half))
    gate_tail = pl.BlockSpec((16, width), lambda i: (2 * half // 16, 0))
    return kernel_call(
        attn_grad_kernel,
        (1,),
        [whole_spec((2 * half, width))]
        + [whole_spec((half, inner))] * 4
        + [whole_spec((half, width))] * 2
        + [columns] * 3
        + [gate_tail],
        [whole_spec((width, inner)), whole_spec((inner, width)), whole_spec((8, width))],
        [shaped((width, inner), f32), shaped((inner, width), bf16), shaped((8, width), f32)],
        [],
        "attn_grad",
    )(low, *ctx_own, *ctx_recv, *segments, probs, chosen, gate_own, back_recv)


def attend_back_kernel(
    query_rows, last, split, info, parity, own, oth, ctx_own, ctx_oth, up_own, up_oth, log_ref,
    normed_own, normed_oth, weights, *refs,
):
    if last:
        before, one_own, one_oth, mine, send, key_sum, value_sum, grads, normed_t, one_sum = refs
    else:
        extra, one_own, one_oth, mine, key_sum, value_sum, grads, normed_t, one_sum = refs
    half = own.shape[0]
    row = lax.broadcasted_iota(jnp.int32, (half, PAIR), 0)
    zeros = jnp.zeros((half, PAIR), bf16)
    seen = (row + info[1] < info[0], row + info[2] < info[0])
    sides = ((own, ctx_own, up_own), (oth, ctx_oth, up_oth))

    def all_keys(part):
        first, last = part * PAIR, (part + 1) * PAIR
        return jnp.concatenate(
            [
                jnp.where(seen[0], own[:, first:last], zeros),
                jnp.where(seen[1], oth[:, first:last], zeros),
            ],
            0,
        )

    keys, values = all_keys(1), all_keys(2)
    keys_t = jnp.transpose(keys)
    lane = lax.broadcasted_iota(jnp.int32, (query_rows, PAIR), 1)
    sum_lane = lax.broadcasted_iota(jnp.int32, (8, PAIR), 1)
    sum_row = lax.broadcasted_iota(jnp.int32, (8, PAIR), 0)
    head_sum = jnp.where((sum_lane < HEAD_DIM) == (sum_row == 0), 1.0, 0.0).astype(bf16)
    for side, (src, ctx, up) in enumerate(sides):
        for block in range(half // query_rows):
            rows = slice(block * query_rows, (block + 1) * query_rows)
            first = side * half + block * query_rows
            query, grad = src[rows, :PAIR], up[rows, :]
            product = grad.astype(f32) * ctx[rows, :].astype(f32)
            coarse = product.astype(bf16)
            fine = (product - coarse.astype(f32)).astype(bf16)
            delta = dot_nt(head_sum, coarse) + dot_nt(head_sum, fine)
            query_grads, key_grads, value_grads = [], [], []
            for head in range(2):
                of_head = (lane < HEAD_DIM) == (head == 0)
                query_h = jnp.where(of_head, query, jnp.zeros_like(query))
                grad_h = jnp.where(of_head, grad, jnp.zeros_like(grad))
                log_row = log_ref[head : head + 1, first : first + query_rows]
                scores = dot_nt(keys, query_h)
                probs = jnp.exp2(jnp.minimum(scores * LOG_SCALE - log_row, 0.0))
                prob_grad = dot_nt(values, grad_h)
                score_grad = (probs * (prob_grad - delta[head : head + 1, :])).astype(bf16)
                value_grads.append(dot(probs.astype(bf16), grad_h))
                key_grads.append(dot(score_grad, query_h))
                query_grads.append(
                    dot(keys_t[head * HEAD_DIM : (head + 1) * HEAD_DIM, :], score_grad)
                )
            value_grad = value_grads[0] + value_grads[1]
            key_grad = key_grads[0] + key_grads[1]
            if side == 0 and block == 0:
                value_sum[...] = value_grad
                key_sum[...] = key_grad
            else:
                value_sum[...] += value_grad
                key_sum[...] += key_grad
            query_grad = jnp.transpose(jnp.concatenate(query_grads, 0)) * HEAD_DIM ** (-0.5)
            grads[first : first + query_rows, :PAIR] = query_grad.astype(bf16)
    for side in range(2):
        part = slice(side * half, (side + 1) * half)
        key_grad = jnp.where(seen[side], key_sum[part, :] * HEAD_DIM ** (-0.5), 0.0)
        grads[part, PAIR : 2 * PAIR] = key_grad.astype(bf16)
        grads[part, 2 * PAIR :] = jnp.where(seen[side], value_sum[part, :], 0.0).astype(bf16)

    pair = pl.program_id(0)

    @pl.when(pair == 0)
    def _():
        normed_t[:, :half] = jnp.transpose(normed_own[...])
        normed_t[:, half:] = jnp.transpose(normed_oth[...])
        one_sum[...] = jnp.zeros_like(one_sum)

    one_sum[...] += dot_nt(grads[...], weights[...])

    @pl.when(pair == pl.num_programs(0) - 1)
    def _():
        one_own[...] = one_sum[:half, :]
        one_oth[:half, :] = one_sum[half:, :].astype(bf16)
        if not last:
            one_oth[half:, :] = extra[...]

    product = dot(normed_t[...], grads[...])
    if not last:
        mine[...] = product
        return
    product = (product + before[...]).astype(bf16)
    if not split:
        mine[...] = product
        return
    block = mine.shape[1]
    odd = parity[0]
    for index in range(mine.shape[0]):
        even = product[2 * index * block : (2 * index + 1) * block]
        other = product[(2 * index + 1) * block : (2 * index + 2) * block]
        mine[index] = jnp.where(odd == 0, even, other)
        send[index] = jnp.where(odd == 0, other, even)


def attend_back(
    info, parity, own, oth, seq, ctx_own, ctx_oth, up_own, up_oth, logs, normed_own, normed_oth,
    weights, blocks, before, last,
):
    half, columns = oth.shape
    width = weights.shape[0]
    pairs = columns // (3 * PAIR)
    query_rows = min(256, half)
    block = width // blocks
    split = block % 16 == 0
    one = pl.BlockSpec((half, PAIR), lambda p: (0, p))
    three = pl.BlockSpec((half, 3 * PAIR), lambda p: (0, p))
    weight = pl.BlockSpec((width, 3 * PAIR), lambda p: (0, p))
    sent = half if last else half + before.shape[0]
    out_specs = [whole_spec((half, width)), whole_spec((sent, width))]
    out_shape = [shaped((half, width), f32), shaped((sent, width), bf16)]
    if not last:
        out_specs.append(weight)
        out_shape.append(shaped((width, columns), f32))
    elif split:
        out_specs += [pl.BlockSpec((blocks // 2, block, 3 * PAIR), lambda p: (0, 0, p))] * 2
        out_shape += [shaped((blocks // 2, block, columns), bf16)] * 2
    else:
        out_specs += [weight, weight]
        out_shape += [shaped((width, columns), bf16)] * 2
    outs = kernel_call(
        functools.partial(attend_back_kernel, query_rows, last, split),
        (pairs,),
        [SMEM_SPEC, SMEM_SPEC, pl.BlockSpec((half, 3 * PAIR), lambda p: (seq, p)), three]
        + [one, one] + [pl.BlockSpec((half, PAIR), lambda p: (seq, p))] * 2
        + [pl.BlockSpec((8, 2 * half), lambda p: (p, 0))]
        + [pl.BlockSpec((half, width), lambda p: (seq, 0)), whole_spec((half, width)), weight]
        + [weight if last else whole_spec(before.shape)],
        out_specs,
        out_shape,
        [
            pltpu.VMEM((2 * half, PAIR), f32),
            pltpu.VMEM((2 * half, PAIR), f32),
            pltpu.VMEM((2 * half, 3 * PAIR), bf16),
            pltpu.VMEM((width, 2 * half), bf16),
            pltpu.VMEM((2 * half, width), f32),
        ],
        "attend_back",
        48,
    )(
        info, parity, own, oth, ctx_own, ctx_oth, up_own, up_oth, logs, normed_own, normed_oth,
        weights, before,
    )
    if last and not split:
        outs = list(outs[:2]) + list(split_even_odd(outs[2].reshape(blocks, block, columns), parity[0]))
    return outs


def finish_kernel(
    steps, info, rows, one_own0, one_own1, recv0, recv1, grad, res0, res1, result_own,
    result_recv, gate, gain, input_grad, activations,
):
    step = pl.program_id(0)
    block = rows.shape[0]
    for seq, refs in enumerate(((one_own0, recv0, res0), (one_own1, recv1, res1))):

        @pl.when(step // steps == seq)
        def _(seq=seq, refs=refs):
            one_own, recv, res = refs
            x = rows[...].astype(f32)
            one_grad = one_own[...] + recv[...].astype(f32)
            input_grad[...] = grad[...] + norm_back(x, inverse_rms(x), gain[...], one_grad)
            combined = result_own[...].astype(f32) + result_recv[...].astype(f32)
            mixed = res[...] + gate[...] * combined
            slot = lax.broadcasted_iota(jnp.int32, (block, 1), 0) + step % steps * block
            valid = slot + info[2] * (steps * block) < info[seq]
            activations[...] = jnp.where(valid, mixed, 0.0).astype(bf16)


def finish(info, rows, one_own, one_recv, grads, residual, result_own, result_recv, gate, gain):
    half, width = residual[0].shape
    block = min(256, half)
    steps = half // block
    tile = pl.BlockSpec((block, width), lambda i: (i, 0))
    first = pl.BlockSpec((block, width), lambda i: (jnp.minimum(i, steps - 1), 0))
    second = pl.BlockSpec((block, width), lambda i: (jnp.maximum(i - steps, 0), 0))
    return kernel_call(
        functools.partial(finish_kernel, steps),
        (2 * steps,),
        [SMEM_SPEC, tile]
        + [first, second] * 2
        + [tile, first, second]
        + [tile, tile, pl.BlockSpec((block, 1), lambda i: (i, 0)), whole_spec((1, width))],
        [tile, tile],
        [shaped((2 * half, width), f32), shaped((2 * half, width), bf16)],
        [],
        "finish",
    )(info, rows, *one_own, *one_recv, grads, *residual, result_own, result_recv, gate, gain)


def after(array, *earlier):
    return lax.optimization_barrier((array,) + earlier)[0]


def split_even_odd(array, odd):
    lead = array.shape[:-3]
    halves = array.reshape(lead + (array.shape[-3] // 2, 2) + array.shape[-2:])
    axis = len(lead) + 1
    return (
        lax.dynamic_index_in_dim(halves, odd, axis, keepdims=False),
        lax.dynamic_index_in_dim(halves, 1 - odd, axis, keepdims=False),
    )


class Halving:
    def __init__(self, parts, experts, block, bits, table, order):
        self.parts = [(array, total, first, list(bits)) for array, total, first in parts]
        self.experts, self.block, self.table = experts, block, table
        self.left, self.order, self.picked = list(bits), list(order), set()
        self.size = len(bits) + 1
        self.columns = parts[0][0].shape[-1]

    def total(self, row, dtype, transpose=False):
        size, picked = self.size, set(self.picked)
        group = 2 if self.experts % 2 == 0 else 1
        arrays, specs = [], []
        for array, total, first, bits in self.parts:
            arrays.append(array.reshape((total,) + (2,) * len(bits) + (self.block, self.columns)))
            shape = tuple(None if bit in picked else 2 for bit in bits)

            def place(step, table, first=first, bits=bits):
                picks = tuple(table[row * size + bit] if bit in picked else 0 for bit in bits)
                return (first // group + step,) + picks + (0, 0)

            specs.append(pl.BlockSpec((group,) + shape + (self.block, self.columns), place))
        tail = (self.columns, self.block) if transpose else (self.block, self.columns)
        out = (self.experts,) + (2,) * len(self.left) + tail

        def kernel(table, *refs):
            value = refs[0][...].astype(f32)
            for ref in refs[1:-1]:
                value += ref[...].astype(f32)
            if transpose:
                for index in range(group):
                    refs[-1][index] = jnp.transpose(value[index]).astype(dtype)
            else:
                refs[-1][...] = value.astype(dtype)

        return pl.pallas_call(
            kernel,
            grid_spec=pltpu.PrefetchScalarGridSpec(
                num_scalar_prefetch=1,
                grid=(self.experts // group,),
                in_specs=specs,
                out_specs=pl.BlockSpec(
                    (group,) + out[1:], lambda e, t: (e,) + (0,) * (len(out) - 1)
                ),
            ),
            out_shape=shaped(out, dtype),
            compiler_params=pltpu.CompilerParams(vmem_limit_bytes=58 * 2**20),
            cost_estimate=SMALL_COST,
            name="half_sum",
        )(self.table, *arrays)

    def send(self):
        bit = self.order[0]
        self.left.remove(bit)
        self.picked.add(bit)
        sent = self.total(bit, bf16)
        return sent.reshape(-1, self.columns)

    def step(self, sent):
        recv = exchange(sent, self.order.pop(0), 2**self.size)
        self.parts.append((recv, self.experts, 0, list(self.left)))

    def spread(self):
        bits = list(self.left)
        size, picked, count = self.size, set(self.picked), len(self.parts)
        masks = range(2 ** len(bits))
        group = 2 if self.experts % 2 == 0 else 1
        arrays, specs = [], []
        for array, total, first, dims in self.parts:
            arrays.append(array.reshape((total,) + (2,) * len(dims) + (self.block, self.columns)))
            shape = tuple(None if bit in picked else 2 for bit in dims)

            def place(step, table, first=first, dims=dims):
                picks = tuple(table[size * size + bit] if bit in picked else 0 for bit in dims)
                return (first // group + step,) + picks + (0, 0)

            specs.append(pl.BlockSpec((group,) + shape + (self.block, self.columns), place))
        out = (self.experts, self.block, self.columns)

        def kernel(table, *refs):
            for mask in masks:
                at = tuple(
                    table[size * size + bit] ^ ((mask >> (len(bits) - 1 - i)) & 1)
                    for i, bit in enumerate(bits)
                )
                at = (slice(None),) + at
                value = refs[0][at].astype(f32)
                for ref in refs[1:count]:
                    value += ref[at].astype(f32)
                refs[count + mask][...] = value.astype(bf16)

        own, *sent = pl.pallas_call(
            kernel,
            grid_spec=pltpu.PrefetchScalarGridSpec(
                num_scalar_prefetch=1,
                grid=(self.experts // group,),
                in_specs=specs,
                out_specs=[
                    pl.BlockSpec((group, self.block, self.columns), lambda e, t: (e, 0, 0))
                ] * len(masks),
            ),
            out_shape=[shaped(out, bf16)] * len(masks),
            compiler_params=pltpu.CompilerParams(vmem_limit_bytes=58 * 2**20),
            cost_estimate=SMALL_COST,
            name="spread_sum",
        )(self.table, *arrays)
        recv = []
        for mask, array in zip(masks[1:], sent):
            flip = sum(
                1 << bit for i, bit in enumerate(bits) if (mask >> (len(bits) - 1 - i)) & 1
            )
            pairs = [(i, i ^ flip) for i in range(2**size)]
            flat = lax.ppermute(array.reshape(-1, self.columns), "dp", pairs)
            recv.append(flat.reshape(out))
        return own, recv

    def last_recv(self, *earlier):
        array, *rest = self.parts[-1]
        if earlier:
            self.parts[-1] = (after(array, *earlier), *rest)
        return self.parts[-1][0]


def exchange(array, bit, size):
    return lax.ppermute(array, "dp", [(i, i ^ (1 << bit)) for i in range(size)])


def body(
    inputs,
    cotangent,
    lengths,
    routes,
    norm1_gain,
    w_query,
    w_key,
    w_value,
    w_attn_out,
    norm2_gain,
    w_router,
    w_expert_in,
    w_expert_out,
):
    seqs, half, width = inputs.shape
    slots = routes.shape[1]
    inner = w_query.shape[1]
    pairs = inner // PAIR
    side = lax.axis_index("tensor")
    dp_index = lax.axis_index("dp")
    dp_size = lax.axis_size("dp")
    own_tokens = seqs * half
    gain_one = norm1_gain.astype(f32)[None, :]
    gain_two = norm2_gain.astype(f32)[None, :]

    def swap(array):
        return lax.ppermute(array, "tensor", [(0, 1), (1, 0)])

    dp_rows = width // dp_size
    bits = dp_size.bit_length() - 1
    parity = (dp_index & 1).reshape(1).astype(jnp.int32)
    rows = inputs.reshape(own_tokens, width)
    cot_rows = cotangent.reshape(own_tokens, width)
    rows_oth = [swap(inputs[0])]
    info = jnp.concatenate([lengths, side[None]]).astype(jnp.int32)
    infos = [
        jnp.stack([lengths[s], side * half, (1 - side) * half]).astype(jnp.int32)
        for s in range(seqs)
    ]
    slots_rows, slots_column, chosen, bounds = plan(info, routes.reshape(seqs, slots))
    w_pairs = jnp.concatenate(
        [w[:, p * PAIR : (p + 1) * PAIR] for p in range(pairs) for w in (w_query, w_key, w_value)],
        1,
    )
    flips = (dp_index >> jnp.arange(bits)) & 1
    table = jnp.concatenate(
        [(flips[None, :] ^ jnp.eye(bits, dtype=flips.dtype)).reshape(-1), flips]
    ).astype(jnp.int32)
    w_route = jnp.pad(w_router.T, ((0, 8 - EXPERTS), (0, 0)))
    normed_own, proj_own = project(rows, gain_one, w_pairs, "project_own")
    first_in = after(rows_oth[0], proj_own, bounds, w_route, table)
    rows_oth[0] = first_in
    for s in range(1, seqs):
        rows_oth.append(swap(after(inputs, rows_oth[-1])[s]))
    normed_oth, proj_oth, ctx_own, ctx_oth, ctx_recv, logs = [], [], [], [], [], []
    for s in range(seqs):
        raw = rows_oth[s] if s == 0 else after(rows_oth[s], ctx_oth[s - 1])
        if s == 1:
            attn_out_oth = swap(after(w_attn_out, raw))
        normed_part, proj_part = project(raw, gain_one, w_pairs, "project_oth")
        normed_oth.append(normed_part)
        proj_oth.append(proj_part)
        own_part, oth_part, log_part = attend(infos[s], proj_own, proj_part, s)
        ctx_own.append(own_part)
        ctx_oth.append(oth_part)
        logs.append(log_part)
        ctx_recv.append(swap(oth_part))
    residual, normed_two, two_oth = [], [], []
    for s in range(seqs):
        ctx_recv[s] = after(ctx_recv[s], ctx_oth[-1] if s == 0 else normed_two[s - 1])
        res_part, normed_part = residual_of(
            rows, s, ctx_own[s], ctx_recv[s], w_attn_out, attn_out_oth, gain_two
        )
        residual.append(res_part)
        normed_two.append(normed_part)
        two_oth.append(swap(normed_part))

    segments = normed_two + two_oth
    cot_oth = swap(after(cotangent, *two_oth))
    x_rows, hidden, slope, result, probs, gate = expert_forward(
        bounds, slots_rows, segments, w_expert_in, w_expert_out, w_route, chosen
    )
    (result_oth,) = collect(
        bounds, slots_column, result, seqs, seqs, width, bf16, "collect_result_oth"
    )
    (result_own,) = collect(
        bounds, slots_column, after(result, result_oth), 0, seqs, width, bf16, "collect_result_own"
    )
    cot_oth = after(cot_oth, result_own)
    up_rows, pre_grad, back = expert_backward(
        bounds, slots_rows, cotangent, cot_oth, w_expert_in, w_expert_out, gate, hidden, slope
    )
    (back_oth,) = collect(
        bounds, slots_column, back, seqs, seqs, width, bf16, "collect_back_oth", True
    )
    back_recv = swap(back_oth)
    halved = list(range(bits - 1, 0, -1))
    order_x = list(range(1, bits))
    columns = w_expert_in.shape[2]
    grad_out_t = expert_grad(
        after(bounds, back_oth), parity, up_rows, hidden, 1, "grad_expert_out"
    )
    back_own, gate_own = collect(
        bounds, slots_column, after(back, grad_out_t), 0, seqs, width, f32, "collect_back_own"
    )
    in_mine, in_send = expert_grad(
        after(bounds, back_own), parity, x_rows, pre_grad, dp_size, "grad_expert_in"
    )
    recv = after(back_recv, in_mine)
    in_recv = exchange(after(in_send, recv).reshape(-1, columns), 0, dp_size)
    out_share_t = lax.psum_scatter(
        after(grad_out_t, recv), "dp", scatter_dimension=1, tiled=True
    )

    residual_grad, residual_low, up_own, up_send = residual_grad_of(
        info, back_own, recv, probs, chosen, gate_own, w_route, residual, cot_rows, gain_two,
        w_attn_out, attn_out_oth,
    )
    up_oth = swap(up_send)
    in_mine, in_recv = in_mine.reshape(-1, columns), after(in_recv, up_send)
    order_z = order_x[1:] + order_x[:1]
    in_sums = [
        Halving(
            [(in_mine, EXPERTS, first), (in_recv, EXPERTS, first)],
            EXPERTS // 2, dp_rows, halved, table, order,
        )
        for first, order in ((0, order_x), (EXPERTS // 2, order_z))
    ]
    in_sent = [part.send() for part in in_sums]
    for part, sent in zip(in_sums, in_sent):
        part.step(sent)
    grad_attn_t, grad_attn_send, grad_router = attn_grad(
        after(residual_low, *in_sent), ctx_own, ctx_recv, normed_two, probs, chosen, gate_own, recv
    )

    log_rows = after(logs[0], grad_attn_t)
    one_own0, one_oth0, grad_pairs = attend_back(
        infos[0], parity, proj_own, proj_oth[0], 0, ctx_own[0], ctx_oth[0], up_own, up_oth,
        log_rows, normed_own, normed_oth[0], w_pairs, dp_size, grad_attn_send, False,
    )
    one_recv = [swap(one_oth0)]
    result_recv = swap(after(result_oth, one_oth0))
    for part in in_sums:
        part.last_recv(one_oth0)
    in_sent = [part.send() for part in in_sums]
    log_rows = after(logs[1], *in_sent)
    one_own1, one_oth1, *grad_pairs = attend_back(
        infos[1], parity, proj_own, proj_oth[1], 1, ctx_own[1], ctx_oth[1], up_own, up_oth,
        log_rows, normed_own, normed_oth[1], w_pairs, dp_size, grad_pairs, True,
    )
    one_recv.append(swap(one_oth1))
    attn_recv = after(one_recv[0], one_oth1)[half:].astype(f32)
    grad_attn_t = grad_attn_t + jnp.concatenate(
        [attn_recv[:, i * inner : (i + 1) * inner] for i in range(width // inner)], 0
    )
    grad_router = after(grad_router, one_oth1)[:EXPERTS].T
    router_high = grad_router.astype(bf16)
    router_low = (grad_router - router_high.astype(f32)).astype(bf16)
    small = jnp.concatenate([router_high, router_low], 1)
    small = jnp.pad(small, ((0, 0), (0, PAIR - 2 * EXPERTS)))
    rest = jnp.concatenate([grad_attn_t.astype(bf16), small], 1).reshape(dp_size, dp_rows, -1)
    rest = split_even_odd(rest, parity[0])
    last_mine, last_send = [jnp.concatenate(pair, 2) for pair in zip(grad_pairs, rest)]
    last_columns = last_mine.shape[-1]
    for part, sent in zip(in_sums, in_sent):
        part.step(sent)
    last_send = after(
        last_send.reshape(-1, last_columns),
        *[part.last_recv() for part in in_sums],
    )
    last_recv = exchange(last_send, 0, dp_size)
    for part in in_sums:
        part.last_recv(last_send)
        while part.order:
            part.step(part.send())
    last_sum = Halving(
        [(last_mine.reshape(-1, last_columns), 1, 0), (last_recv, 1, 0)],
        1, dp_rows, halved, table, [bit for bit in order_x if bit < bits - 3],
    )
    while last_sum.order:
        last_sum.step(last_sum.send())
    last_own, last_recv = last_sum.spread()
    input_grad, activations = finish(
        info, rows, (one_own0, one_own1), (one_recv[0], after(one_recv[1], last_own)), residual_grad,
        residual, result_own, result_recv, gate, gain_one,
    )
    last_recv = [after(part, input_grad) for part in last_recv]
    last_share = sum(part.astype(f32) for part in [last_own] + last_recv)[0]
    in_share = jnp.concatenate([part.total(bits, f32) for part in in_sums], 0)
    out_share = jnp.swapaxes(out_share_t, 1, 2).astype(f32)

    own_rows = dp_rows // 2

    def share_rows(array, axis=0):
        return lax.dynamic_slice_in_dim(array, dp_index * dp_rows, dp_rows, axis)

    pair_share = last_share[:, : 3 * inner]
    shares = [
        jnp.concatenate(
            [pair_share[:, (3 * p + k) * PAIR : (3 * p + k + 1) * PAIR] for p in range(pairs)], 1
        )
        for k in range(3)
    ]
    attn_share = last_share[:, 3 * inner : 4 * inner].T
    router_share = (
        last_share[:, 4 * inner : 4 * inner + EXPERTS]
        + last_share[:, 4 * inner + EXPERTS : 4 * inner + 2 * EXPERTS]
    )
    sum_one = jnp.sum(pair_share * share_rows(w_pairs).astype(f32), axis=1)
    sum_two = jnp.sum(in_share * share_rows(w_expert_in, 1).astype(f32), axis=(0, 2))
    sums = jnp.concatenate([jnp.stack([sum_one, sum_two]), router_share.T], 0)
    sums = sums + swap(sums)
    router_share = sums[2:].T
    router_sum = jnp.sum(router_share * share_rows(w_router).astype(f32), axis=1)
    gain_grads = jnp.stack(
        [sums[0] / share_rows(gain_one[0]), (sums[1] + router_sum) / share_rows(gain_two[0])]
    )
    gain_grads = lax.dynamic_slice_in_dim(gain_grads, side * own_rows, own_rows, 1)
    router_out = lax.dynamic_slice_in_dim(router_share, side * own_rows, own_rows, 0)
    return (
        activations.reshape(inputs.shape),
        input_grad.reshape(inputs.shape),
        gain_grads[0],
        shares[0],
        shares[1],
        shares[2],
        attn_share,
        gain_grads[1],
        router_out,
        in_share,
        out_share,
    )


def solution(mesh):
    in_specs = (
        P("dp", "tensor", None),
        P("dp", "tensor", None),
        P("dp"),
        P("dp", None, None),
        P(),
        P(None, "tensor"),
        P(None, "tensor"),
        P(None, "tensor"),
        P("tensor", None),
        P(),
        P(),
        P(None, None, "tensor"),
        P(None, "tensor", None),
    )
    out_specs = (
        P("dp", "tensor", None),
        P("dp", "tensor", None),
        P(("dp", "tensor")),
        P("dp", "tensor"),
        P("dp", "tensor"),
        P("dp", "tensor"),
        P("tensor", "dp"),
        P(("dp", "tensor")),
        P(("dp", "tensor"), None),
        P(None, "dp", "tensor"),
        P(None, "tensor", "dp"),
    )
    return jax.shard_map(body, mesh=mesh, in_specs=in_specs, out_specs=out_specs, check_vma=False)
```

```python
import functools
import math

import jax
import jax.numpy as jnp
from jax import lax
from jax.experimental import pallas as pl
from jax.experimental.pallas import tpu as pltpu
from jax.sharding import PartitionSpec as P

HEAD_DIM = 64
EXPERTS = 4
CAP = 640
PAIR = 2 * HEAD_DIM
GELU_C = math.sqrt(2.0 / math.pi)
GELU_A = 0.044715
LOG_SCALE = math.log2(math.e) * HEAD_DIM ** (-0.5)

norm_eps = 1e-06
bf16 = jnp.bfloat16
f32 = jnp.float32
SMALL_COST = pl.CostEstimate(flops=1, bytes_accessed=1, transcendentals=0)


def dot(left, right):
    return lax.dot_general(left, right, (((1,), (0,)), ((), ())), preferred_element_type=f32)


def dot_nt(left, right):
    return lax.dot_general(left, right, (((1,), (1,)), ((), ())), preferred_element_type=f32)


def dot_tn(left, right):
    return lax.dot_general(left, right, (((0,), (0,)), ((), ())), preferred_element_type=f32)


def whole_spec(shape):
    return pl.BlockSpec(shape, lambda *_: (0,) * len(shape))


SMEM_SPEC = pl.BlockSpec(memory_space=pltpu.SMEM)


def kernel_call(kernel, grid, in_specs, out_specs, out_shape, scratch, name, limit=58):
    return pl.pallas_call(
        kernel,
        grid=grid,
        in_specs=in_specs,
        out_specs=out_specs,
        out_shape=out_shape,
        scratch_shapes=scratch,
        compiler_params=pltpu.CompilerParams(vmem_limit_bytes=limit * 2**20),
        cost_estimate=SMALL_COST,
        name=name,
    )


def shaped(shape, dtype):
    return jax.ShapeDtypeStruct(shape, dtype)


def inverse_rms(rows):
    return lax.rsqrt(jnp.mean(rows * rows, axis=-1, keepdims=True) + norm_eps)


def norm_back(rows, inverse, gain, upstream):
    weighted = upstream * gain
    inner_mean = jnp.mean(rows * weighted, axis=-1, keepdims=True)
    return inverse * weighted - rows * inverse**3 * inner_mean


def as_column(row):
    return jnp.transpose(jnp.broadcast_to(row, (PAIR, row.shape[1])))[:, :1]


def plan_kernel(info, routes, slots_rows, slots_column, chosen, bounds):
    half = slots_rows.shape[1]
    side = info[2]
    before_of = lax.broadcasted_iota(jnp.int32, (half, half), 0)
    upto = jnp.where(before_of <= lax.broadcasted_iota(jnp.int32, (half, half), 1), 1.0, 0.0)
    upto = upto.astype(bf16)
    expert = lax.broadcasted_iota(jnp.int32, (8, half), 0)
    capacity = (5 * (info[0] + info[1]) + 4 * EXPERTS - 1) // (4 * EXPERTS)
    column = jnp.zeros((8, 1), f32)
    row = jnp.zeros((8, 8), f32)
    limit = capacity.astype(f32)
    for seq in range(2):
        for part in range(2):
            local = seq + jnp.where(side == part, 0, 2)
            route = routes[seq : seq + 1, part * half : (part + 1) * half]
            slot = lax.broadcasted_iota(jnp.int32, (1, half), 1) + part * half
            valid = slot < info[seq]
            routed = expert == route
            hit = jnp.where(jnp.logical_and(routed, valid), 1.0, 0.0)
            counts = dot(hit.astype(bf16), upto) + column
            position = jnp.sum(hit * counts, axis=0, keepdims=True).astype(jnp.int32) - 1
            keep = jnp.logical_and(valid, position < capacity)
            taken = jnp.where(keep, route * CAP + position, EXPERTS * CAP)
            slots_rows[pl.ds(local, 1), :] = taken
            first = pl.multiple_of(local * half, half)
            slots_column[pl.ds(first, half), :] = as_column(taken.astype(f32)).astype(jnp.int32)
            picked = jnp.where(expert == EXPERTS, jnp.where(valid, 1.0, 0.0), 0.0)
            chosen[:, pl.ds(first, half)] = jnp.where(routed, 1.0, picked)
            bounds[pl.ds(local, 1), :] = jnp.minimum(row[:1], limit).astype(jnp.int32)
            column += jnp.sum(hit, axis=1, keepdims=True)
            row += dot_nt(jnp.ones((8, half), bf16), hit.astype(bf16))
            bounds[pl.ds(4 + local, 1), :] = jnp.minimum(row[:1], limit).astype(jnp.int32)
    bounds[8:16, :] = jnp.minimum(row, limit).astype(jnp.int32)


def plan(info, routes):
    seqs, slots = routes.shape
    half = slots // 2
    return kernel_call(
        plan_kernel,
        (1,),
        [SMEM_SPEC, whole_spec((seqs, slots))],
        [
            whole_spec((4, half)),
            whole_spec((4 * half, 1)),
            whole_spec((8, 4 * half)),
            whole_spec((16, 8)),
        ],
        [
            shaped((4, half), jnp.int32),
            shaped((4 * half, 1), jnp.int32),
            shaped((8, 4 * half), f32),
            shaped((16, 8), jnp.int32),
        ],
        [],
        "plan",
        12,
    )(info, routes)


def project_kernel(rows, gain, weights, normed, proj):
    x = rows[...].astype(f32)
    low = (x * inverse_rms(x) * gain[...]).astype(bf16)
    normed[...] = low
    proj[...] = dot(low, weights[...]).astype(bf16)


def project(rows, gain, weights, name):
    count, width = rows.shape
    columns = weights.shape[1]
    block = min(256, count)
    tile = pl.BlockSpec((block, width), lambda i: (i, 0))
    return kernel_call(
        project_kernel,
        (count // block,),
        [tile, whole_spec((1, width)), whole_spec((width, columns))],
        [tile, pl.BlockSpec((block, columns), lambda i: (i, 0))],
        [shaped((count, width), bf16), shaped((count, columns), bf16)],
        [],
        name,
        40,
    )(rows, gain, weights)


def residual_kernel(rows, ctx_own, ctx_recv, w_own, w_oth, gain, residual, normed):
    total = rows[...].astype(f32) + dot(ctx_own[...], w_own[...])
    total += dot(ctx_recv[...], w_oth[...])
    residual[...] = total
    normed[...] = (total * inverse_rms(total) * gain[...]).astype(bf16)


def residual_of(rows, seq, ctx_own, ctx_recv, w_own, w_oth, gain):
    half, inner = ctx_own.shape
    width = rows.shape[1]
    block = min(256, half)
    steps = half // block
    tile = pl.BlockSpec((block, width), lambda i: (i, 0))
    ctx = pl.BlockSpec((block, inner), lambda i: (i, 0))
    weight = whole_spec((inner, width))
    return kernel_call(
        residual_kernel,
        (steps,),
        [
            pl.BlockSpec((block, width), lambda i: (i + seq * steps, 0)),
            ctx, ctx, weight, weight, whole_spec((1, width)),
        ],
        [tile, tile],
        [shaped((half, width), f32), shaped((half, width), bf16)],
        [],
        "residual",
        40,
    )(rows, ctx_own, ctx_recv, w_own, w_oth, gain)


def attend_kernel(query_rows, info, own, oth, ctx_own, ctx_oth, log_ref):
    half = own.shape[0]
    row = lax.broadcasted_iota(jnp.int32, (half, PAIR), 0)
    lane = lax.broadcasted_iota(jnp.int32, (half, PAIR), 1)
    zeros = jnp.zeros((half, PAIR), bf16)
    hidden_key = jnp.full((half, PAIR), -1e30, bf16)
    sides = ((own, ctx_own, row + info[1] < info[0]), (oth, ctx_oth, row + info[2] < info[0]))
    keys = []
    for head in range(2):
        mine = (lane < HEAD_DIM) == (head == 0)
        spare = lane == (HEAD_DIM if head == 0 else 0)
        parts = []
        for ref, _, seen in sides:
            mask_value = jnp.where(seen, zeros, hidden_key)
            key = ref[:, PAIR : 2 * PAIR]
            parts.append(jnp.where(mine, key, jnp.where(spare, mask_value, zeros)))
        keys.append(jnp.concatenate(parts, 0))
    values_t = jnp.transpose(jnp.concatenate([own[:, 2 * PAIR :], oth[:, 2 * PAIR :]], 0))
    q_lane = lax.broadcasted_iota(jnp.int32, (query_rows, PAIR), 1)
    steps = [
        (side, block, head)
        for side in range(2)
        for block in range(half // query_rows)
        for head in range(2)
    ]

    def scores_of(step):
        side, block, head = step
        query = sides[side][0][block * query_rows : (block + 1) * query_rows, :PAIR]
        mine = (q_lane < HEAD_DIM) == (head == 0)
        spare = q_lane == (HEAD_DIM if head == 0 else 0)
        query = jnp.where(
            mine, query, jnp.where(spare, jnp.ones_like(query), jnp.zeros_like(query))
        )
        return dot_nt(keys[head], query)

    current = scores_of(steps[0])
    outs = [None, None]
    for index, (side, block, head) in enumerate(steps):
        following = scores_of(steps[index + 1]) if index + 1 < len(steps) else None
        top = jnp.max(current, axis=0, keepdims=True) * LOG_SCALE
        exponent = jnp.exp2(current * LOG_SCALE - top)
        total = jnp.sum(exponent, axis=0, keepdims=True)
        head_values = values_t[head * HEAD_DIM : (head + 1) * HEAD_DIM, :]
        outs[head] = dot(head_values, exponent.astype(bf16)) * (1.0 / total)
        first = side * half + block * query_rows
        log_ref[head : head + 1, first : first + query_rows] = top + jnp.log2(total)
        if head == 1:
            sides[side][1][block * query_rows : (block + 1) * query_rows, :] = jnp.transpose(
                jnp.concatenate(outs, 0)
            ).astype(bf16)
        current = following


def attend(info, own, oth, seq):
    half, width = oth.shape
    pairs = width // (3 * PAIR)
    query_rows = min(512, half)
    out = pl.BlockSpec((half, PAIR), lambda p: (0, p))
    shape = jax.ShapeDtypeStruct((half, width // 3), bf16)
    return pl.pallas_call(
        functools.partial(attend_kernel, query_rows),
        grid=(pairs,),
        in_specs=[
            pl.BlockSpec(memory_space=pltpu.SMEM),
            pl.BlockSpec((half, 3 * PAIR), lambda p: (seq, p)),
            pl.BlockSpec((half, 3 * PAIR), lambda p: (0, p)),
        ],
        out_specs=[out, out, pl.BlockSpec((8, 2 * half), lambda p: (p, 0))],
        out_shape=[shape, shape, jax.ShapeDtypeStruct((8 * pairs, 2 * half), f32)],
        compiler_params=pltpu.CompilerParams(vmem_limit_bytes=40 * 2**20),
        cost_estimate=SMALL_COST,
        name="attend",
    )(info, own, oth)


WINDOW = 256


def window_rows(count_low, count_high):
    start = (count_low // 16) * 16
    windows = jnp.where(count_high > count_low, (count_high - start + WINDOW - 1) // WINDOW, 0)
    return start, windows


def dispatch_rows(bounds, slots, sources, total, expert):
    total[...] = jnp.zeros_like(total)
    for seg, source in enumerate(sources):
        start, windows = window_rows(bounds[seg, expert], bounds[4 + seg, expert])
        taken = slots[seg : seg + 1, :] - expert * CAP

        @pl.loop(0, windows)
        def _(step, start=start, taken=taken, source=source):
            begin = start + step * WINDOW
            row = pl.multiple_of(jnp.minimum(begin, CAP - WINDOW), 16)
            offset = jnp.where(taken >= begin, taken - row, -1)
            slot = lax.broadcasted_iota(jnp.int32, (WINDOW, offset.shape[1]), 0)
            place = jnp.where(slot == offset, 1.0, 0.0).astype(bf16)
            total[pl.ds(row, WINDOW), :] += dot(place, source[...])


ROW_COUNTS = (256, 320, 384, 512, CAP)


def by_row_count(taken, work):
    below = -1
    for rows in ROW_COUNTS:
        pl.when(jnp.logical_and(taken > below, taken <= rows))(functools.partial(work, rows))
        below = rows


def expert_forward_kernel(
    chunk, bounds, slots, seg0, seg1, seg2, seg3, w_in, w_out, w_route, chosen,
    x_out, hidden_out, slope_out, result_out, probs_out, gate_out, total,
):
    expert = pl.program_id(0)
    half = seg0.shape[0]

    @pl.when(expert == 0)
    def _():
        row = lax.broadcasted_iota(jnp.int32, (8, half), 0)
        for index, seg in enumerate((seg0, seg1, seg2, seg3)):
            part = slice(index * half, (index + 1) * half)
            logits = jnp.where(row < EXPERTS, dot_nt(w_route[...], seg[...]), -1e30)
            exponent = jnp.exp(logits - jnp.max(logits, axis=0, keepdims=True))
            probs = exponent / jnp.sum(exponent, axis=0, keepdims=True)
            probs = jnp.where(row < EXPERTS, probs, 0.0)
            probs_out[:, part] = probs
            gate = jnp.sum(probs * chosen[:, part], axis=0, keepdims=True)
            gate = jnp.where(chosen[EXPERTS : EXPERTS + 1, part] > 0, gate, 0.0)
            gate_out[part, :] = as_column(gate)

    dispatch_rows(bounds, slots, (seg0, seg1, seg2, seg3), total, expert)
    x_out[0] = total[...].astype(bf16)
    block = CAP // 2
    blocks = (bounds[8, expert] + block - 1) // block
    hidden_units = w_in.shape[2]
    columns = [slice(c, c + chunk) for c in range(0, hidden_units, chunk)]

    @pl.loop(blocks, CAP // block)
    def _(step):
        rows = pl.ds(pl.multiple_of(step * block, block), block)
        for out in (hidden_out, slope_out, result_out):
            out[0, rows, :] = jnp.zeros((block, out.shape[2]), bf16)

    @pl.loop(0, blocks)
    def _(step):
        rows = pl.ds(pl.multiple_of(step * block, block), block)
        x = x_out[0, rows, :]
        pre = dot(x, w_in[0, :, columns[0]])
        result = None
        for index, cols in enumerate(columns):
            following = None
            if index + 1 < len(columns):
                following = dot(x, w_in[0, :, columns[index + 1]])
            square = pre * pre
            bend = jnp.tanh(pre * (GELU_C + GELU_C * GELU_A * square))
            half_up = 0.5 + 0.5 * bend
            hidden = (pre * half_up).astype(bf16)
            slope = half_up + pre * (0.5 * GELU_C + 1.5 * GELU_C * GELU_A * square) * (
                1.0 - bend * bend
            )
            hidden_out[0, rows, cols] = hidden
            slope_out[0, rows, cols] = slope.astype(bf16)
            part = dot(hidden, w_out[0, cols, :])
            result = part if result is None else result + part
            pre = following
        result_out[0, rows, :] = result.astype(bf16)


def expert_backward_kernel(
    chunk, bounds, slots, cot_own, cot_oth, w_in, w_out, gate, result, slope,
    up_out, pre_out, back_out, total, gated,
):
    expert = pl.program_id(0)
    seqs, half = cot_own.shape[:2]
    parts = [pl.ds(index * half, half) for index in range(2 * seqs)]

    @pl.when(expert == 0)
    def _():
        for index, part in enumerate(parts):
            cot = (cot_own if index < seqs else cot_oth)[index % seqs].astype(f32)
            gated[part, :] = (gate[part, :] * cot).astype(bf16)

    dispatch_rows(bounds, slots, [gated.at[part] for part in parts], total, expert)
    up_out[0] = total[...].astype(bf16)
    width, hidden_units = w_in.shape[1], w_in.shape[2]
    columns = [slice(c, c + chunk) for c in range(0, hidden_units, chunk)]

    def work(count):
        if count < CAP:
            for out in (pre_out, back_out):
                out[0, count:, :] = jnp.zeros((CAP - count, out.shape[2]), bf16)
        rows = slice(0, count)
        lane = lax.broadcasted_iota(jnp.int32, (count, PAIR), 1)
        up = up_out[0, rows, :]
        grad = dot_nt(up, w_out[0, columns[0], :])
        back = None
        gate_grad = jnp.sum(
            up.astype(f32) * result[0, rows, :].astype(f32), axis=1, keepdims=True
        )
        for index, cols in enumerate(columns):
            following = None
            if index + 1 < len(columns):
                following = dot_nt(up, w_out[0, columns[index + 1], :])
            pre_grad = (grad * slope[0, rows, cols].astype(f32)).astype(bf16)
            pre_out[0, rows, cols] = pre_grad
            part = dot_nt(pre_grad, w_in[0, :, cols])
            back = part if back is None else back + part
            grad = following
        back_out[0, rows, :width] = back.astype(bf16)
        high = gate_grad.astype(bf16).astype(f32)
        extra = jnp.where(lane == 0, high, jnp.where(lane == 1, gate_grad - high, 0.0))
        back_out[0, rows, width:] = extra.astype(bf16)

    by_row_count(bounds[8, expert], work)


def slot_spec(columns):
    return pl.BlockSpec((1, CAP, columns), lambda e: (e, 0, 0))


def slot_shape(columns):
    return shaped((EXPERTS, CAP, columns), bf16)


def weight_spec(weights):
    return pl.BlockSpec((1,) + weights.shape[1:], lambda e: (e, 0, 0))


def expert_forward(bounds, slots, segments, w_in, w_out, w_route, chosen):
    _, width, hidden_units = w_in.shape
    half = segments[0].shape[0]
    return kernel_call(
        functools.partial(expert_forward_kernel, 512),
        (EXPERTS,),
        [SMEM_SPEC, whole_spec((4, half))]
        + [whole_spec((half, width))] * 4
        + [weight_spec(w_in), weight_spec(w_out), whole_spec((8, width)), whole_spec((8, 4 * half))],
        [
            slot_spec(width),
            slot_spec(hidden_units),
            slot_spec(hidden_units),
            slot_spec(width),
            whole_spec((8, 4 * half)),
            whole_spec((4 * half, 1)),
        ],
        [
            slot_shape(width),
            slot_shape(hidden_units),
            slot_shape(hidden_units),
            slot_shape(width),
            shaped((8, 4 * half), f32),
            shaped((4 * half, 1), f32),
        ],
        [pltpu.VMEM((CAP, width), f32)],
        "expert_forward",
    )(bounds, slots, *segments, w_in, w_out, w_route, chosen)


def expert_backward(bounds, slots, cot_own, cot_oth, w_in, w_out, gate, result, slope):
    _, width, hidden_units = w_in.shape
    half = slots.shape[1]
    return kernel_call(
        functools.partial(expert_backward_kernel, 512),
        (EXPERTS,),
        [SMEM_SPEC, whole_spec((4, half)), whole_spec(cot_own.shape), whole_spec(cot_oth.shape)]
        + [weight_spec(w_in), weight_spec(w_out), whole_spec((4 * half, 1))]
        + [slot_spec(width), slot_spec(hidden_units)],
        [slot_spec(width), slot_spec(hidden_units), slot_spec(width + PAIR)],
        [slot_shape(width), slot_shape(hidden_units), slot_shape(width + PAIR)],
        [pltpu.VMEM((CAP, width), f32), pltpu.VMEM((4 * half, width), bf16)],
        "expert_backward",
    )(bounds, slots, cot_own, cot_oth, w_in, w_out, gate, result, slope)


def expert_grad_kernel(chunk, split, bounds, parity, left, right, mine, *refs):
    send, left_t = refs[0], refs[-1]
    expert = pl.program_id(0)
    left_t[...] = jnp.transpose(left[0])
    taken, odd = bounds[8, expert], parity[0]
    sizes = [rows for rows in (256, 512) if rows < CAP] + [CAP]
    below = -1
    for rows in sizes:

        @pl.when(jnp.logical_and(taken > below, taken <= rows))
        def _(rows=rows):
            for c in range(0, right.shape[2], chunk):
                product = dot(left_t[:, :rows], right[0, :rows, c : c + chunk]).astype(bf16)
                if not split:
                    mine[0, :, c : c + chunk] = product
                    continue
                block = mine.shape[2]
                for pair in range(mine.shape[1]):
                    even = product[2 * pair * block : (2 * pair + 1) * block]
                    other = product[(2 * pair + 1) * block : (2 * pair + 2) * block]
                    mine[0, pair, :, c : c + chunk] = jnp.where(odd == 0, even, other)
                    send[0, pair, :, c : c + chunk] = jnp.where(odd == 0, other, even)

        below = rows


def expert_grad(bounds, parity, left, right, blocks, name):
    width, hidden_units = left.shape[2], right.shape[2]
    block = width // blocks
    split = blocks > 1 and block % 16 == 0
    shape = (EXPERTS, blocks // 2, block, hidden_units) if split else (EXPERTS, width, hidden_units)
    spec = pl.BlockSpec((1,) + shape[1:], lambda e: (e,) + (0,) * (len(shape) - 1))
    mine, *send = kernel_call(
        functools.partial(expert_grad_kernel, 512, split),
        (EXPERTS,),
        [SMEM_SPEC, SMEM_SPEC, slot_spec(width), slot_spec(hidden_units)],
        [spec] * (2 if split else 1),
        [shaped(shape, bf16)] * (2 if split else 1),
        [pltpu.VMEM((width, CAP), bf16)],
        name,
    )(bounds, parity, left, right)
    if blocks == 1:
        return mine
    if split:
        return mine, send[0]
    return split_even_odd(mine.reshape(EXPERTS, blocks, block, hidden_units), parity[0])


def collect_kernel(first_seg, segs, bounds, slots, rows_in, *refs):
    outs, total = refs[:-1], refs[-1]
    expert = pl.program_id(0)
    half = slots.shape[0] // segs

    @pl.when(expert == 0)
    def _():
        total[...] = jnp.zeros_like(total)

    for index in range(segs):
        seg = first_seg + index
        start, windows = window_rows(bounds[seg, expert], bounds[4 + seg, expert])
        part = slice(index * half, (index + 1) * half)
        taken = slots[part, :] - expert * CAP

        @pl.loop(0, windows)
        def _(step, start=start, part=part, taken=taken):
            begin = start + step * WINDOW
            row = pl.multiple_of(jnp.minimum(begin, CAP - WINDOW), 16)
            offset = jnp.where(taken >= begin, taken - row, -1)
            slot = lax.broadcasted_iota(jnp.int32, (half, WINDOW), 1)
            place = jnp.where(slot == offset, 1.0, 0.0).astype(bf16)
            total[part, :] += dot(place, rows_in[0, pl.ds(row, WINDOW), :])

    @pl.when(expert == EXPERTS - 1)
    def _():
        width = outs[0].shape[1]
        for index in range(segs):
            part = slice(index * half, (index + 1) * half)
            outs[0][part, :] = total[part, :width].astype(outs[0].dtype)
            if rows_in.shape[2] == width:
                tail = outs[0].shape[0] - segs * half
                if tail:
                    outs[0][segs * half :, :] = jnp.zeros((tail, width), outs[0].dtype)
                continue
            extra = jnp.transpose(total[part, width:])[:8, :]
            if len(outs) > 1:
                outs[1][:, part] = extra
            else:
                first = segs * half + 8 * index
                outs[0][first : first + 8, :half] = extra.astype(outs[0].dtype)
                outs[0][first : first + 8, half:] = jnp.zeros((8, width - half), outs[0].dtype)


def collect(bounds, slots_column, rows_in, first_seg, segs, width, dtype, name, tail=0):
    columns = rows_in.shape[2]
    half = slots_column.shape[0] // 4
    rows = segs * (half + tail)
    out_specs = [pl.BlockSpec((rows, width), lambda e: (0, 0))]
    out_shape = [jax.ShapeDtypeStruct((rows, width), dtype)]
    if columns > width and not tail:
        out_specs.append(pl.BlockSpec((8, segs * half), lambda e: (0, 0)))
        out_shape.append(jax.ShapeDtypeStruct((8, segs * half), f32))
    return pl.pallas_call(
        functools.partial(collect_kernel, first_seg, segs),
        grid=(EXPERTS,),
        in_specs=[
            pl.BlockSpec(memory_space=pltpu.SMEM),
            pl.BlockSpec((segs * half, 1), lambda e: (first_seg // segs, 0)),
            slot_spec(columns),
        ],
        out_specs=out_specs,
        out_shape=out_shape,
        scratch_shapes=[pltpu.VMEM((segs * half, columns), f32)],
        compiler_params=pltpu.CompilerParams(vmem_limit_bytes=58 * 2**20),
        cost_estimate=SMALL_COST,
        name=name,
    )(bounds, slots_column, rows_in)


def logit_grads(chosen, probs, gate_own, gate_recv):
    gate_grad = gate_own[:1, :] + gate_own[1:2, :] + gate_recv[:1, :] + gate_recv[1:2, :]
    expert = lax.broadcasted_iota(jnp.int32, chosen.shape, 0)
    return jnp.where(expert < EXPERTS, chosen - probs, 0.0) * gate_grad


def residual_grad_kernel(
    steps, info, back_own, back_recv, probs, chosen, gate_own, gate_tail, w_route, res0, res1, cot,
    gain, w_own, w_oth, grad_out, low_out, up_own, up_send,
):
    step = pl.program_id(0)
    block = cot.shape[0]
    logit_grad = logit_grads(
        chosen[...], probs[...], gate_own[...], gate_tail[:8, :].astype(f32)
    )
    two_grad = back_own[...] + back_recv[...].astype(f32)
    for _ in range(3):
        part = logit_grad.astype(bf16)
        two_grad += dot_tn(part, w_route[...])
        logit_grad = logit_grad - part.astype(f32)
    rows = jnp.where(step < steps, res0[...], res1[...])
    slot = lax.broadcasted_iota(jnp.int32, (block, 1), 0) + step % steps * block
    valid = slot + info[2] * (block * steps) < info[step // steps]
    upstream = jnp.where(valid, cot[...].astype(f32), 0.0)
    grad = upstream + norm_back(rows, inverse_rms(rows), gain[...], two_grad)
    grad_out[...] = grad
    low = grad.astype(bf16)
    low_out[...] = low
    up_send[...] = dot_nt(low, w_oth[...]).astype(bf16)
    up_own[...] = dot_nt(low, w_own[...]).astype(bf16)


def residual_grad_of(
    info, back_own, back_recv, probs, chosen, gate_own, w_route, residual, cot, gain, w_own, w_oth,
):
    half, width = residual[0].shape
    inner = w_own.shape[0]
    block = min(256, half)
    steps = half // block
    tile = pl.BlockSpec((block, width), lambda i: (i, 0))
    first = pl.BlockSpec((block, width), lambda i: (jnp.minimum(i, steps - 1), 0))
    second = pl.BlockSpec((block, width), lambda i: (jnp.maximum(i - steps, 0), 0))
    columns = pl.BlockSpec((8, block), lambda i: (0, i))
    gate_tail = pl.BlockSpec((8, block), lambda i: (2 * half // 8 + i // steps, i % steps))
    ctx = pl.BlockSpec((block, inner), lambda i: (i, 0))
    weight = whole_spec((inner, width))
    return kernel_call(
        functools.partial(residual_grad_kernel, steps),
        (2 * steps,),
        [SMEM_SPEC, tile, tile, columns, columns, columns, gate_tail]
        + [whole_spec((8, width)), first, second, tile, whole_spec((1, width)), weight, weight],
        [tile, tile, ctx, ctx],
        [shaped((2 * half, width), f32), shaped((2 * half, width), bf16)]
        + [shaped((2 * half, inner), bf16)] * 2,
        [],
        "residual_grad",
    )(
        info, back_own, back_recv, probs, chosen, gate_own, back_recv, w_route, *residual, cot, gain,
        w_own, w_oth,
    )


def attn_grad_kernel(
    low, own0, own1, recv0, recv1, seg0, seg1, probs, chosen, gate_own, gate_tail,
    own_out, send_out, router_out,
):
    half = seg0.shape[0]
    low_t = [jnp.transpose(low[:half, :]), jnp.transpose(low[half:, :])]
    own_out[...] = dot(low_t[0], own0[...]) + dot(low_t[1], own1[...])
    send = (dot(low_t[0], recv0[...]) + dot(low_t[1], recv1[...])).astype(bf16)
    inner = send_out.shape[0]
    for index in range(send_out.shape[1] // inner):
        part = slice(index * inner, (index + 1) * inner)
        send_out[:, part] = send[part, :]
    total = None
    for index, seg in enumerate((seg0, seg1)):
        part = slice(index * half, (index + 1) * half)
        tail = gate_tail[8 * index : 8 * index + 8, :half].astype(f32)
        logit_grad = logit_grads(chosen[:, part], probs[:, part], gate_own[:, part], tail)
        for _ in range(3):
            piece = logit_grad.astype(bf16)
            product = dot(piece, seg[...])
            total = product if total is None else total + product
            logit_grad = logit_grad - piece.astype(f32)
    router_out[...] = total


def attn_grad(low, ctx_own, ctx_recv, segments, probs, chosen, gate_own, back_recv):
    half, inner = ctx_own[0].shape
    width = low.shape[1]
    columns = whole_spec((8, 2 * half))
    gate_tail = pl.BlockSpec((16, width), lambda i: (2 * half // 16, 0))
    return kernel_call(
        attn_grad_kernel,
        (1,),
        [whole_spec((2 * half, width))]
        + [whole_spec((half, inner))] * 4
        + [whole_spec((half, width))] * 2
        + [columns] * 3
        + [gate_tail],
        [whole_spec((width, inner)), whole_spec((inner, width)), whole_spec((8, width))],
        [shaped((width, inner), f32), shaped((inner, width), bf16), shaped((8, width), f32)],
        [],
        "attn_grad",
        20,
    )(low, *ctx_own, *ctx_recv, *segments, probs, chosen, gate_own, back_recv)


def attend_back_kernel(
    query_rows, last, split, info, parity, own, oth, ctx_own, ctx_oth, up_own, up_oth, log_ref,
    normed_own, normed_oth, weights, *refs,
):
    if last:
        before, one_own, one_oth, mine, send, key_sum, value_sum, grads, normed_t, all_grads = refs
    else:
        extra, one_own, one_oth, mine, key_sum, value_sum, grads, normed_t, all_grads = refs
    half = own.shape[0]
    row = lax.broadcasted_iota(jnp.int32, (half, PAIR), 0)
    zeros = jnp.zeros((half, PAIR), bf16)
    seen = (row + info[1] < info[0], row + info[2] < info[0])
    sides = ((own, ctx_own, up_own), (oth, ctx_oth, up_oth))

    def all_keys(part):
        first, last = part * PAIR, (part + 1) * PAIR
        return jnp.concatenate(
            [
                jnp.where(seen[0], own[:, first:last], zeros),
                jnp.where(seen[1], oth[:, first:last], zeros),
            ],
            0,
        )

    keys, values = all_keys(1), all_keys(2)
    keys_t = jnp.transpose(keys)
    lane = lax.broadcasted_iota(jnp.int32, (query_rows, PAIR), 1)
    sum_lane = lax.broadcasted_iota(jnp.int32, (8, PAIR), 1)
    sum_row = lax.broadcasted_iota(jnp.int32, (8, PAIR), 0)
    head_sum = jnp.where((sum_lane < HEAD_DIM) == (sum_row == 0), 1.0, 0.0).astype(bf16)
    for side, (src, ctx, up) in enumerate(sides):
        for block in range(half // query_rows):
            rows = slice(block * query_rows, (block + 1) * query_rows)
            first = side * half + block * query_rows
            query, grad = src[rows, :PAIR], up[rows, :]
            product = grad.astype(f32) * ctx[rows, :].astype(f32)
            coarse = product.astype(bf16)
            fine = (product - coarse.astype(f32)).astype(bf16)
            delta = dot_nt(head_sum, coarse) + dot_nt(head_sum, fine)
            query_grads, key_grads, value_grads = [], [], []
            for head in range(2):
                of_head = (lane < HEAD_DIM) == (head == 0)
                query_h = jnp.where(of_head, query, jnp.zeros_like(query))
                grad_h = jnp.where(of_head, grad, jnp.zeros_like(grad))
                log_row = log_ref[head : head + 1, first : first + query_rows]
                scores = dot_nt(keys, query_h)
                probs = jnp.exp2(jnp.minimum(scores * LOG_SCALE - log_row, 0.0))
                prob_grad = dot_nt(values, grad_h)
                score_grad = (probs * (prob_grad - delta[head : head + 1, :])).astype(bf16)
                value_grads.append(dot(probs.astype(bf16), grad_h))
                key_grads.append(dot(score_grad, query_h))
                query_grads.append(
                    dot(keys_t[head * HEAD_DIM : (head + 1) * HEAD_DIM, :], score_grad)
                )
            value_grad = value_grads[0] + value_grads[1]
            key_grad = key_grads[0] + key_grads[1]
            if side == 0 and block == 0:
                value_sum[...] = value_grad
                key_sum[...] = key_grad
            else:
                value_sum[...] += value_grad
                key_sum[...] += key_grad
            query_grad = jnp.transpose(jnp.concatenate(query_grads, 0)) * HEAD_DIM ** (-0.5)
            grads[first : first + query_rows, :PAIR] = query_grad.astype(bf16)
    for side in range(2):
        part = slice(side * half, (side + 1) * half)
        key_grad = jnp.where(seen[side], key_sum[part, :] * HEAD_DIM ** (-0.5), 0.0)
        grads[part, PAIR : 2 * PAIR] = key_grad.astype(bf16)
        grads[part, 2 * PAIR :] = jnp.where(seen[side], value_sum[part, :], 0.0).astype(bf16)

    pair = pl.program_id(0)

    @pl.when(pair == 0)
    def _():
        normed_t[:, :half] = jnp.transpose(normed_own[...])
        normed_t[:, half:] = jnp.transpose(normed_oth[...])

    all_grads[:, pl.ds(pl.multiple_of(pair * 3 * PAIR, 3 * PAIR), 3 * PAIR)] = grads[...]

    @pl.when(pair == pl.num_programs(0) - 1)
    def _():
        one_own[...] = dot_nt(all_grads[:half, :], weights[...])
        one_oth[:half, :] = dot_nt(all_grads[half:, :], weights[...]).astype(bf16)
        if not last:
            one_oth[half:, :] = extra[...]

    product = dot(normed_t[...], grads[...])
    if not last:
        mine[...] = product
        return
    product = (product + before[...]).astype(bf16)
    if not split:
        mine[...] = product
        return
    block = mine.shape[1]
    odd = parity[0]
    for index in range(mine.shape[0]):
        even = product[2 * index * block : (2 * index + 1) * block]
        other = product[(2 * index + 1) * block : (2 * index + 2) * block]
        mine[index] = jnp.where(odd == 0, even, other)
        send[index] = jnp.where(odd == 0, other, even)


def attend_back(
    info, parity, own, oth, seq, ctx_own, ctx_oth, up_own, up_oth, logs, normed_own, normed_oth,
    weights, blocks, before, last,
):
    half, columns = oth.shape
    width = weights.shape[0]
    pairs = columns // (3 * PAIR)
    query_rows = min(256, half)
    block = width // blocks
    split = block % 16 == 0
    one = pl.BlockSpec((half, PAIR), lambda p: (0, p))
    three = pl.BlockSpec((half, 3 * PAIR), lambda p: (0, p))
    weight = pl.BlockSpec((width, 3 * PAIR), lambda p: (0, p))
    sent = half if last else half + before.shape[0]
    out_specs = [whole_spec((half, width)), whole_spec((sent, width))]
    out_shape = [shaped((half, width), f32), shaped((sent, width), bf16)]
    if not last:
        out_specs.append(weight)
        out_shape.append(shaped((width, columns), f32))
    elif split:
        out_specs += [pl.BlockSpec((blocks // 2, block, 3 * PAIR), lambda p: (0, 0, p))] * 2
        out_shape += [shaped((blocks // 2, block, columns), bf16)] * 2
    else:
        out_specs += [weight, weight]
        out_shape += [shaped((width, columns), bf16)] * 2
    outs = kernel_call(
        functools.partial(attend_back_kernel, query_rows, last, split),
        (pairs,),
        [SMEM_SPEC, SMEM_SPEC, pl.BlockSpec((half, 3 * PAIR), lambda p: (seq, p)), three]
        + [one, one] + [pl.BlockSpec((half, PAIR), lambda p: (seq, p))] * 2
        + [pl.BlockSpec((8, 2 * half), lambda p: (p, 0))]
        + [pl.BlockSpec((half, width), lambda p: (seq, 0)), whole_spec((half, width)), whole_spec((width, columns))]
        + [weight if last else whole_spec(before.shape)],
        out_specs,
        out_shape,
        [
            pltpu.VMEM((2 * half, PAIR), f32),
            pltpu.VMEM((2 * half, PAIR), f32),
            pltpu.VMEM((2 * half, 3 * PAIR), bf16),
            pltpu.VMEM((width, 2 * half), bf16),
            pltpu.VMEM((2 * half, columns), bf16),
        ],
        "attend_back",
        48,
    )(
        info, parity, own, oth, ctx_own, ctx_oth, up_own, up_oth, logs, normed_own, normed_oth,
        weights, before,
    )
    if last and not split:
        outs = list(outs[:2]) + list(split_even_odd(outs[2].reshape(blocks, block, columns), parity[0]))
    return outs


def finish_kernel(
    steps, info, rows, one_own0, one_own1, recv0, recv1, grad, res0, res1, result_own,
    result_recv, gate, gain, input_grad, activations,
):
    step = pl.program_id(0)
    block = rows.shape[0]
    for seq, refs in enumerate(((one_own0, recv0, res0), (one_own1, recv1, res1))):

        @pl.when(step // steps == seq)
        def _(seq=seq, refs=refs):
            one_own, recv, res = refs
            x = rows[...].astype(f32)
            one_grad = one_own[...] + recv[...].astype(f32)
            input_grad[...] = grad[...] + norm_back(x, inverse_rms(x), gain[...], one_grad)
            combined = result_own[...].astype(f32) + result_recv[...].astype(f32)
            mixed = res[...] + gate[...] * combined
            slot = lax.broadcasted_iota(jnp.int32, (block, 1), 0) + step % steps * block
            valid = slot + info[2] * (steps * block) < info[seq]
            activations[...] = jnp.where(valid, mixed, 0.0).astype(bf16)


def finish(info, rows, one_own, one_recv, grads, residual, result_own, result_recv, gate, gain):
    half, width = residual[0].shape
    block = min(256, half)
    steps = half // block
    tile = pl.BlockSpec((block, width), lambda i: (i, 0))
    first = pl.BlockSpec((block, width), lambda i: (jnp.minimum(i, steps - 1), 0))
    second = pl.BlockSpec((block, width), lambda i: (jnp.maximum(i - steps, 0), 0))
    return kernel_call(
        functools.partial(finish_kernel, steps),
        (2 * steps,),
        [SMEM_SPEC, tile]
        + [first, second] * 2
        + [tile, first, second]
        + [tile, tile, pl.BlockSpec((block, 1), lambda i: (i, 0)), whole_spec((1, width))],
        [tile, tile],
        [shaped((2 * half, width), f32), shaped((2 * half, width), bf16)],
        [],
        "finish",
        58,
    )(info, rows, *one_own, *one_recv, grads, *residual, result_own, result_recv, gate, gain)


def after(array, *earlier):
    return lax.optimization_barrier((array,) + earlier)[0]


def split_even_odd(array, odd):
    lead = array.shape[:-3]
    halves = array.reshape(lead + (array.shape[-3] // 2, 2) + array.shape[-2:])
    axis = len(lead) + 1
    return (
        lax.dynamic_index_in_dim(halves, odd, axis, keepdims=False),
        lax.dynamic_index_in_dim(halves, 1 - odd, axis, keepdims=False),
    )


class Halving:
    def __init__(self, parts, experts, block, bits, table, order):
        self.parts = [(array, total, first, list(bits)) for array, total, first in parts]
        self.experts, self.block, self.table = experts, block, table
        self.left, self.order, self.picked = list(bits), list(order), set()
        self.size = len(bits) + 1
        self.columns = parts[0][0].shape[-1]

    def total(self, row, dtype, transpose=False):
        size, picked = self.size, set(self.picked)
        group = 2 if self.experts % 2 == 0 else 1
        arrays, specs = [], []
        for array, total, first, bits in self.parts:
            arrays.append(array.reshape((total,) + (2,) * len(bits) + (self.block, self.columns)))
            shape = tuple(None if bit in picked else 2 for bit in bits)

            def place(step, table, first=first, bits=bits):
                picks = tuple(table[row * size + bit] if bit in picked else 0 for bit in bits)
                return (first // group + step,) + picks + (0, 0)

            specs.append(pl.BlockSpec((group,) + shape + (self.block, self.columns), place))
        tail = (self.columns, self.block) if transpose else (self.block, self.columns)
        out = (self.experts,) + (2,) * len(self.left) + tail

        def kernel(table, *refs):
            value = refs[0][...].astype(f32)
            for ref in refs[1:-1]:
                value += ref[...].astype(f32)
            if transpose:
                for index in range(group):
                    refs[-1][index] = jnp.transpose(value[index]).astype(dtype)
            else:
                refs[-1][...] = value.astype(dtype)

        return pl.pallas_call(
            kernel,
            grid_spec=pltpu.PrefetchScalarGridSpec(
                num_scalar_prefetch=1,
                grid=(self.experts // group,),
                in_specs=specs,
                out_specs=pl.BlockSpec(
                    (group,) + out[1:], lambda e, t: (e,) + (0,) * (len(out) - 1)
                ),
            ),
            out_shape=shaped(out, dtype),
            compiler_params=pltpu.CompilerParams(vmem_limit_bytes=58 * 2**20),
            cost_estimate=SMALL_COST,
            name="half_sum",
        )(self.table, *arrays)

    def send(self):
        bit = self.order[0]
        self.left.remove(bit)
        self.picked.add(bit)
        sent = self.total(bit, bf16)
        return sent.reshape(-1, self.columns)

    def step(self, sent):
        recv = exchange(sent, self.order.pop(0), 2**self.size)
        self.parts.append((recv, self.experts, 0, list(self.left)))

    def spread(self):
        bits = list(self.left)
        size, picked, count = self.size, set(self.picked), len(self.parts)
        masks = range(2 ** len(bits))
        group = 2 if self.experts % 2 == 0 else 1
        arrays, specs = [], []
        for array, total, first, dims in self.parts:
            arrays.append(array.reshape((total,) + (2,) * len(dims) + (self.block, self.columns)))
            shape = tuple(None if bit in picked else 2 for bit in dims)

            def place(step, table, first=first, dims=dims):
                picks = tuple(table[size * size + bit] if bit in picked else 0 for bit in dims)
                return (first // group + step,) + picks + (0, 0)

            specs.append(pl.BlockSpec((group,) + shape + (self.block, self.columns), place))
        out = (self.experts, self.block, self.columns)

        def kernel(table, *refs):
            for mask in masks:
                at = tuple(
                    table[size * size + bit] ^ ((mask >> (len(bits) - 1 - i)) & 1)
                    for i, bit in enumerate(bits)
                )
                at = (slice(None),) + at
                value = refs[0][at].astype(f32)
                for ref in refs[1:count]:
                    value += ref[at].astype(f32)
                refs[count + mask][...] = value.astype(bf16)

        own, *sent = pl.pallas_call(
            kernel,
            grid_spec=pltpu.PrefetchScalarGridSpec(
                num_scalar_prefetch=1,
                grid=(self.experts // group,),
                in_specs=specs,
                out_specs=[
                    pl.BlockSpec((group, self.block, self.columns), lambda e, t: (e, 0, 0))
                ] * len(masks),
            ),
            out_shape=[shaped(out, bf16)] * len(masks),
            compiler_params=pltpu.CompilerParams(vmem_limit_bytes=14 * 2**20),
            cost_estimate=SMALL_COST,
            name="spread_sum",
        )(self.table, *arrays)
        recv = []
        for mask, array in zip(masks[1:], sent):
            flip = sum(
                1 << bit for i, bit in enumerate(bits) if (mask >> (len(bits) - 1 - i)) & 1
            )
            pairs = [(i, i ^ flip) for i in range(2**size)]
            flat = lax.ppermute(array.reshape(-1, self.columns), "dp", pairs)
            recv.append(flat.reshape(out))
        return own, recv

    def last_recv(self, *earlier):
        array, *rest = self.parts[-1]
        if earlier:
            self.parts[-1] = (after(array, *earlier), *rest)
        return self.parts[-1][0]


def exchange(array, bit, size):
    return lax.ppermute(array, "dp", [(i, i ^ (1 << bit)) for i in range(size)])


def body(
    inputs,
    cotangent,
    lengths,
    routes,
    norm1_gain,
    w_query,
    w_key,
    w_value,
    w_attn_out,
    norm2_gain,
    w_router,
    w_expert_in,
    w_expert_out,
):
    seqs, half, width = inputs.shape
    slots = routes.shape[1]
    inner = w_query.shape[1]
    pairs = inner // PAIR
    side = lax.axis_index("tensor")
    dp_index = lax.axis_index("dp")
    dp_size = lax.axis_size("dp")
    own_tokens = seqs * half
    gain_one = norm1_gain.astype(f32)[None, :]
    gain_two = norm2_gain.astype(f32)[None, :]

    def swap(array):
        return lax.ppermute(array, "tensor", [(0, 1), (1, 0)])

    dp_rows = width // dp_size
    bits = dp_size.bit_length() - 1
    parity = (dp_index & 1).reshape(1).astype(jnp.int32)
    rows = inputs.reshape(own_tokens, width)
    cot_rows = cotangent.reshape(own_tokens, width)
    rows_oth = [swap(inputs[0])]
    info = jnp.concatenate([lengths, side[None]]).astype(jnp.int32)
    infos = [
        jnp.stack([lengths[s], side * half, (1 - side) * half]).astype(jnp.int32)
        for s in range(seqs)
    ]
    slots_rows, slots_column, chosen, bounds = plan(info, routes.reshape(seqs, slots))
    w_pairs = jnp.concatenate(
        [w[:, p * PAIR : (p + 1) * PAIR] for p in range(pairs) for w in (w_query, w_key, w_value)],
        1,
    )
    flips = (dp_index >> jnp.arange(bits)) & 1
    table = jnp.concatenate(
        [(flips[None, :] ^ jnp.eye(bits, dtype=flips.dtype)).reshape(-1), flips]
    ).astype(jnp.int32)
    w_route = jnp.pad(w_router.T, ((0, 8 - EXPERTS), (0, 0)))
    normed_own, proj_own = project(rows, gain_one, w_pairs, "project_own")
    first_in = after(rows_oth[0], proj_own, bounds, w_route, table)
    rows_oth[0] = first_in
    for s in range(1, seqs):
        rows_oth.append(swap(after(inputs, rows_oth[-1])[s]))
    normed_oth, proj_oth, ctx_own, ctx_oth, ctx_recv, logs = [], [], [], [], [], []
    for s in range(seqs):
        raw = rows_oth[s] if s == 0 else after(rows_oth[s], ctx_oth[s - 1])
        if s == 1:
            attn_out_oth = swap(after(w_attn_out, raw))
        normed_part, proj_part = project(raw, gain_one, w_pairs, "project_oth")
        normed_oth.append(normed_part)
        proj_oth.append(proj_part)
        own_part, oth_part, log_part = attend(infos[s], proj_own, proj_part, s)
        ctx_own.append(own_part)
        ctx_oth.append(oth_part)
        logs.append(log_part)
        ctx_recv.append(swap(oth_part))
    residual, normed_two, two_oth = [], [], []
    for s in range(seqs):
        ctx_recv[s] = after(ctx_recv[s], ctx_oth[-1] if s == 0 else normed_two[s - 1])
        res_part, normed_part = residual_of(
            rows, s, ctx_own[s], ctx_recv[s], w_attn_out, attn_out_oth, gain_two
        )
        residual.append(res_part)
        normed_two.append(normed_part)
        two_oth.append(swap(normed_part))

    segments = normed_two + two_oth
    cot_oth = swap(after(cotangent, *two_oth))
    x_rows, hidden, slope, result, probs, gate = expert_forward(
        bounds, slots_rows, segments, w_expert_in, w_expert_out, w_route, chosen
    )
    (result_oth,) = collect(
        bounds, slots_column, result, seqs, seqs, width, bf16, "collect_result_oth", 64
    )
    (result_own,) = collect(
        bounds, slots_column, after(result, result_oth), 0, seqs, width, bf16, "collect_result_own"
    )
    result_recv = swap(result_oth)
    cot_oth = after(cot_oth, result_own)
    up_rows, pre_grad, back = expert_backward(
        bounds, slots_rows, cotangent, cot_oth, w_expert_in, w_expert_out, gate, result, slope
    )
    (back_oth,) = collect(
        bounds, slots_column, back, seqs, seqs, width, bf16, "collect_back_oth", 8
    )
    back_recv = swap(back_oth)
    halved = list(range(bits - 1, 0, -1))
    order_x = list(range(1, bits))
    columns = w_expert_in.shape[2]
    grad_out_t = expert_grad(
        after(bounds, back_oth, result_recv), parity, up_rows, hidden, 1, "grad_expert_out"
    )
    back_own, gate_own = collect(
        bounds, slots_column, after(back, grad_out_t), 0, seqs, width, f32, "collect_back_own"
    )
    in_mine, in_send = expert_grad(
        after(bounds, back_own), parity, x_rows, pre_grad, dp_size, "grad_expert_in"
    )
    recv = after(back_recv, in_mine)
    in_recv = exchange(after(in_send, recv).reshape(-1, columns), 0, dp_size)
    out_share_t = lax.psum_scatter(
        after(grad_out_t, recv), "dp", scatter_dimension=1, tiled=True
    )

    residual_grad, residual_low, up_own, up_send = residual_grad_of(
        info, back_own, recv, probs, chosen, gate_own, w_route, residual, cot_rows, gain_two,
        w_attn_out, attn_out_oth,
    )
    up_oth = swap(up_send)
    in_mine, in_recv = in_mine.reshape(-1, columns), after(in_recv, up_send)
    order_z = order_x[1:] + order_x[:1]
    in_sums = [
        Halving(
            [(in_mine, EXPERTS, first), (in_recv, EXPERTS, first)],
            EXPERTS // 2, dp_rows, halved, table, order,
        )
        for first, order in ((0, order_x), (EXPERTS // 2, order_z))
    ]
    in_sent = [part.send() for part in in_sums]
    for part, sent in zip(in_sums, in_sent):
        part.step(sent)
    grad_attn_t, grad_attn_send, grad_router = attn_grad(
        after(residual_low, *in_sent), ctx_own, ctx_recv, normed_two, probs, chosen, gate_own, recv
    )

    log_rows = after(logs[0], grad_attn_t)
    one_own0, one_oth0, grad_pairs = attend_back(
        infos[0], parity, proj_own, proj_oth[0], 0, ctx_own[0], ctx_oth[0], up_own, up_oth,
        log_rows, normed_own, normed_oth[0], w_pairs, dp_size, grad_attn_send, False,
    )
    one_recv = [swap(one_oth0)]
    for part in in_sums:
        part.last_recv(one_oth0)
    in_sent = [part.send() for part in in_sums]
    log_rows = after(logs[1], *in_sent)
    one_own1, one_oth1, *grad_pairs = attend_back(
        infos[1], parity, proj_own, proj_oth[1], 1, ctx_own[1], ctx_oth[1], up_own, up_oth,
        log_rows, normed_own, normed_oth[1], w_pairs, dp_size, grad_pairs, True,
    )
    one_recv.append(swap(one_oth1))
    attn_recv = after(one_recv[0], one_oth1)[half:].astype(f32)
    grad_attn_t = grad_attn_t + jnp.concatenate(
        [attn_recv[:, i * inner : (i + 1) * inner] for i in range(width // inner)], 0
    )
    grad_router = after(grad_router, one_oth1)[:EXPERTS].T
    router_high = grad_router.astype(bf16)
    router_low = (grad_router - router_high.astype(f32)).astype(bf16)
    small = jnp.concatenate([router_high, router_low], 1)
    small = jnp.pad(small, ((0, 0), (0, PAIR - 2 * EXPERTS)))
    rest = jnp.concatenate([grad_attn_t.astype(bf16), small], 1).reshape(dp_size, dp_rows, -1)
    rest = split_even_odd(rest, parity[0])
    pairs_mine, pairs_send = [part.reshape(-1, part.shape[-1]) for part in grad_pairs]
    rest_mine, rest_send = [part.reshape(-1, part.shape[-1]) for part in rest]
    for part, sent in zip(in_sums, in_sent):
        part.step(sent)
    last_send = after(pairs_send, *[part.last_recv() for part in in_sums])
    last_mine = jnp.concatenate([pairs_mine, rest_mine], 1)
    last_recv = jnp.concatenate(
        [exchange(last_send, 0, dp_size), exchange(rest_send, 0, dp_size)], 1
    )
    for part in in_sums:
        part.last_recv(last_send)
        while part.order:
            part.step(part.send())
    last_sum = Halving(
        [(last_mine, 1, 0), (last_recv, 1, 0)],
        1, dp_rows, halved, table, [bit for bit in order_x if bit < bits - 2],
    )
    while last_sum.order:
        last_sum.step(last_sum.send())
    last_sum.last_recv(one_recv[1])
    last_own, last_recv = last_sum.spread()
    last_share = sum(part.astype(f32) for part in [last_own] + last_recv)[0]
    input_grad, activations = finish(
        info, rows, (one_own0, one_own1), (one_recv[0], after(one_recv[1], last_own)), residual_grad,
        residual, result_own, result_recv, gate, gain_one,
    )
    late = in_sums[1].total(bits, f32)
    in_sums[0].last_recv(input_grad, late)
    in_share = jnp.concatenate([in_sums[0].total(bits, f32), late], 0)
    out_share = jnp.swapaxes(out_share_t, 1, 2).astype(f32)

    own_rows = dp_rows // 2

    def share_rows(array, axis=0):
        return lax.dynamic_slice_in_dim(array, dp_index * dp_rows, dp_rows, axis)

    pair_share = last_share[:, : 3 * inner]
    shares = [
        jnp.concatenate(
            [pair_share[:, (3 * p + k) * PAIR : (3 * p + k + 1) * PAIR] for p in range(pairs)], 1
        )
        for k in range(3)
    ]
    attn_share = last_share[:, 3 * inner : 4 * inner].T
    router_share = (
        last_share[:, 4 * inner : 4 * inner + EXPERTS]
        + last_share[:, 4 * inner + EXPERTS : 4 * inner + 2 * EXPERTS]
    )
    sum_one = jnp.sum(pair_share * share_rows(w_pairs).astype(f32), axis=1)
    sum_two = jnp.sum(in_share * share_rows(w_expert_in, 1).astype(f32), axis=(0, 2))
    sums = jnp.concatenate([jnp.stack([sum_one, sum_two]), router_share.T], 0)
    sums_recv = swap(sums)
    sums = sums + after(sums_recv, out_share)
    router_share = sums[2:].T
    router_sum = jnp.sum(router_share * share_rows(w_router).astype(f32), axis=1)
    gain_grads = jnp.stack(
        [sums[0] / share_rows(gain_one[0]), (sums[1] + router_sum) / share_rows(gain_two[0])]
    )
    gain_grads = lax.dynamic_slice_in_dim(gain_grads, side * own_rows, own_rows, 1)
    router_out = lax.dynamic_slice_in_dim(router_share, side * own_rows, own_rows, 0)
    return (
        activations.reshape(inputs.shape),
        input_grad.reshape(inputs.shape),
        gain_grads[0],
        shares[0],
        shares[1],
        shares[2],
        attn_share,
        gain_grads[1],
        router_out,
        in_share,
        out_share,
    )


def solution(mesh):
    in_specs = (
        P("dp", "tensor", None),
        P("dp", "tensor", None),
        P("dp"),
        P("dp", None, None),
        P(),
        P(None, "tensor"),
        P(None, "tensor"),
        P(None, "tensor"),
        P("tensor", None),
        P(),
        P(),
        P(None, None, "tensor"),
        P(None, "tensor", None),
    )
    out_specs = (
        P("dp", "tensor", None),
        P("dp", "tensor", None),
        P(("dp", "tensor")),
        P("dp", "tensor"),
        P("dp", "tensor"),
        P("dp", "tensor"),
        P("tensor", "dp"),
        P(("dp", "tensor")),
        P(("dp", "tensor"), None),
        P(None, "dp", "tensor"),
        P(None, "tensor", "dp"),
    )
    return jax.shard_map(body, mesh=mesh, in_specs=in_specs, out_specs=out_specs, check_vma=False)
```

```python
import functools
import math

import jax
import jax.numpy as jnp
from jax import lax
from jax.experimental import pallas as pl
from jax.experimental.pallas import tpu as pltpu
from jax.sharding import PartitionSpec as P

HEAD_DIM = 64
EXPERTS = 4
CAP = 640
PAIR = 2 * HEAD_DIM
GELU_C = math.sqrt(2.0 / math.pi)
GELU_A = 0.044715
LOG_SCALE = math.log2(math.e) * HEAD_DIM ** (-0.5)

norm_eps = 1e-06
bf16 = jnp.bfloat16
f32 = jnp.float32
SMALL_COST = pl.CostEstimate(flops=1, bytes_accessed=1, transcendentals=0)


def dot(left, right):
    return lax.dot_general(left, right, (((1,), (0,)), ((), ())), preferred_element_type=f32)


def dot_nt(left, right):
    return lax.dot_general(left, right, (((1,), (1,)), ((), ())), preferred_element_type=f32)


def dot_tn(left, right):
    return lax.dot_general(left, right, (((0,), (0,)), ((), ())), preferred_element_type=f32)


def whole_spec(shape):
    return pl.BlockSpec(shape, lambda *_: (0,) * len(shape))


SMEM_SPEC = pl.BlockSpec(memory_space=pltpu.SMEM)


def kernel_call(kernel, grid, in_specs, out_specs, out_shape, scratch, name, limit=58):
    return pl.pallas_call(
        kernel,
        grid=grid,
        in_specs=in_specs,
        out_specs=out_specs,
        out_shape=out_shape,
        scratch_shapes=scratch,
        compiler_params=pltpu.CompilerParams(vmem_limit_bytes=limit * 2**20),
        cost_estimate=SMALL_COST,
        name=name,
    )


def shaped(shape, dtype):
    return jax.ShapeDtypeStruct(shape, dtype)


def inverse_rms(rows):
    return lax.rsqrt(jnp.mean(rows * rows, axis=-1, keepdims=True) + norm_eps)


def norm_back(rows, inverse, gain, upstream):
    weighted = upstream * gain
    inner_mean = jnp.mean(rows * weighted, axis=-1, keepdims=True)
    return inverse * weighted - rows * inverse**3 * inner_mean


def as_column(row):
    return jnp.transpose(jnp.broadcast_to(row, (PAIR, row.shape[1])))[:, :1]


def plan_kernel(info, routes, slots_rows, slots_column, chosen, bounds):
    half = slots_rows.shape[1]
    side = info[2]
    before_of = lax.broadcasted_iota(jnp.int32, (half, half), 0)
    upto = jnp.where(before_of <= lax.broadcasted_iota(jnp.int32, (half, half), 1), 1.0, 0.0)
    upto = upto.astype(bf16)
    expert = lax.broadcasted_iota(jnp.int32, (8, half), 0)
    capacity = (5 * (info[0] + info[1]) + 4 * EXPERTS - 1) // (4 * EXPERTS)
    column = jnp.zeros((8, 1), f32)
    row = jnp.zeros((8, 8), f32)
    limit = capacity.astype(f32)
    for seq in range(2):
        for part in range(2):
            local = seq + jnp.where(side == part, 0, 2)
            route = routes[seq : seq + 1, part * half : (part + 1) * half]
            slot = lax.broadcasted_iota(jnp.int32, (1, half), 1) + part * half
            valid = slot < info[seq]
            routed = expert == route
            hit = jnp.where(jnp.logical_and(routed, valid), 1.0, 0.0)
            counts = dot(hit.astype(bf16), upto) + column
            position = jnp.sum(hit * counts, axis=0, keepdims=True).astype(jnp.int32) - 1
            keep = jnp.logical_and(valid, position < capacity)
            taken = jnp.where(keep, route * CAP + position, EXPERTS * CAP)
            slots_rows[pl.ds(local, 1), :] = taken
            first = pl.multiple_of(local * half, half)
            slots_column[pl.ds(first, half), :] = as_column(taken.astype(f32)).astype(jnp.int32)
            picked = jnp.where(expert == EXPERTS, jnp.where(valid, 1.0, 0.0), 0.0)
            chosen[:, pl.ds(first, half)] = jnp.where(routed, 1.0, picked)
            bounds[pl.ds(local, 1), :] = jnp.minimum(row[:1], limit).astype(jnp.int32)
            column += jnp.sum(hit, axis=1, keepdims=True)
            row += dot_nt(jnp.ones((8, half), bf16), hit.astype(bf16))
            bounds[pl.ds(4 + local, 1), :] = jnp.minimum(row[:1], limit).astype(jnp.int32)
    bounds[8:16, :] = jnp.minimum(row, limit).astype(jnp.int32)


def plan(info, routes):
    seqs, slots = routes.shape
    half = slots // 2
    return kernel_call(
        plan_kernel,
        (1,),
        [SMEM_SPEC, whole_spec((seqs, slots))],
        [
            whole_spec((4, half)),
            whole_spec((4 * half, 1)),
            whole_spec((8, 4 * half)),
            whole_spec((16, 8)),
        ],
        [
            shaped((4, half), jnp.int32),
            shaped((4 * half, 1), jnp.int32),
            shaped((8, 4 * half), f32),
            shaped((16, 8), jnp.int32),
        ],
        [],
        "plan",
        12,
    )(info, routes)


def project_kernel(rows, gain, weights, normed, proj):
    x = rows[...].astype(f32)
    low = (x * inverse_rms(x) * gain[...]).astype(bf16)
    normed[...] = low
    proj[...] = dot(low, weights[...]).astype(bf16)


def project(rows, gain, weights, name):
    count, width = rows.shape
    columns = weights.shape[1]
    block = min(256, count)
    tile = pl.BlockSpec((block, width), lambda i: (i, 0))
    return kernel_call(
        project_kernel,
        (count // block,),
        [tile, whole_spec((1, width)), whole_spec((width, columns))],
        [tile, pl.BlockSpec((block, columns), lambda i: (i, 0))],
        [shaped((count, width), bf16), shaped((count, columns), bf16)],
        [],
        name,
        40,
    )(rows, gain, weights)


def residual_kernel(rows, ctx_own, ctx_recv, w_own, w_oth, gain, residual, normed):
    total = rows[...].astype(f32) + dot(ctx_own[...], w_own[...])
    total += dot(ctx_recv[...], w_oth[...])
    residual[...] = total
    normed[...] = (total * inverse_rms(total) * gain[...]).astype(bf16)


def residual_of(rows, seq, ctx_own, ctx_recv, w_own, w_oth, gain):
    half, inner = ctx_own.shape
    width = rows.shape[1]
    block = min(256, half)
    steps = half // block
    tile = pl.BlockSpec((block, width), lambda i: (i, 0))
    ctx = pl.BlockSpec((block, inner), lambda i: (i, 0))
    weight = whole_spec((inner, width))
    return kernel_call(
        residual_kernel,
        (steps,),
        [
            pl.BlockSpec((block, width), lambda i: (i + seq * steps, 0)),
            ctx, ctx, weight, weight, whole_spec((1, width)),
        ],
        [tile, tile],
        [shaped((half, width), f32), shaped((half, width), bf16)],
        [],
        "residual",
        40,
    )(rows, ctx_own, ctx_recv, w_own, w_oth, gain)


def attend_kernel(query_rows, info, own, oth, ctx_own, ctx_oth, log_ref):
    half = own.shape[0]
    row = lax.broadcasted_iota(jnp.int32, (half, PAIR), 0)
    lane = lax.broadcasted_iota(jnp.int32, (half, PAIR), 1)
    zeros = jnp.zeros((half, PAIR), bf16)
    hidden_key = jnp.full((half, PAIR), -1e30, bf16)
    sides = ((own, ctx_own, row + info[1] < info[0]), (oth, ctx_oth, row + info[2] < info[0]))
    keys = []
    for head in range(2):
        mine = (lane < HEAD_DIM) == (head == 0)
        spare = lane == (HEAD_DIM if head == 0 else 0)
        parts = []
        for ref, _, seen in sides:
            mask_value = jnp.where(seen, zeros, hidden_key)
            key = ref[:, PAIR : 2 * PAIR]
            parts.append(jnp.where(mine, key, jnp.where(spare, mask_value, zeros)))
        keys.append(jnp.concatenate(parts, 0))
    values_t = jnp.transpose(jnp.concatenate([own[:, 2 * PAIR :], oth[:, 2 * PAIR :]], 0))
    q_lane = lax.broadcasted_iota(jnp.int32, (query_rows, PAIR), 1)
    steps = [
        (side, block, head)
        for side in range(2)
        for block in range(half // query_rows)
        for head in range(2)
    ]

    def scores_of(step):
        side, block, head = step
        query = sides[side][0][block * query_rows : (block + 1) * query_rows, :PAIR]
        mine = (q_lane < HEAD_DIM) == (head == 0)
        spare = q_lane == (HEAD_DIM if head == 0 else 0)
        query = jnp.where(
            mine, query, jnp.where(spare, jnp.ones_like(query), jnp.zeros_like(query))
        )
        return dot_nt(keys[head], query)

    current = scores_of(steps[0])
    outs = [None, None]
    for index, (side, block, head) in enumerate(steps):
        following = scores_of(steps[index + 1]) if index + 1 < len(steps) else None
        top = jnp.max(current, axis=0, keepdims=True) * LOG_SCALE
        exponent = jnp.exp2(current * LOG_SCALE - top)
        total = jnp.sum(exponent, axis=0, keepdims=True)
        head_values = values_t[head * HEAD_DIM : (head + 1) * HEAD_DIM, :]
        outs[head] = dot(head_values, exponent.astype(bf16)) * (1.0 / total)
        first = side * half + block * query_rows
        log_ref[head : head + 1, first : first + query_rows] = top + jnp.log2(total)
        if head == 1:
            sides[side][1][block * query_rows : (block + 1) * query_rows, :] = jnp.transpose(
                jnp.concatenate(outs, 0)
            ).astype(bf16)
        current = following


def attend(info, own, oth, seq):
    half, width = oth.shape
    pairs = width // (3 * PAIR)
    query_rows = min(512, half)
    out = pl.BlockSpec((half, PAIR), lambda p: (0, p))
    shape = jax.ShapeDtypeStruct((half, width // 3), bf16)
    return pl.pallas_call(
        functools.partial(attend_kernel, query_rows),
        grid=(pairs,),
        in_specs=[
            pl.BlockSpec(memory_space=pltpu.SMEM),
            pl.BlockSpec((half, 3 * PAIR), lambda p: (seq, p)),
            pl.BlockSpec((half, 3 * PAIR), lambda p: (0, p)),
        ],
        out_specs=[out, out, pl.BlockSpec((8, 2 * half), lambda p: (p, 0))],
        out_shape=[shape, shape, jax.ShapeDtypeStruct((8 * pairs, 2 * half), f32)],
        compiler_params=pltpu.CompilerParams(vmem_limit_bytes=40 * 2**20),
        cost_estimate=SMALL_COST,
        name="attend",
    )(info, own, oth)


WINDOW = 256


def window_rows(count_low, count_high):
    start = (count_low // 16) * 16
    windows = jnp.where(count_high > count_low, (count_high - start + WINDOW - 1) // WINDOW, 0)
    return start, windows


def dispatch_rows(bounds, slots, sources, total, expert):
    total[...] = jnp.zeros_like(total)
    for seg, source in enumerate(sources):
        start, windows = window_rows(bounds[seg, expert], bounds[4 + seg, expert])
        taken = slots[seg : seg + 1, :] - expert * CAP

        @pl.loop(0, windows)
        def _(step, start=start, taken=taken, source=source):
            begin = start + step * WINDOW
            row = pl.multiple_of(jnp.minimum(begin, CAP - WINDOW), 16)
            offset = jnp.where(taken >= begin, taken - row, -1)
            slot = lax.broadcasted_iota(jnp.int32, (WINDOW, offset.shape[1]), 0)
            place = jnp.where(slot == offset, 1.0, 0.0).astype(bf16)
            total[pl.ds(row, WINDOW), :] += dot(place, source[...])


ROW_COUNTS = (256, 320, 384, 512, CAP)


def by_row_count(taken, work):
    below = -1
    for rows in ROW_COUNTS:
        pl.when(jnp.logical_and(taken > below, taken <= rows))(functools.partial(work, rows))
        below = rows


def expert_forward_kernel(
    chunk, bounds, slots, seg0, seg1, seg2, seg3, w_in, w_out, w_route, chosen,
    x_out, hidden_out, slope_out, result_out, probs_out, gate_out, total,
):
    expert = pl.program_id(0)
    half = seg0.shape[0]

    @pl.when(expert == 0)
    def _():
        row = lax.broadcasted_iota(jnp.int32, (8, half), 0)
        for index, seg in enumerate((seg0, seg1, seg2, seg3)):
            part = slice(index * half, (index + 1) * half)
            logits = jnp.where(row < EXPERTS, dot_nt(w_route[...], seg[...]), -1e30)
            exponent = jnp.exp(logits - jnp.max(logits, axis=0, keepdims=True))
            probs = exponent / jnp.sum(exponent, axis=0, keepdims=True)
            probs = jnp.where(row < EXPERTS, probs, 0.0)
            probs_out[:, part] = probs
            gate = jnp.sum(probs * chosen[:, part], axis=0, keepdims=True)
            gate = jnp.where(chosen[EXPERTS : EXPERTS + 1, part] > 0, gate, 0.0)
            gate_out[part, :] = as_column(gate)

    dispatch_rows(bounds, slots, (seg0, seg1, seg2, seg3), total, expert)
    x_out[0] = total[...].astype(bf16)
    block = CAP // 2
    blocks = (bounds[8, expert] + block - 1) // block
    hidden_units = w_in.shape[2]
    columns = [slice(c, c + chunk) for c in range(0, hidden_units, chunk)]

    @pl.loop(blocks, CAP // block)
    def _(step):
        rows = pl.ds(pl.multiple_of(step * block, block), block)
        for out in (hidden_out, slope_out, result_out):
            out[0, rows, :] = jnp.zeros((block, out.shape[2]), bf16)

    @pl.loop(0, blocks)
    def _(step):
        rows = pl.ds(pl.multiple_of(step * block, block), block)
        x = x_out[0, rows, :]
        pre = dot(x, w_in[0, :, columns[0]])
        result = None
        for index, cols in enumerate(columns):
            following = None
            if index + 1 < len(columns):
                following = dot(x, w_in[0, :, columns[index + 1]])
            square = pre * pre
            bend = jnp.tanh(pre * (GELU_C + GELU_C * GELU_A * square))
            half_up = 0.5 + 0.5 * bend
            hidden = (pre * half_up).astype(bf16)
            slope = half_up + pre * (0.5 * GELU_C + 1.5 * GELU_C * GELU_A * square) * (
                1.0 - bend * bend
            )
            hidden_out[0, rows, cols] = hidden
            slope_out[0, rows, cols] = slope.astype(bf16)
            part = dot(hidden, w_out[0, cols, :])
            result = part if result is None else result + part
            pre = following
        result_out[0, rows, :] = result.astype(bf16)


def expert_backward_kernel(
    chunk, bounds, slots, cot_own, cot_oth, w_in, w_out, gate, result, slope,
    up_out, pre_out, back_out, total, gated,
):
    expert = pl.program_id(0)
    seqs, half = cot_own.shape[:2]
    parts = [pl.ds(index * half, half) for index in range(2 * seqs)]

    @pl.when(expert == 0)
    def _():
        for index, part in enumerate(parts):
            cot = (cot_own if index < seqs else cot_oth)[index % seqs].astype(f32)
            gated[part, :] = (gate[part, :] * cot).astype(bf16)

    dispatch_rows(bounds, slots, [gated.at[part] for part in parts], total, expert)
    up_out[0] = total[...].astype(bf16)
    width, hidden_units = w_in.shape[1], w_in.shape[2]
    columns = [slice(c, c + chunk) for c in range(0, hidden_units, chunk)]

    def work(count):
        if count < CAP:
            for out in (pre_out, back_out):
                out[0, count:, :] = jnp.zeros((CAP - count, out.shape[2]), bf16)
        rows = slice(0, count)
        lane = lax.broadcasted_iota(jnp.int32, (count, PAIR), 1)
        up = up_out[0, rows, :]
        grad = dot_nt(up, w_out[0, columns[0], :])
        back = None
        gate_grad = jnp.sum(
            up.astype(f32) * result[0, rows, :].astype(f32), axis=1, keepdims=True
        )
        for index, cols in enumerate(columns):
            following = None
            if index + 1 < len(columns):
                following = dot_nt(up, w_out[0, columns[index + 1], :])
            pre_grad = (grad * slope[0, rows, cols].astype(f32)).astype(bf16)
            pre_out[0, rows, cols] = pre_grad
            part = dot_nt(pre_grad, w_in[0, :, cols])
            back = part if back is None else back + part
            grad = following
        back_out[0, rows, :width] = back.astype(bf16)
        high = gate_grad.astype(bf16).astype(f32)
        extra = jnp.where(lane == 0, high, jnp.where(lane == 1, gate_grad - high, 0.0))
        back_out[0, rows, width:] = extra.astype(bf16)

    by_row_count(bounds[8, expert], work)


def slot_spec(columns):
    return pl.BlockSpec((1, CAP, columns), lambda e: (e, 0, 0))


def slot_shape(columns):
    return shaped((EXPERTS, CAP, columns), bf16)


def weight_spec(weights):
    return pl.BlockSpec((1,) + weights.shape[1:], lambda e: (e, 0, 0))


def expert_forward(bounds, slots, segments, w_in, w_out, w_route, chosen):
    _, width, hidden_units = w_in.shape
    half = segments[0].shape[0]
    return kernel_call(
        functools.partial(expert_forward_kernel, 512),
        (EXPERTS,),
        [SMEM_SPEC, whole_spec((4, half))]
        + [whole_spec((half, width))] * 4
        + [weight_spec(w_in), weight_spec(w_out), whole_spec((8, width)), whole_spec((8, 4 * half))],
        [
            slot_spec(width),
            slot_spec(hidden_units),
            slot_spec(hidden_units),
            slot_spec(width),
            whole_spec((8, 4 * half)),
            whole_spec((4 * half, 1)),
        ],
        [
            slot_shape(width),
            slot_shape(hidden_units),
            slot_shape(hidden_units),
            slot_shape(width),
            shaped((8, 4 * half), f32),
            shaped((4 * half, 1), f32),
        ],
        [pltpu.VMEM((CAP, width), f32)],
        "expert_forward",
    )(bounds, slots, *segments, w_in, w_out, w_route, chosen)


def expert_backward(bounds, slots, cot_own, cot_oth, w_in, w_out, gate, result, slope):
    _, width, hidden_units = w_in.shape
    half = slots.shape[1]
    return kernel_call(
        functools.partial(expert_backward_kernel, 512),
        (EXPERTS,),
        [SMEM_SPEC, whole_spec((4, half)), whole_spec(cot_own.shape), whole_spec(cot_oth.shape)]
        + [weight_spec(w_in), weight_spec(w_out), whole_spec((4 * half, 1))]
        + [slot_spec(width), slot_spec(hidden_units)],
        [slot_spec(width), slot_spec(hidden_units), slot_spec(width + PAIR)],
        [slot_shape(width), slot_shape(hidden_units), slot_shape(width + PAIR)],
        [pltpu.VMEM((CAP, width), f32), pltpu.VMEM((4 * half, width), bf16)],
        "expert_backward",
    )(bounds, slots, cot_own, cot_oth, w_in, w_out, gate, result, slope)


def expert_grad_kernel(chunk, split, bounds, parity, left, right, mine, *refs):
    send, left_t = refs[0], refs[-1]
    expert = pl.program_id(0)
    left_t[...] = jnp.transpose(left[0])
    taken, odd = bounds[8, expert], parity[0]
    sizes = [rows for rows in (256, 512) if rows < CAP] + [CAP]
    below = -1
    for rows in sizes:

        @pl.when(jnp.logical_and(taken > below, taken <= rows))
        def _(rows=rows):
            for c in range(0, right.shape[2], chunk):
                product = dot(left_t[:, :rows], right[0, :rows, c : c + chunk]).astype(bf16)
                if not split:
                    mine[0, :, c : c + chunk] = product
                    continue
                block = mine.shape[2]
                for pair in range(mine.shape[1]):
                    even = product[2 * pair * block : (2 * pair + 1) * block]
                    other = product[(2 * pair + 1) * block : (2 * pair + 2) * block]
                    mine[0, pair, :, c : c + chunk] = jnp.where(odd == 0, even, other)
                    send[0, pair, :, c : c + chunk] = jnp.where(odd == 0, other, even)

        below = rows


def expert_grad(bounds, parity, left, right, blocks, name):
    width, hidden_units = left.shape[2], right.shape[2]
    block = width // blocks
    split = blocks > 1 and block % 16 == 0
    shape = (EXPERTS, blocks // 2, block, hidden_units) if split else (EXPERTS, width, hidden_units)
    spec = pl.BlockSpec((1,) + shape[1:], lambda e: (e,) + (0,) * (len(shape) - 1))
    mine, *send = kernel_call(
        functools.partial(expert_grad_kernel, 512, split),
        (EXPERTS,),
        [SMEM_SPEC, SMEM_SPEC, slot_spec(width), slot_spec(hidden_units)],
        [spec] * (2 if split else 1),
        [shaped(shape, bf16)] * (2 if split else 1),
        [pltpu.VMEM((width, CAP), bf16)],
        name,
    )(bounds, parity, left, right)
    if blocks == 1:
        return mine
    if split:
        return mine, send[0]
    return split_even_odd(mine.reshape(EXPERTS, blocks, block, hidden_units), parity[0])


def collect_kernel(first_seg, segs, bounds, slots, rows_in, *refs):
    outs, total = refs[:-1], refs[-1]
    expert = pl.program_id(0)
    half = slots.shape[0] // segs

    @pl.when(expert == 0)
    def _():
        total[...] = jnp.zeros_like(total)

    for index in range(segs):
        seg = first_seg + index
        start, windows = window_rows(bounds[seg, expert], bounds[4 + seg, expert])
        part = slice(index * half, (index + 1) * half)
        taken = slots[part, :] - expert * CAP

        @pl.loop(0, windows)
        def _(step, start=start, part=part, taken=taken):
            begin = start + step * WINDOW
            row = pl.multiple_of(jnp.minimum(begin, CAP - WINDOW), 16)
            offset = jnp.where(taken >= begin, taken - row, -1)
            slot = lax.broadcasted_iota(jnp.int32, (half, WINDOW), 1)
            place = jnp.where(slot == offset, 1.0, 0.0).astype(bf16)
            total[part, :] += dot(place, rows_in[0, pl.ds(row, WINDOW), :])

    @pl.when(expert == EXPERTS - 1)
    def _():
        width = outs[0].shape[1]
        for index in range(segs):
            part = slice(index * half, (index + 1) * half)
            outs[0][part, :] = total[part, :width].astype(outs[0].dtype)
            if rows_in.shape[2] == width:
                tail = outs[0].shape[0] - segs * half
                if tail:
                    outs[0][segs * half :, :] = jnp.zeros((tail, width), outs[0].dtype)
                continue
            extra = jnp.transpose(total[part, width:])[:8, :]
            if len(outs) > 1:
                outs[1][:, part] = extra
            else:
                first = segs * half + 8 * index
                outs[0][first : first + 8, :half] = extra.astype(outs[0].dtype)
                outs[0][first : first + 8, half:] = jnp.zeros((8, width - half), outs[0].dtype)


def collect(bounds, slots_column, rows_in, first_seg, segs, width, dtype, name, tail=0):
    columns = rows_in.shape[2]
    half = slots_column.shape[0] // 4
    rows = segs * (half + tail)
    out_specs = [pl.BlockSpec((rows, width), lambda e: (0, 0))]
    out_shape = [jax.ShapeDtypeStruct((rows, width), dtype)]
    if columns > width and not tail:
        out_specs.append(pl.BlockSpec((8, segs * half), lambda e: (0, 0)))
        out_shape.append(jax.ShapeDtypeStruct((8, segs * half), f32))
    return pl.pallas_call(
        functools.partial(collect_kernel, first_seg, segs),
        grid=(EXPERTS,),
        in_specs=[
            pl.BlockSpec(memory_space=pltpu.SMEM),
            pl.BlockSpec((segs * half, 1), lambda e: (first_seg // segs, 0)),
            slot_spec(columns),
        ],
        out_specs=out_specs,
        out_shape=out_shape,
        scratch_shapes=[pltpu.VMEM((segs * half, columns), f32)],
        compiler_params=pltpu.CompilerParams(vmem_limit_bytes=58 * 2**20),
        cost_estimate=SMALL_COST,
        name=name,
    )(bounds, slots_column, rows_in)


def logit_grads(chosen, probs, gate_own, gate_recv):
    gate_grad = gate_own[:1, :] + gate_own[1:2, :] + gate_recv[:1, :] + gate_recv[1:2, :]
    expert = lax.broadcasted_iota(jnp.int32, chosen.shape, 0)
    return jnp.where(expert < EXPERTS, chosen - probs, 0.0) * gate_grad


def residual_grad_kernel(
    steps, info, back_own, back_recv, probs, chosen, gate_own, gate_tail, w_route, res0, res1, cot,
    gain, w_own, w_oth, low_out, up_own, up_send,
):
    step = pl.program_id(0)
    block = cot.shape[0]
    logit_grad = logit_grads(
        chosen[...], probs[...], gate_own[...], gate_tail[:8, :].astype(f32)
    )
    two_grad = back_own[...].astype(f32) + back_recv[...].astype(f32)
    for _ in range(3):
        part = logit_grad.astype(bf16)
        two_grad += dot_tn(part, w_route[...])
        logit_grad = logit_grad - part.astype(f32)
    rows = jnp.where(step < steps, res0[...], res1[...])
    slot = lax.broadcasted_iota(jnp.int32, (block, 1), 0) + step % steps * block
    valid = slot + info[2] * (block * steps) < info[step // steps]
    upstream = jnp.where(valid, cot[...].astype(f32), 0.0)
    grad = upstream + norm_back(rows, inverse_rms(rows), gain[...], two_grad)
    low = grad.astype(bf16)
    low_out[...] = low
    up_send[...] = dot_nt(low, w_oth[...]).astype(bf16)
    up_own[...] = dot_nt(low, w_own[...]).astype(bf16)


def residual_grad_of(
    info, back_own, back_recv, probs, chosen, gate_own, w_route, residual, cot, gain, w_own, w_oth,
):
    half, width = residual[0].shape
    inner = w_own.shape[0]
    block = min(256, half)
    steps = half // block
    tile = pl.BlockSpec((block, width), lambda i: (i, 0))
    first = pl.BlockSpec((block, width), lambda i: (jnp.minimum(i, steps - 1), 0))
    second = pl.BlockSpec((block, width), lambda i: (jnp.maximum(i - steps, 0), 0))
    columns = pl.BlockSpec((8, block), lambda i: (0, i))
    gate_tail = pl.BlockSpec((8, block), lambda i: (2 * half // 8 + i // steps, i % steps))
    ctx = pl.BlockSpec((block, inner), lambda i: (i, 0))
    weight = whole_spec((inner, width))
    return kernel_call(
        functools.partial(residual_grad_kernel, steps),
        (2 * steps,),
        [SMEM_SPEC, tile, tile, columns, columns, columns, gate_tail]
        + [whole_spec((8, width)), first, second, tile, whole_spec((1, width)), weight, weight],
        [tile, ctx, ctx],
        [shaped((2 * half, width), bf16)] + [shaped((2 * half, inner), bf16)] * 2,
        [],
        "residual_grad",
    )(
        info, back_own, back_recv, probs, chosen, gate_own, back_recv, w_route, *residual, cot, gain,
        w_own, w_oth,
    )


def attn_grad_kernel(
    low, own0, own1, recv0, recv1, seg0, seg1, probs, chosen, gate_own, gate_tail,
    own_out, send_out, router_out,
):
    half = seg0.shape[0]
    low_t = [jnp.transpose(low[:half, :]), jnp.transpose(low[half:, :])]
    own_out[...] = dot(low_t[0], own0[...]) + dot(low_t[1], own1[...])
    send = (dot(low_t[0], recv0[...]) + dot(low_t[1], recv1[...])).astype(bf16)
    inner = send_out.shape[0]
    for index in range(send_out.shape[1] // inner):
        part = slice(index * inner, (index + 1) * inner)
        send_out[:, part] = send[part, :]
    total = None
    for index, seg in enumerate((seg0, seg1)):
        part = slice(index * half, (index + 1) * half)
        tail = gate_tail[8 * index : 8 * index + 8, :half].astype(f32)
        logit_grad = logit_grads(chosen[:, part], probs[:, part], gate_own[:, part], tail)
        for _ in range(3):
            piece = logit_grad.astype(bf16)
            product = dot(piece, seg[...])
            total = product if total is None else total + product
            logit_grad = logit_grad - piece.astype(f32)
    router_out[...] = total


def attn_grad(low, ctx_own, ctx_recv, segments, probs, chosen, gate_own, back_recv):
    half, inner = ctx_own[0].shape
    width = low.shape[1]
    columns = whole_spec((8, 2 * half))
    gate_tail = pl.BlockSpec((16, width), lambda i: (2 * half // 16, 0))
    return kernel_call(
        attn_grad_kernel,
        (1,),
        [whole_spec((2 * half, width))]
        + [whole_spec((half, inner))] * 4
        + [whole_spec((half, width))] * 2
        + [columns] * 3
        + [gate_tail],
        [whole_spec((width, inner)), whole_spec((inner, width)), whole_spec((8, width))],
        [shaped((width, inner), f32), shaped((inner, width), bf16), shaped((8, width), f32)],
        [],
        "attn_grad",
        20,
    )(low, *ctx_own, *ctx_recv, *segments, probs, chosen, gate_own, back_recv)


def attend_back_kernel(
    query_rows, last, split, info, parity, own, oth, ctx_own, ctx_oth, up_own, up_oth, log_ref,
    normed_own, normed_oth, weights, *refs,
):
    if last:
        before, one_own, one_oth, mine, send, key_sum, value_sum, grads, normed_t, all_grads = refs
    else:
        extra, one_own, one_oth, mine, key_sum, value_sum, grads, normed_t, all_grads = refs
    half = own.shape[0]
    row = lax.broadcasted_iota(jnp.int32, (half, PAIR), 0)
    zeros = jnp.zeros((half, PAIR), bf16)
    seen = (row + info[1] < info[0], row + info[2] < info[0])
    sides = ((own, ctx_own, up_own), (oth, ctx_oth, up_oth))

    def all_keys(part):
        first, last = part * PAIR, (part + 1) * PAIR
        return jnp.concatenate(
            [
                jnp.where(seen[0], own[:, first:last], zeros),
                jnp.where(seen[1], oth[:, first:last], zeros),
            ],
            0,
        )

    keys, values = all_keys(1), all_keys(2)
    keys_t = jnp.transpose(keys)
    lane = lax.broadcasted_iota(jnp.int32, (query_rows, PAIR), 1)
    sum_lane = lax.broadcasted_iota(jnp.int32, (8, PAIR), 1)
    sum_row = lax.broadcasted_iota(jnp.int32, (8, PAIR), 0)
    head_sum = jnp.where((sum_lane < HEAD_DIM) == (sum_row == 0), 1.0, 0.0).astype(bf16)
    for side, (src, ctx, up) in enumerate(sides):
        for block in range(half // query_rows):
            rows = slice(block * query_rows, (block + 1) * query_rows)
            first = side * half + block * query_rows
            query, grad = src[rows, :PAIR], up[rows, :]
            product = grad.astype(f32) * ctx[rows, :].astype(f32)
            coarse = product.astype(bf16)
            fine = (product - coarse.astype(f32)).astype(bf16)
            delta = dot_nt(head_sum, coarse) + dot_nt(head_sum, fine)
            query_grads, key_grads, value_grads = [], [], []
            for head in range(2):
                of_head = (lane < HEAD_DIM) == (head == 0)
                query_h = jnp.where(of_head, query, jnp.zeros_like(query))
                grad_h = jnp.where(of_head, grad, jnp.zeros_like(grad))
                log_row = log_ref[head : head + 1, first : first + query_rows]
                scores = dot_nt(keys, query_h)
                probs = jnp.exp2(jnp.minimum(scores * LOG_SCALE - log_row, 0.0))
                prob_grad = dot_nt(values, grad_h)
                score_grad = (probs * (prob_grad - delta[head : head + 1, :])).astype(bf16)
                value_grads.append(dot(probs.astype(bf16), grad_h))
                key_grads.append(dot(score_grad, query_h))
                query_grads.append(
                    dot(keys_t[head * HEAD_DIM : (head + 1) * HEAD_DIM, :], score_grad)
                )
            value_grad = value_grads[0] + value_grads[1]
            key_grad = key_grads[0] + key_grads[1]
            if side == 0 and block == 0:
                value_sum[...] = value_grad
                key_sum[...] = key_grad
            else:
                value_sum[...] += value_grad
                key_sum[...] += key_grad
            query_grad = jnp.transpose(jnp.concatenate(query_grads, 0)) * HEAD_DIM ** (-0.5)
            grads[first : first + query_rows, :PAIR] = query_grad.astype(bf16)
    for side in range(2):
        part = slice(side * half, (side + 1) * half)
        key_grad = jnp.where(seen[side], key_sum[part, :] * HEAD_DIM ** (-0.5), 0.0)
        grads[part, PAIR : 2 * PAIR] = key_grad.astype(bf16)
        grads[part, 2 * PAIR :] = jnp.where(seen[side], value_sum[part, :], 0.0).astype(bf16)

    pair = pl.program_id(0)

    @pl.when(pair == 0)
    def _():
        normed_t[:, :half] = jnp.transpose(normed_own[...])
        normed_t[:, half:] = jnp.transpose(normed_oth[...])

    all_grads[:, pl.ds(pl.multiple_of(pair * 3 * PAIR, 3 * PAIR), 3 * PAIR)] = grads[...]

    @pl.when(pair == pl.num_programs(0) - 1)
    def _():
        one_own[...] = dot_nt(all_grads[:half, :], weights[...])
        one_oth[:half, :] = dot_nt(all_grads[half:, :], weights[...]).astype(bf16)
        if not last:
            one_oth[half:, :] = extra[...]

    product = dot(normed_t[...], grads[...])
    if not last:
        mine[...] = product
        return
    product = (product + before[...]).astype(bf16)
    if not split:
        mine[...] = product
        return
    block = mine.shape[1]
    odd = parity[0]
    for index in range(mine.shape[0]):
        even = product[2 * index * block : (2 * index + 1) * block]
        other = product[(2 * index + 1) * block : (2 * index + 2) * block]
        mine[index] = jnp.where(odd == 0, even, other)
        send[index] = jnp.where(odd == 0, other, even)


def attend_back(
    info, parity, own, oth, seq, ctx_own, ctx_oth, up_own, up_oth, logs, normed_own, normed_oth,
    weights, blocks, before, last,
):
    half, columns = oth.shape
    width = weights.shape[0]
    pairs = columns // (3 * PAIR)
    query_rows = min(256, half)
    block = width // blocks
    split = block % 16 == 0
    one = pl.BlockSpec((half, PAIR), lambda p: (0, p))
    three = pl.BlockSpec((half, 3 * PAIR), lambda p: (0, p))
    weight = pl.BlockSpec((width, 3 * PAIR), lambda p: (0, p))
    sent = half if last else half + before.shape[0]
    out_specs = [whole_spec((half, width)), whole_spec((sent, width))]
    out_shape = [shaped((half, width), f32), shaped((sent, width), bf16)]
    if not last:
        out_specs.append(weight)
        out_shape.append(shaped((width, columns), f32))
    elif split:
        out_specs += [pl.BlockSpec((blocks // 2, block, 3 * PAIR), lambda p: (0, 0, p))] * 2
        out_shape += [shaped((blocks // 2, block, columns), bf16)] * 2
    else:
        out_specs += [weight, weight]
        out_shape += [shaped((width, columns), bf16)] * 2
    outs = kernel_call(
        functools.partial(attend_back_kernel, query_rows, last, split),
        (pairs,),
        [SMEM_SPEC, SMEM_SPEC, pl.BlockSpec((half, 3 * PAIR), lambda p: (seq, p)), three]
        + [one, one] + [pl.BlockSpec((half, PAIR), lambda p: (seq, p))] * 2
        + [pl.BlockSpec((8, 2 * half), lambda p: (p, 0))]
        + [pl.BlockSpec((half, width), lambda p: (seq, 0)), whole_spec((half, width)), whole_spec((width, columns))]
        + [weight if last else whole_spec(before.shape)],
        out_specs,
        out_shape,
        [
            pltpu.VMEM((2 * half, PAIR), f32),
            pltpu.VMEM((2 * half, PAIR), f32),
            pltpu.VMEM((2 * half, 3 * PAIR), bf16),
            pltpu.VMEM((width, 2 * half), bf16),
            pltpu.VMEM((2 * half, columns), bf16),
        ],
        "attend_back",
        48,
    )(
        info, parity, own, oth, ctx_own, ctx_oth, up_own, up_oth, logs, normed_own, normed_oth,
        weights, before,
    )
    if last and not split:
        outs = list(outs[:2]) + list(split_even_odd(outs[2].reshape(blocks, block, columns), parity[0]))
    return outs


def finish_kernel(
    steps, info, rows, one_own0, one_own1, recv0, recv1, grad, res0, res1, result_own,
    result_recv, gate, gain, input_grad, activations,
):
    step = pl.program_id(0)
    block = rows.shape[0]
    for seq, refs in enumerate(((one_own0, recv0, res0), (one_own1, recv1, res1))):

        @pl.when(step // steps == seq)
        def _(seq=seq, refs=refs):
            one_own, recv, res = refs
            x = rows[...].astype(f32)
            one_grad = one_own[...] + recv[...].astype(f32)
            input_grad[...] = grad[...].astype(f32) + norm_back(x, inverse_rms(x), gain[...], one_grad)
            combined = result_own[...].astype(f32) + result_recv[...].astype(f32)
            mixed = res[...] + gate[...] * combined
            slot = lax.broadcasted_iota(jnp.int32, (block, 1), 0) + step % steps * block
            valid = slot + info[2] * (steps * block) < info[seq]
            activations[...] = jnp.where(valid, mixed, 0.0).astype(bf16)


def finish(info, rows, one_own, one_recv, grads, residual, result_own, result_recv, gate, gain):
    half, width = residual[0].shape
    block = min(256, half)
    steps = half // block
    tile = pl.BlockSpec((block, width), lambda i: (i, 0))
    first = pl.BlockSpec((block, width), lambda i: (jnp.minimum(i, steps - 1), 0))
    second = pl.BlockSpec((block, width), lambda i: (jnp.maximum(i - steps, 0), 0))
    return kernel_call(
        functools.partial(finish_kernel, steps),
        (2 * steps,),
        [SMEM_SPEC, tile]
        + [first, second] * 2
        + [tile, first, second]
        + [tile, tile, pl.BlockSpec((block, 1), lambda i: (i, 0)), whole_spec((1, width))],
        [tile, tile],
        [shaped((2 * half, width), f32), shaped((2 * half, width), bf16)],
        [],
        "finish",
        58,
    )(info, rows, *one_own, *one_recv, grads, *residual, result_own, result_recv, gate, gain)


def after(array, *earlier):
    return lax.optimization_barrier((array,) + earlier)[0]


def split_even_odd(array, odd):
    lead = array.shape[:-3]
    halves = array.reshape(lead + (array.shape[-3] // 2, 2) + array.shape[-2:])
    axis = len(lead) + 1
    return (
        lax.dynamic_index_in_dim(halves, odd, axis, keepdims=False),
        lax.dynamic_index_in_dim(halves, 1 - odd, axis, keepdims=False),
    )


class Halving:
    def __init__(self, parts, experts, block, bits, table, order):
        self.parts = [(array, total, first, list(bits)) for array, total, first in parts]
        self.experts, self.block, self.table = experts, block, table
        self.left, self.order, self.picked = list(bits), list(order), set()
        self.size = len(bits) + 1
        self.columns = parts[0][0].shape[-1]

    def total(self, row, dtype, transpose=False):
        size, picked = self.size, set(self.picked)
        group = 2 if self.experts % 2 == 0 else 1
        arrays, specs = [], []
        for array, total, first, bits in self.parts:
            arrays.append(array.reshape((total,) + (2,) * len(bits) + (self.block, self.columns)))
            shape = tuple(None if bit in picked else 2 for bit in bits)

            def place(step, table, first=first, bits=bits):
                picks = tuple(table[row * size + bit] if bit in picked else 0 for bit in bits)
                return (first // group + step,) + picks + (0, 0)

            specs.append(pl.BlockSpec((group,) + shape + (self.block, self.columns), place))
        tail = (self.columns, self.block) if transpose else (self.block, self.columns)
        out = (self.experts,) + (2,) * len(self.left) + tail

        def kernel(table, *refs):
            value = refs[0][...].astype(f32)
            for ref in refs[1:-1]:
                value += ref[...].astype(f32)
            if transpose:
                for index in range(group):
                    refs[-1][index] = jnp.transpose(value[index]).astype(dtype)
            else:
                refs[-1][...] = value.astype(dtype)

        return pl.pallas_call(
            kernel,
            grid_spec=pltpu.PrefetchScalarGridSpec(
                num_scalar_prefetch=1,
                grid=(self.experts // group,),
                in_specs=specs,
                out_specs=pl.BlockSpec(
                    (group,) + out[1:], lambda e, t: (e,) + (0,) * (len(out) - 1)
                ),
            ),
            out_shape=shaped(out, dtype),
            compiler_params=pltpu.CompilerParams(vmem_limit_bytes=58 * 2**20),
            cost_estimate=SMALL_COST,
            name="half_sum",
        )(self.table, *arrays)

    def send(self):
        bit = self.order[0]
        self.left.remove(bit)
        self.picked.add(bit)
        sent = self.total(bit, bf16)
        return sent.reshape(-1, self.columns)

    def step(self, sent):
        recv = exchange(sent, self.order.pop(0), 2**self.size)
        self.parts.append((recv, self.experts, 0, list(self.left)))

    def spread(self):
        bits = list(self.left)
        size, picked, count = self.size, set(self.picked), len(self.parts)
        masks = range(2 ** len(bits))
        group = 2 if self.experts % 2 == 0 else 1
        arrays, specs = [], []
        for array, total, first, dims in self.parts:
            arrays.append(array.reshape((total,) + (2,) * len(dims) + (self.block, self.columns)))
            shape = tuple(None if bit in picked else 2 for bit in dims)

            def place(step, table, first=first, dims=dims):
                picks = tuple(table[size * size + bit] if bit in picked else 0 for bit in dims)
                return (first // group + step,) + picks + (0, 0)

            specs.append(pl.BlockSpec((group,) + shape + (self.block, self.columns), place))
        out = (self.experts, self.block, self.columns)

        def kernel(table, *refs):
            for mask in masks:
                at = tuple(
                    table[size * size + bit] ^ ((mask >> (len(bits) - 1 - i)) & 1)
                    for i, bit in enumerate(bits)
                )
                at = (slice(None),) + at
                value = refs[0][at].astype(f32)
                for ref in refs[1:count]:
                    value += ref[at].astype(f32)
                refs[count + mask][...] = value.astype(bf16)

        own, *sent = pl.pallas_call(
            kernel,
            grid_spec=pltpu.PrefetchScalarGridSpec(
                num_scalar_prefetch=1,
                grid=(self.experts // group,),
                in_specs=specs,
                out_specs=[
                    pl.BlockSpec((group, self.block, self.columns), lambda e, t: (e, 0, 0))
                ] * len(masks),
            ),
            out_shape=[shaped(out, bf16)] * len(masks),
            compiler_params=pltpu.CompilerParams(vmem_limit_bytes=14 * 2**20),
            cost_estimate=SMALL_COST,
            name="spread_sum",
        )(self.table, *arrays)
        recv = []
        for mask, array in zip(masks[1:], sent):
            flip = sum(
                1 << bit for i, bit in enumerate(bits) if (mask >> (len(bits) - 1 - i)) & 1
            )
            pairs = [(i, i ^ flip) for i in range(2**size)]
            flat = lax.ppermute(array.reshape(-1, self.columns), "dp", pairs)
            recv.append(flat.reshape(out))
        return own, recv

    def last_recv(self, *earlier):
        array, *rest = self.parts[-1]
        if earlier:
            self.parts[-1] = (after(array, *earlier), *rest)
        return self.parts[-1][0]


def exchange(array, bit, size):
    return lax.ppermute(array, "dp", [(i, i ^ (1 << bit)) for i in range(size)])


def body(
    inputs,
    cotangent,
    lengths,
    routes,
    norm1_gain,
    w_query,
    w_key,
    w_value,
    w_attn_out,
    norm2_gain,
    w_router,
    w_expert_in,
    w_expert_out,
):
    seqs, half, width = inputs.shape
    slots = routes.shape[1]
    inner = w_query.shape[1]
    pairs = inner // PAIR
    side = lax.axis_index("tensor")
    dp_index = lax.axis_index("dp")
    dp_size = lax.axis_size("dp")
    own_tokens = seqs * half
    gain_one = norm1_gain.astype(f32)[None, :]
    gain_two = norm2_gain.astype(f32)[None, :]

    def swap(array):
        return lax.ppermute(array, "tensor", [(0, 1), (1, 0)])

    dp_rows = width // dp_size
    bits = dp_size.bit_length() - 1
    parity = (dp_index & 1).reshape(1).astype(jnp.int32)
    rows = inputs.reshape(own_tokens, width)
    cot_rows = cotangent.reshape(own_tokens, width)
    rows_oth = [swap(inputs[0])]
    info = jnp.concatenate([lengths, side[None]]).astype(jnp.int32)
    infos = [
        jnp.stack([lengths[s], side * half, (1 - side) * half]).astype(jnp.int32)
        for s in range(seqs)
    ]
    slots_rows, slots_column, chosen, bounds = plan(info, routes.reshape(seqs, slots))
    w_pairs = jnp.concatenate(
        [w[:, p * PAIR : (p + 1) * PAIR] for p in range(pairs) for w in (w_query, w_key, w_value)],
        1,
    )
    flips = (dp_index >> jnp.arange(bits)) & 1
    table = jnp.concatenate(
        [(flips[None, :] ^ jnp.eye(bits, dtype=flips.dtype)).reshape(-1), flips]
    ).astype(jnp.int32)
    w_route = jnp.pad(w_router.T, ((0, 8 - EXPERTS), (0, 0)))
    normed_own, proj_own = project(rows, gain_one, w_pairs, "project_own")
    first_in = after(rows_oth[0], proj_own, bounds, w_route, table)
    rows_oth[0] = first_in
    for s in range(1, seqs):
        rows_oth.append(swap(after(inputs, rows_oth[-1])[s]))
    normed_oth, proj_oth, ctx_own, ctx_oth, ctx_recv, logs = [], [], [], [], [], []
    for s in range(seqs):
        raw = rows_oth[s] if s == 0 else after(rows_oth[s], ctx_oth[s - 1])
        if s == 1:
            attn_out_oth = swap(after(w_attn_out, raw))
        normed_part, proj_part = project(raw, gain_one, w_pairs, "project_oth")
        normed_oth.append(normed_part)
        proj_oth.append(proj_part)
        own_part, oth_part, log_part = attend(infos[s], proj_own, proj_part, s)
        ctx_own.append(own_part)
        ctx_oth.append(oth_part)
        logs.append(log_part)
        ctx_recv.append(swap(oth_part))
    residual, normed_two, two_oth = [], [], []
    for s in range(seqs):
        ctx_recv[s] = after(ctx_recv[s], ctx_oth[-1] if s == 0 else normed_two[s - 1])
        res_part, normed_part = residual_of(
            rows, s, ctx_own[s], ctx_recv[s], w_attn_out, attn_out_oth, gain_two
        )
        residual.append(res_part)
        normed_two.append(normed_part)
        two_oth.append(swap(normed_part))

    segments = normed_two + two_oth
    cot_oth = swap(after(cotangent, *two_oth))
    x_rows, hidden, slope, result, probs, gate = expert_forward(
        bounds, slots_rows, segments, w_expert_in, w_expert_out, w_route, chosen
    )
    (result_oth,) = collect(
        bounds, slots_column, result, seqs, seqs, width, bf16, "collect_result_oth", 64
    )
    (result_own,) = collect(
        bounds, slots_column, after(result, result_oth), 0, seqs, width, bf16, "collect_result_own"
    )
    result_recv = swap(result_oth)
    cot_oth = after(cot_oth, result_own)
    up_rows, pre_grad, back = expert_backward(
        bounds, slots_rows, cotangent, cot_oth, w_expert_in, w_expert_out, gate, result, slope
    )
    (back_oth,) = collect(
        bounds, slots_column, back, seqs, seqs, width, bf16, "collect_back_oth", 8
    )
    back_recv = swap(back_oth)
    halved = list(range(bits - 1, 0, -1))
    order_x = list(range(1, bits))
    columns = w_expert_in.shape[2]
    grad_out_t = expert_grad(
        after(bounds, back_oth, result_recv), parity, up_rows, hidden, 1, "grad_expert_out"
    )
    back_own, gate_own = collect(
        bounds, slots_column, after(back, grad_out_t), 0, seqs, width, bf16, "collect_back_own"
    )
    in_mine, in_send = expert_grad(
        after(bounds, back_own), parity, x_rows, pre_grad, dp_size, "grad_expert_in"
    )
    recv = after(back_recv, in_mine)
    in_recv = exchange(after(in_send, recv).reshape(-1, columns), 0, dp_size)
    out_share_t = lax.psum_scatter(
        after(grad_out_t, recv), "dp", scatter_dimension=1, tiled=True
    )

    residual_low, up_own, up_send = residual_grad_of(
        info, back_own, recv, probs, chosen, gate_own, w_route, residual, cot_rows, gain_two,
        w_attn_out, attn_out_oth,
    )
    up_oth = swap(up_send)
    in_mine, in_recv = in_mine.reshape(-1, columns), after(in_recv, up_send)
    order_z = order_x[1:] + order_x[:1]
    in_sums = [
        Halving(
            [(in_mine, EXPERTS, first), (in_recv, EXPERTS, first)],
            EXPERTS // 2, dp_rows, halved, table, order,
        )
        for first, order in ((0, order_x), (EXPERTS // 2, order_z))
    ]
    in_sent = [part.send() for part in in_sums]
    for part, sent in zip(in_sums, in_sent):
        part.step(sent)
    grad_attn_t, grad_attn_send, grad_router = attn_grad(
        after(residual_low, *in_sent), ctx_own, ctx_recv, normed_two, probs, chosen, gate_own, recv
    )

    log_rows = after(logs[0], grad_attn_t)
    one_own0, one_oth0, grad_pairs = attend_back(
        infos[0], parity, proj_own, proj_oth[0], 0, ctx_own[0], ctx_oth[0], up_own, up_oth,
        log_rows, normed_own, normed_oth[0], w_pairs, dp_size, grad_attn_send, False,
    )
    one_recv = [swap(one_oth0)]
    for part in in_sums:
        part.last_recv(one_oth0)
    in_sent = [part.send() for part in in_sums]
    log_rows = after(logs[1], *in_sent)
    one_own1, one_oth1, *grad_pairs = attend_back(
        infos[1], parity, proj_own, proj_oth[1], 1, ctx_own[1], ctx_oth[1], up_own, up_oth,
        log_rows, normed_own, normed_oth[1], w_pairs, dp_size, grad_pairs, True,
    )
    one_recv.append(swap(one_oth1))
    attn_recv = after(one_recv[0], one_oth1)[half:].astype(f32)
    grad_attn_t = grad_attn_t + jnp.concatenate(
        [attn_recv[:, i * inner : (i + 1) * inner] for i in range(width // inner)], 0
    )
    grad_router = after(grad_router, one_oth1)[:EXPERTS].T
    router_high = grad_router.astype(bf16)
    router_low = (grad_router - router_high.astype(f32)).astype(bf16)
    small = jnp.concatenate([router_high, router_low], 1)
    small = jnp.pad(small, ((0, 0), (0, PAIR - 2 * EXPERTS)))
    rest = jnp.concatenate([grad_attn_t.astype(bf16), small], 1).reshape(dp_size, dp_rows, -1)
    rest = split_even_odd(rest, parity[0])
    pairs_mine, pairs_send = [part.reshape(-1, part.shape[-1]) for part in grad_pairs]
    rest_mine, rest_send = [part.reshape(-1, part.shape[-1]) for part in rest]
    for part, sent in zip(in_sums, in_sent):
        part.step(sent)
    last_send = after(pairs_send, *[part.last_recv() for part in in_sums])
    last_mine = jnp.concatenate([pairs_mine, rest_mine], 1)
    last_recv = jnp.concatenate(
        [exchange(last_send, 0, dp_size), exchange(rest_send, 0, dp_size)], 1
    )
    for part in in_sums:
        part.last_recv(last_send)
        while part.order:
            part.step(part.send())
    last_sum = Halving(
        [(last_mine, 1, 0), (last_recv, 1, 0)],
        1, dp_rows, halved, table, [bit for bit in order_x if bit < bits - 2],
    )
    while last_sum.order:
        last_sum.step(last_sum.send())
    last_sum.last_recv(one_recv[1])
    last_own, last_recv = last_sum.spread()
    last_share = sum(part.astype(f32) for part in [last_own] + last_recv)[0]
    input_grad, activations = finish(
        info, rows, (one_own0, one_own1), (one_recv[0], after(one_recv[1], last_own)), residual_low,
        residual, result_own, result_recv, gate, gain_one,
    )
    late = in_sums[1].total(bits, f32)
    in_sums[0].last_recv(input_grad, late)
    in_share = jnp.concatenate([in_sums[0].total(bits, f32), late], 0)
    out_share = jnp.swapaxes(out_share_t, 1, 2).astype(f32)

    own_rows = dp_rows // 2

    def share_rows(array, axis=0):
        return lax.dynamic_slice_in_dim(array, dp_index * dp_rows, dp_rows, axis)

    pair_share = last_share[:, : 3 * inner]
    shares = [
        jnp.concatenate(
            [pair_share[:, (3 * p + k) * PAIR : (3 * p + k + 1) * PAIR] for p in range(pairs)], 1
        )
        for k in range(3)
    ]
    attn_share = last_share[:, 3 * inner : 4 * inner].T
    router_share = (
        last_share[:, 4 * inner : 4 * inner + EXPERTS]
        + last_share[:, 4 * inner + EXPERTS : 4 * inner + 2 * EXPERTS]
    )
    sum_one = jnp.sum(pair_share * share_rows(w_pairs).astype(f32), axis=1)
    sum_two = jnp.sum(in_share * share_rows(w_expert_in, 1).astype(f32), axis=(0, 2))
    sums = jnp.concatenate([jnp.stack([sum_one, sum_two]), router_share.T], 0)
    sums_recv = swap(sums)
    sums = sums + after(sums_recv, out_share)
    router_share = sums[2:].T
    router_sum = jnp.sum(router_share * share_rows(w_router).astype(f32), axis=1)
    gain_grads = jnp.stack(
        [sums[0] / share_rows(gain_one[0]), (sums[1] + router_sum) / share_rows(gain_two[0])]
    )
    gain_grads = lax.dynamic_slice_in_dim(gain_grads, side * own_rows, own_rows, 1)
    router_out = lax.dynamic_slice_in_dim(router_share, side * own_rows, own_rows, 0)
    return (
        activations.reshape(inputs.shape),
        input_grad.reshape(inputs.shape),
        gain_grads[0],
        shares[0],
        shares[1],
        shares[2],
        attn_share,
        gain_grads[1],
        router_out,
        in_share,
        out_share,
    )


def solution(mesh):
    in_specs = (
        P("dp", "tensor", None),
        P("dp", "tensor", None),
        P("dp"),
        P("dp", None, None),
        P(),
        P(None, "tensor"),
        P(None, "tensor"),
        P(None, "tensor"),
        P("tensor", None),
        P(),
        P(),
        P(None, None, "tensor"),
        P(None, "tensor", None),
    )
    out_specs = (
        P("dp", "tensor", None),
        P("dp", "tensor", None),
        P(("dp", "tensor")),
        P("dp", "tensor"),
        P("dp", "tensor"),
        P("dp", "tensor"),
        P("tensor", "dp"),
        P(("dp", "tensor")),
        P(("dp", "tensor"), None),
        P(None, "dp", "tensor"),
        P(None, "tensor", "dp"),
    )
    return jax.shard_map(body, mesh=mesh, in_specs=in_specs, out_specs=out_specs, check_vma=False)
```
